128 devices in a mesh: dp: 16 (over x_hi, y, core), tensor: 8 (over x_lo, z).
Axes of the slice: x: 4 (x_hi: 2, x_lo: 2; x = x_hi * 2 + x_lo), y: 4, z: 4, core: 2. Of those that a mesh axis runs over, the one named last changes fastest.
Arguments:
- layer_in: bfloat16 [16384, 2048], P(('dp', 'tensor')), may hold values from -6 to 6
- grad_out: bfloat16 [16384, 2048], P(('dp', 'tensor')), may hold values from -6 to 6
- routes: int32 [16384, 1], P('dp'), may hold values from 0 to 1; in each aligned block of 1024 rows (0 to 1023, 1024 to 2047, ...) at most 640 rows name the same one
- prefix: int32 [16], P('dp'), may hold values from 102 to 512
- attn_gain: bfloat16 [2048], replicated, may hold values from 0.5 to 1.5
- query_proj: bfloat16 [2048, 3072], P(None, 'tensor'), may hold values from -0.125 to 0.125
- kv_down: bfloat16 [2048, 576], replicated, may hold values from -0.125 to 0.125
- latent_gain: bfloat16 [512], replicated, may hold values from 0.5 to 1.5
- kv_up: bfloat16 [512, 4096], P(None, 'tensor'), may hold values from -0.25 to 0.25
- out_proj: bfloat16 [2048, 2048], P('tensor'), may hold values from -2 to 2
- ffn_gain: bfloat16 [2048], replicated, may hold values from 0.5 to 1.5
- router_proj: bfloat16 [2048, 2], replicated, may hold values from -0.0625 to 0.0625
- shared_gate: bfloat16 [2048, 2816], P(None, 'tensor'), may hold values from -0.125 to 0.125
- shared_up: bfloat16 [2048, 2816], P(None, 'tensor'), may hold values from -0.125 to 0.125
- shared_down: bfloat16 [2816, 2048], P('tensor'), may hold values from -0.109375 to 0.109375
- expert_gate: bfloat16 [2, 2048, 1408], P(None, None, 'tensor'), may hold values from -0.125 to 0.125
- expert_up: bfloat16 [2, 2048, 1408], P(None, None, 'tensor'), may hold values from -0.125 to 0.125
- expert_down: bfloat16 [2, 1408, 2048], P(None, 'tensor'), may hold values from -0.3125 to 0.3125
Outputs:
- layer_out: bfloat16 [16384, 2048], P(('dp', 'tensor'))
- layer_in_grad: bfloat16 [16384, 2048], P(('dp', 'tensor'))
- attn_gain_grad: float32 [2048], P('tensor')
- query_proj_grad: float32 [2048, 3072], P(None, 'tensor')
- kv_down_grad: float32 [2048, 576], P('tensor')
- latent_gain_grad: float32 [512], P('tensor')
- kv_up_grad: float32 [512, 4096], P(None, 'tensor')
- out_proj_grad: float32 [2048, 2048], P('tensor')
- ffn_gain_grad: float32 [2048], P('tensor')
- router_proj_grad: float32 [2048, 2], P('tensor')
- shared_gate_grad: float32 [2048, 2816], P(None, 'tensor')
- shared_up_grad: float32 [2048, 2816], P(None, 'tensor')
- shared_down_grad: float32 [2816, 2048], P('tensor')
- expert_gate_grad: float32 [2, 2048, 1408], P(None, None, 'tensor')
- expert_up_grad: float32 [2, 2048, 1408], P(None, None, 'tensor')
- expert_down_grad: float32 [2, 1408, 2048], P(None, 'tensor')
The draws below stay inside these ranges and needn't reach their ends.
Inputs may be any that keep to these rules, and one draw needn't show every extreme that they name: `routes`: a row names 1 different experts; in each aligned block of 1024 tokens (one sequence) no expert is named by more than 640 tokens, and in some block one expert is named by exactly 640.
All inputs are finite; a program needn't handle non-finite values.
Results may differ from the reference program's by a relative error of at most 0.04.
Values may be sent and summed in bfloat16 or wider, within the bound.
A program may use at most 256 MiB of HBM per device.

```python
import math
import jax
import jax.numpy as jnp
import numpy as np
from jax import lax

D = 2048
H = 16
DN = 128
DR = 64
DV = 128
KVR = 512
FE = 1408
FS = 2816
EXPERTS = 2
TOP = 1
SEQ_LEN = 1024
CAP = 640
SEQS = 16
TOKENS = 16384


def touch_ends(drawn, own_key, smallest, largest):
    spot = [jax.random.randint(jax.random.fold_in(own_key, axis), (), 0, length) for axis, length in enumerate(drawn.shape)]
    main_axis = drawn.shape.index(max(drawn.shape))
    next_to = spot[:main_axis] + [(spot[main_axis] + 1) % drawn.shape[main_axis]] + spot[main_axis + 1:]
    return drawn.at[tuple(spot)].set(smallest).at[tuple(next_to)].set(largest)


def level_of(rng, extent, split, least, largest):
    def one(dim, shards_of):
        heights = jax.random.uniform(jax.random.fold_in(jax.random.fold_in(rng, 6), dim), (shards_of,), jnp.float32, least / len(split), largest / len(split))
        return jnp.repeat(jnp.exp(heights), extent[dim] // shards_of).reshape((-1,) + (1,) * (len(extent) - dim - 1))

    gain = one(*split[0])
    for cut in split[1:]:
        gain = gain * one(*cut)
    return gain


def deal_out(stream_key, own, number, rows, count, top, limit, slope):
    sequence = jax.random.permutation(stream_key, count)
    packed, ordinary = shares(count, rows * top, limit, slope, True), shares(count, rows * top, limit, slope, False)
    places = jnp.arange(count)

    def named(lengths, rotation):
        used = int((lengths > 0).sum())
        fixed = max(1, used // 4)
        passed = fixed + (places - fixed + rotation * (used - fixed)) % max(1, count - fixed)
        return jnp.zeros((count,), jnp.int32).at[sequence[jnp.where(places < fixed, places, passed)]].set(jnp.asarray(lengths, jnp.int32))

    lengths = jnp.where(number % 4 == 0, named(packed, number // 4), named(ordinary, number - number // 4 - 1))
    mixed = jax.random.permutation(jax.random.fold_in(own, 3), count)
    donor, receiver = mixed[0:count // 2 * 2:2], mixed[1:count // 2 * 2:2]
    margin = jnp.minimum(lengths[donor] - 1, limit - lengths[receiver]) // 2
    margin = jnp.where((donor == sequence[0]) | (receiver == sequence[0]) | (lengths[receiver] == 0), 0, jnp.maximum(margin, 0))
    passed = jax.random.randint(jax.random.fold_in(own, 4), (count // 2,), 0, 1 << 20) % (margin + 1)
    lengths = lengths.at[donor].add(-passed).at[receiver].add(passed)
    labels = jnp.searchsorted(jnp.cumsum(lengths), jnp.arange(rows * top), side="right").astype(jnp.int32)
    table = labels.reshape(top, rows).T
    table = table[jax.random.permutation(jax.random.fold_in(own, 1), rows)]
    rotation = jax.random.randint(jax.random.fold_in(own, 2), (rows, 1), 0, top)
    return jnp.take_along_axis(table, (jnp.arange(top)[None, :] + rotation) % top, axis=1)


def shares(number_of, total, bound, skew, full):
    loads = [(1 << 20) // math.isqrt(standing ** skew) + 1 for standing in range(1, number_of + 1)]
    largest = bound if full else min(bound, max(-(-total // number_of), total * loads[0] // sum(loads)))
    least = 1 if total - largest >= number_of - 1 else 0
    given, spare = [largest] + [least] * (number_of - 1), total - largest - least * (number_of - 1)
    while spare > 0:
        free = [i for i in range(1, number_of) if given[i] < largest] or [i for i in range(1, number_of) if given[i] < bound]
        whole, remaining = sum([loads[i] for i in free]), spare
        for i in free:
            extra = min(bound - given[i], max(1, remaining * loads[i] // whole), spare)
            given[i] = given[i] + extra
            spare = spare - extra
    return np.array(given)


def noise(rng, dims, spread, most, cuts=(), held_as=jnp.bfloat16):
    entries = spread * jax.random.normal(rng, dims, jnp.float32)
    if cuts:
        entries = entries * level_of(rng, dims, cuts, -0.22, 0.18)
    return jnp.clip(entries, -most, most).astype(held_as)


def setup_inputs(seed: int = 0) -> dict:
    arg_keys = jax.random.split(jax.random.key(seed), 19)
    layer_in = noise(arg_keys[0], (TOKENS, D), 1.0, 6.0, ((0, 128),))
    grad_out = noise(arg_keys[1], (TOKENS, D), 1.0, 6.0, ((0, 128),))
    routes_keys = jax.random.split(jax.random.fold_in(arg_keys[2], 1), TOKENS // SEQ_LEN)
    routes_turns = jax.random.permutation(jax.random.fold_in(arg_keys[2], 3), TOKENS // SEQ_LEN)
    routes = jax.vmap(lambda own, number: deal_out(jax.random.fold_in(arg_keys[2], 2), own, number, SEQ_LEN, EXPERTS, TOP, CAP, 1))(routes_keys, routes_turns).reshape((TOKENS, TOP))
    prefix = touch_ends(jax.random.randint(arg_keys[3], (SEQS,), SEQ_LEN // 10, SEQ_LEN // 2 + 1), jax.random.fold_in(arg_keys[3], 1), SEQ_LEN // 10, (SEQ_LEN // 2 + 1) - 1).astype(jnp.int32)
    attn_gain = jnp.clip(1.0 + 0.1 * jax.random.normal(arg_keys[4], (D,), jnp.float32), 0.5, 1.5).astype(jnp.bfloat16)
    query_proj = noise(arg_keys[5], (D, H * (DN + DR)), D ** -0.5, 0.125, ((1, 8),))
    kv_down = noise(arg_keys[6], (D, KVR + DR), D ** -0.5, 0.125)
    latent_gain = jnp.clip(1.0 + 0.1 * jax.random.normal(arg_keys[7], (KVR,), jnp.float32), 0.5, 1.5).astype(jnp.bfloat16)
    kv_up = noise(arg_keys[8], (KVR, H * (DN + DV)), KVR ** -0.5, 0.25, ((1, 8),))
    out_proj = noise(arg_keys[9], (H * DV, D), (max(1, H * DV // 256)) ** -0.5, 2.0, ((0, 8),))
    ffn_gain = jnp.clip(1.0 + 0.1 * jax.random.normal(arg_keys[10], (D,), jnp.float32), 0.5, 1.5).astype(jnp.bfloat16)
    router_proj = noise(arg_keys[11], (D, EXPERTS), (4 * D) ** -0.5, 0.0625)
    shared_gate = noise(arg_keys[12], (D, FS), D ** -0.5, 0.125, ((1, 8),))
    shared_up = noise(arg_keys[13], (D, FS), D ** -0.5, 0.125, ((1, 8),))
    shared_down = noise(arg_keys[14], (FS, D), FS ** -0.5, 0.109375, ((0, 8),))
    expert_gate = noise(arg_keys[15], (EXPERTS, D, FE), D ** -0.5, 0.125, ((2, 8),))
    expert_up = noise(arg_keys[16], (EXPERTS, D, FE), D ** -0.5, 0.125, ((2, 8),))
    expert_down = noise(arg_keys[17], (EXPERTS, FE, D), (FE // 4) ** -0.5, 0.3125, ((1, 8),))
    return dict(layer_in=layer_in, grad_out=grad_out, routes=routes, prefix=prefix, attn_gain=attn_gain, query_proj=query_proj, kv_down=kv_down, latent_gain=latent_gain, kv_up=kv_up, out_proj=out_proj, ffn_gain=ffn_gain, router_proj=router_proj, shared_gate=shared_gate, shared_up=shared_up, shared_down=shared_down, expert_gate=expert_gate, expert_up=expert_up, expert_down=expert_down)


@jax.custom_vjp
def low(v):
    return lax.optimization_barrier(v.astype(jnp.bfloat16)).astype(jnp.float32)

@jax.custom_vjp
def low_back(v):
    return v

def low_keep(v):
    return (low(v), None)

def low_pass(kept, grad):
    return (grad,)

def back_keep(v):
    return (v, None)

def back_low(kept, grad):
    return (low(grad),)
low.defvjp(low_keep, low_pass)
low_back.defvjp(back_keep, back_low)
EPS = 1e-06
ROPE_BASE = 10000.0
NEGATIVE_PAD = -1e+30
HIGH_PREC = lax.Precision.HIGHEST

def matmul(left_side, right_side):
    return jnp.dot(left_side, right_side, precision=HIGH_PREC)

def rms_scale(values, gain_vec):
    return values * lax.rsqrt(lax.optimization_barrier(jnp.mean(values * values, axis=-1, keepdims=True)) + EPS) * gain_vec

def rope_table(seq_rows):
    half_width = DR // 2
    frequency = ROPE_BASE ** (-(jnp.arange(half_width, dtype=jnp.float32) * 2.0) / DR)
    angles = jnp.arange(seq_rows, dtype=jnp.float32)[:, None] * frequency[None, :]
    return (jnp.cos(angles), jnp.sin(angles))

def rotate(values, cos_tab, sin_tab):
    half_width = values.shape[-1] // 2
    first_half = values[..., :half_width]
    second_half = values[..., half_width:]
    return jnp.concatenate([first_half * cos_tab - second_half * sin_tab, second_half * cos_tab + first_half * sin_tab], axis=-1)

def softmax_rows(scores):
    row_max = lax.optimization_barrier(jnp.max(scores, axis=-1, keepdims=True))
    shifted = jnp.exp(scores - row_max)
    return shifted / lax.optimization_barrier(jnp.sum(shifted, axis=-1, keepdims=True))

def forward(params, layer_rows, route_rows, prefix_end):
    attn_gain, query_proj, kv_down, latent_gain, kv_up, out_proj, ffn_gain, router_proj, shared_gate, shared_up, shared_down, expert_gate, expert_up, expert_down = params
    seq_rows = layer_rows.shape[0]
    cos_tab, sin_tab = rope_table(seq_rows)
    normed = low(rms_scale(layer_rows, attn_gain))
    kv_joint = low_back(matmul(normed, kv_down))
    latent_norm = low(rms_scale(kv_joint[:, :KVR], latent_gain))
    key_rope = low(rotate(kv_joint[:, KVR:], cos_tab, sin_tab))
    query_raw = low_back(matmul(normed, query_proj)).reshape(seq_rows, H, DN + DR)
    queries = low(jnp.concatenate([query_raw[..., :DN], rotate(query_raw[..., DN:], cos_tab[:, None], sin_tab[:, None])], axis=-1))
    kv_wide = low(low_back(matmul(latent_norm, kv_up))).reshape(seq_rows, H, DN + DV)
    key_all = jnp.concatenate([kv_wide[..., :DN], jnp.broadcast_to(key_rope[:, None, :], (seq_rows, H, DR))], axis=-1)
    value_all = kv_wide[..., DN:]
    block_rows = min(512, seq_rows)
    block_count = seq_rows // block_rows
    key_pos = jnp.arange(seq_rows, dtype=jnp.int32)
    score_scale = (DN + DR) ** (-0.5)

    def attend(block_args):
        query_block, start_row = block_args
        query_positions = start_row + jnp.arange(block_rows, dtype=jnp.int32)
        visible = (key_pos[None, :] <= query_positions[:, None]) | (key_pos[None, :] < prefix_end)
        raw_scores = jnp.einsum('qhd,khd->hqk', query_block, key_all, precision=HIGH_PREC)
        scores = jnp.where(visible[None], low_back(raw_scores * score_scale), NEGATIVE_PAD)
        attn_probs = softmax_rows(scores)
        return jnp.einsum('hqk,khd->qhd', low(attn_probs), value_all, precision=HIGH_PREC)
    starts = jnp.arange(block_count, dtype=jnp.int32) * block_rows
    attended = lax.map(jax.checkpoint(attend), (queries.reshape(block_count, block_rows, H, DN + DR), starts))
    attn = low(low_back(attended.reshape(seq_rows, H * DV)))
    hidden = layer_rows + low_back(matmul(attn, out_proj))
    mixed = low(rms_scale(hidden, ffn_gain))
    router = softmax_rows(low_back(matmul(mixed, router_proj)))
    chosen = (route_rows[:, :, None] == jnp.arange(EXPERTS, dtype=jnp.int32)[None, None, :]).astype(jnp.float32)
    token_gates = lax.optimization_barrier(jnp.sum(router[:, None, :] * chosen, axis=-1))
    gate_table = lax.optimization_barrier(jnp.sum(token_gates[:, :, None] * chosen, axis=1))
    shared_pre_gate = low_back(matmul(mixed, shared_gate))
    shared_pre_up = low_back(matmul(mixed, shared_up))
    shared_m = low(jax.nn.silu(shared_pre_gate) * shared_pre_up)
    total_out = matmul(shared_m, shared_down)
    for expert in range(EXPERTS):
        gate_pre = low_back(matmul(mixed, expert_gate[expert]))
        up_pre = low_back(matmul(mixed, expert_up[expert]))
        expert_m = low(gate_table[:, expert:expert + 1] * jax.nn.silu(gate_pre) * up_pre)
        total_out = total_out + matmul(expert_m, expert_down[expert])
    return hidden + total_out

def reference(layer_in, grad_out, routes, prefix, attn_gain, query_proj, kv_down, latent_gain, kv_up, out_proj, ffn_gain, router_proj, shared_gate, shared_up, shared_down, expert_gate, expert_up, expert_down):
    params = (attn_gain.astype(jnp.float32), query_proj.astype(jnp.float32), kv_down.astype(jnp.float32), latent_gain.astype(jnp.float32), kv_up.astype(jnp.float32), out_proj.astype(jnp.float32), ffn_gain.astype(jnp.float32), router_proj.astype(jnp.float32), shared_gate.astype(jnp.float32), shared_up.astype(jnp.float32), shared_down.astype(jnp.float32), expert_gate.astype(jnp.float32), expert_up.astype(jnp.float32), expert_down.astype(jnp.float32))
    rows_seq = layer_in.astype(jnp.float32).reshape(SEQS, SEQ_LEN, D)
    grads_seq = grad_out.astype(jnp.float32).reshape(SEQS, SEQ_LEN, D)
    routes_seq = routes.reshape(SEQS, SEQ_LEN, TOP)

    def one_sequence(grad_sum, inputs):
        layer_rows, route_rows, prefix_end, out_grad = inputs

        def apply_layer(param_set, rows_now):
            return forward(param_set, rows_now, route_rows, prefix_end)
        outputs, pullback = jax.vjp(apply_layer, params, layer_rows)
        param_grads, row_grads = pullback(out_grad)
        grad_sum = jax.tree.map(jnp.add, grad_sum, param_grads)
        return (grad_sum, (outputs.astype(jnp.bfloat16), row_grads.astype(jnp.bfloat16)))
    zero_grads = jax.tree.map(jnp.zeros_like, params)
    totals, (outs_seq, back_seq) = lax.scan(one_sequence, zero_grads, (rows_seq, routes_seq, prefix, grads_seq))
    return (outs_seq.reshape(TOKENS, D), back_seq.reshape(TOKENS, D), totals[0], totals[1], totals[2], totals[3], totals[4], totals[5], totals[6], totals[7], totals[8], totals[9], totals[10], totals[11], totals[12], totals[13])
```

```python
import functools

import jax
import jax.numpy as jnp
import numpy as np
from jax import lax
from jax.experimental import pallas as pl
from jax.experimental.pallas import tpu as pltpu
from jax.sharding import PartitionSpec as P

DN = 128
DR = 64
DV = 128
KVR = 512
EPS = 1e-06
ROPE_BASE = 10000.0
LOG2E = 1.4426950408889634
SCALE = (DN + DR) ** (-0.5)
NEG = -1e30
MIB = 2**20
MESH = pl.DeviceIdType.MESH
f32 = jnp.float32
bf16 = jnp.bfloat16
VMEM = pltpu.VMEM
DMA = pltpu.SemaphoreType.DMA

OWN = 128
SHARDS = 8
LENGTH = OWN * SHARDS
WIDE = 2048
FS_OWN = 352
FE_OWN = 176
HID = 768
QCOLS = 384
LATENT_ROWS = 640


def vmem():
    return pl.BlockSpec(memory_space=pltpu.VMEM)


def anym():
    return pl.BlockSpec(memory_space=pl.ANY)


def dot(a, b):
    return jnp.dot(a, b, preferred_element_type=f32)


def dot_nt(a, b):
    return lax.dot_general(a, b, (((1,), (1,)), ((), ())), preferred_element_type=f32)


def dot_tn(a, b):
    return lax.dot_general(a, b, (((0,), (0,)), ((), ())), preferred_element_type=f32)


def neighbours():
    t = lax.axis_index("tensor")
    x = t // 4
    z = t % 4
    zp = lax.rem(z + 1, 4)
    zm = lax.rem(z + 3, 4)
    z2 = lax.rem(z + 2, 4)
    own = x * 4
    far = (1 - x) * 4
    return dict(
        me=t, tp=own + zp, tm=own + zm, t2=own + z2, tx=far + z, xp=far + zp, xm=far + zm, x2=far + z2
    )


def copies_of():
    d = lax.axis_index("dp")
    c = lax.rem(d, 2)
    y = lax.rem(d // 2, 4)
    plane = d // 8
    here = plane * 8 + c
    return dict(
        c=c, y=y, core=d + 1 - 2 * c, yp=here + lax.rem(y + 1, 4) * 2, ym=here + lax.rem(y + 3, 4) * 2,
        xo=(1 - plane) * 8 + y * 2 + c,
    )


def entry_barrier(tensor=(), dp=()):
    sem = pltpu.get_barrier_semaphore()
    for peer in tensor:
        pl.semaphore_signal(sem, inc=1, device_id={"tensor": peer}, device_id_type=MESH)
    for peer in dp:
        pl.semaphore_signal(sem, inc=1, device_id={"dp": peer}, device_id_type=MESH)
    pl.semaphore_wait(sem, len(tensor) + len(dp))


def ring_peers(n):
    return (n["tp"], n["tm"], n["tx"])


def added(a, b):
    return (a.astype(f32) + b.astype(f32)).astype(bf16)


class YSum:
    def __init__(self, d, rows, a_ref, got, ss, rs):
        self.d, self.rows, self.a, self.got, self.ss, self.rs = d, rows, a_ref, got, ss, rs
        self.pending = None
        self.all = []

    def piece(self, way, hops):
        owner = lax.rem(self.d["y"] + ((3 - hops) if way == 0 else (1 + hops)) + 4, 4)
        start = pl.multiple_of((owner * 2 + way) * self.rows, 16)
        return pl.ds(start, self.rows)

    def step(self, s):
        if s:
            for c in self.pending:
                c.wait_recv()
            for way in range(2):
                here = self.piece(way, s)
                self.got[s - 1, way] = added(self.got[s - 1, way], self.a[here, :])
        if s == 3:
            return
        self.pending = []
        for way in range(2):
            src = self.a.at[self.piece(way, 0)] if s == 0 else self.got.at[s - 1, way]
            c = pltpu.make_async_remote_copy(
                src_ref=src,
                dst_ref=self.got.at[s, way],
                send_sem=self.ss.at[s * 2 + way],
                recv_sem=self.rs.at[s * 2 + way],
                device_id={"dp": self.d["yp"] if way == 0 else self.d["ym"]},
                device_id_type=MESH,
            )
            c.start()
            self.pending.append(c)
            self.all.append(c)

    def close(self):
        for c in self.all:
            c.wait_send()


class YGather:
    def __init__(self, d, rows, g_ref, ss, rs):
        self.d, self.rows, self.g, self.ss, self.rs = d, rows, g_ref, ss, rs
        self.all = []

    def send(self, i, slot, start, count, way):
        view = self.g.at[slot, pl.ds(start, count)]
        c = pltpu.make_async_remote_copy(
            src_ref=view,
            dst_ref=view,
            send_sem=self.ss.at[i],
            recv_sem=self.rs.at[i],
            device_id={"dp": self.d["yp"] if way == 0 else self.d["ym"]},
            device_id_type=MESH,
        )
        c.start()
        self.all.append(c)

    def step(self, s):
        y = self.d["y"]
        if s == 0:
            self.send(0, y, 0, 2 * self.rows, 0)
            self.send(1, y, 0, 2 * self.rows, 1)
        elif s == 1:
            self.all[0].wait_recv()
            self.send(2, lax.rem(y + 3, 4), 0, self.rows, 0)
            self.all[1].wait_recv()
            self.send(3, lax.rem(y + 1, 4), self.rows, self.rows, 1)
        else:
            self.all[2].wait_recv()
            self.all[3].wait_recv()

    def close(self):
        for c in self.all:
            c.wait_send()


def dp_copy(src, dst, ss, rs, peer):
    return pltpu.make_async_remote_copy(
        src_ref=src, dst_ref=dst, send_sem=ss, recv_sem=rs, device_id={"dp": peer}, device_id_type=MESH
    )


def sender(ss, rs):
    def send(i, src, dst, dev):
        return pltpu.make_async_remote_copy(
            src_ref=src,
            dst_ref=dst,
            send_sem=ss.at[i],
            recv_sem=rs.at[i],
            device_id={"tensor": dev},
            device_id_type=MESH,
        )

    return send


def gather_ring(n, x_ref, o_ref, ss, rs, on_shard=None):
    send = sender(ss, rs)
    on_shard = on_shard or (lambda slot: None)

    def s(i, src, slot, o, k, dev):
        return send(i, src, o_ref.at[slot, pl.ds(o, k)], dev)

    def part(slot, o, k):
        return o_ref.at[slot, pl.ds(o, k)]

    me, tp, tm, tx, t2, xp, xm, x2 = (n[k] for k in ("me", "tp", "tm", "tx", "t2", "xp", "xm", "x2"))
    s1 = s(0, x_ref, me, 0, 128, tp)
    s2 = s(1, x_ref, me, 0, 128, tm)
    s3 = s(2, x_ref, me, 0, 128, tx)
    s1.start()
    s2.start()
    s3.start()
    on_shard(me)
    s1.wait_recv()
    s4 = s(3, part(tm, 0, 64), tm, 0, 64, tp)
    s6 = s(5, part(tm, 0, 80), tm, 0, 80, tx)
    s4.start()
    s6.start()
    s2.wait_recv()
    s5 = s(4, part(tp, 64, 64), tp, 64, 64, tm)
    s7 = s(6, part(tp, 48, 80), tp, 48, 80, tx)
    s5.start()
    s7.start()
    s3.wait_recv()
    s8 = s(7, part(tx, 80, 48), tx, 80, 48, tp)
    s9 = s(8, part(tx, 0, 48), tx, 0, 48, tm)
    s8.start()
    s9.start()
    on_shard(tm)
    s6.wait_recv()
    s10 = s(9, part(xm, 0, 64), xm, 0, 64, tp)
    s10.start()
    s7.wait_recv()
    s11 = s(10, part(xp, 64, 64), xp, 64, 64, tm)
    s11.start()
    on_shard(tp)
    on_shard(tx)
    s4.wait_recv()
    s5.wait_recv()
    on_shard(t2)
    s8.wait_recv()
    on_shard(xm)
    s9.wait_recv()
    on_shard(xp)
    s10.wait_recv()
    s11.wait_recv()
    on_shard(x2)
    for c in (s1, s2, s3, s4, s5, s6, s7, s8, s9, s10, s11):
        c.wait_send()


def reduce_ring(n, pv, ready, bufs, ss, rs, work=None):
    work = work or (lambda point: None)
    send = sender(ss, rs)
    me, tp, tm, tx, t2, xp, xm, x2 = (n[k] for k in ("me", "tp", "tm", "tx", "t2", "xp", "xm", "x2"))
    r10, r11, r8, r9, r6, r7, r4, r5, m1, m2, m3 = bufs

    def s(i, slot, o, k, dst, dev):
        return send(i, pv.at[slot, pl.ds(o, k)], dst, dev)

    def add(slot, o, k, buf):
        here = pv[slot, pl.ds(o, k)].astype(f32) + buf[...].astype(f32)
        pv[slot, pl.ds(o, k)] = here.astype(bf16)

    ready("x2")
    s10 = s(0, x2, 0, 64, r10, tm)
    s11 = s(1, x2, 64, 64, r11, tp)
    s10.start()
    s11.start()
    ready("tx")
    s3b = s(10, tx, 48, 32, m3.at[pl.ds(48, 32)], tx)
    s3b.start()
    ready("t2")
    s4 = s(2, t2, 0, 64, r4, tm)
    s5 = s(3, t2, 64, 64, r5, tp)
    s4.start()
    s5.start()
    ready("xm")
    ready("xp")
    s8 = s(4, xm, 80, 48, r8, tm)
    s9 = s(5, xp, 0, 48, r9, tp)
    s8.start()
    s9.start()
    ready("tm")
    ready("tp")
    s1b = s(11, tm, 80, 48, m1.at[pl.ds(80, 48)], tm)
    s2b = s(12, tp, 0, 48, m2.at[pl.ds(0, 48)], tp)
    s1b.start()
    s2b.start()
    work(0)
    s10.wait_recv()
    add(xm, 0, 64, r10)
    s6 = s(6, xm, 0, 80, r6, tx)
    s6.start()
    s11.wait_recv()
    add(xp, 64, 64, r11)
    s7 = s(7, xp, 48, 80, r7, tx)
    s7.start()
    work(1)
    s8.wait_recv()
    add(tx, 80, 48, r8)
    s9.wait_recv()
    add(tx, 0, 48, r9)
    s3a = s(13, tx, 80, 48, m3.at[pl.ds(80, 48)], tx)
    s3c = s(14, tx, 0, 48, m3.at[pl.ds(0, 48)], tx)
    s3a.start()
    s3c.start()
    work(2)
    s4.wait_recv()
    add(tm, 0, 64, r4)
    s6.wait_recv()
    add(tm, 0, 80, r6)
    s1 = s(8, tm, 0, 80, m1.at[pl.ds(0, 80)], tm)
    s1.start()
    work(3)
    s5.wait_recv()
    add(tp, 64, 64, r5)
    s7.wait_recv()
    add(tp, 48, 80, r7)
    s2 = s(9, tp, 48, 80, m2.at[pl.ds(48, 80)], tp)
    s2.start()
    work(4)
    ready("me")
    for c in (s3a, s3b, s3c, s1b, s2b, s1, s2):
        c.wait_recv()
    for c in (s1, s1b, s2, s2b, s3a, s3b, s3c, s4, s5, s6, s7, s8, s9, s10, s11):
        c.wait_send()


def reduce_scratch(columns):
    rows = (64, 64, 48, 48, 80, 80, 64, 64, 128, 128, 128)
    return [VMEM((r, columns), bf16) for r in rows]


def load_partials(n, p_ref, pv, ls):
    order = ("x2", "tx", "t2", "xm", "xp", "tm", "tp", "me")
    copies = {}
    for i, name in enumerate(order):
        copies[name] = pltpu.make_async_copy(p_ref.at[n[name]], pv.at[n[name]], ls.at[i])
        copies[name].start()
    return lambda name: copies[name].wait()


def inverse_rms(v):
    return lax.rsqrt(jnp.mean(v * v, axis=-1, keepdims=True) + EPS)


def turn(v, cos, sin):
    lane = lax.broadcasted_iota(jnp.int32, v.shape, 1)
    low = lax.rem(lane, 64) < 32
    swapped = jnp.where(low, pltpu.roll(v, 96, 1), pltpu.roll(v, 32, 1))
    return v * cos + swapped * sin


def fetch_latent_weights(kvd_hbm, kvd_ref, sems):
    copies = [
        pltpu.make_async_copy(kvd_hbm, kvd_ref.at[pl.ds(0, KVR + DR)], sems.at[0]),
        pltpu.make_async_copy(kvd_hbm.at[pl.ds(KVR, DR)], kvd_ref.at[pl.ds(KVR + DR, DR)], sems.at[1]),
    ]
    for c in copies:
        c.start()
    return copies


def project_kernel(
    x_ref, gain_ref, wq_hbm, kvd_hbm, lgain_ref, kvup_ref, cos_ref, sin_ref,
    normed_ref, q_ref, kvw_ref, kr_ref, lnorm_ref, latent_ref,
    xall, wq_ref, kvd_ref, ss, rs, ls,
):
    n = neighbours()
    wcopy = pltpu.make_async_copy(wq_hbm, wq_ref, ls.at[2])
    wcopy.start()
    copies = fetch_latent_weights(kvd_hbm, kvd_ref, ls)
    entry_barrier(ring_peers(n))

    def compute(slot, src):
        x = src.astype(f32)
        normed = (x * inverse_rms(x) * gain_ref[...].astype(f32)).astype(bf16)
        normed_ref[slot] = normed
        raw = dot(normed, wq_ref[...])
        rows = pl.ds(pl.multiple_of(slot * OWN, OWN), OWN)
        cos = cos_ref[rows, :]
        sin = sin_ref[rows, :]
        q_ref[slot, :, :128] = raw[:, :128].astype(bf16)
        q_ref[slot, :, 128:256] = raw[:, 192:320].astype(bf16)
        rope = jnp.concatenate([raw[:, 128:192], raw[:, 320:384]], axis=1)
        q_ref[slot, :, 256:] = turn(rope, cos, sin).astype(bf16)
        raw = dot_nt(normed, kvd_ref[...])
        latent = raw[:, :KVR]
        latent_ref[slot] = latent
        lnorm = (latent * inverse_rms(latent) * lgain_ref[...].astype(f32)).astype(bf16)
        lnorm_ref[slot] = lnorm
        kr_ref[slot] = turn(raw[:, KVR:], cos, sin).astype(bf16)
        kvw_ref[slot] = dot(lnorm, kvup_ref[...]).astype(bf16)

    started = []

    def on_shard(slot):
        if not started:
            started.append(1)
            for c in copies + [wcopy]:
                c.wait()
            compute(slot, x_ref[...])
        else:
            compute(slot, xall[slot])

    gather_ring(n, x_ref, xall, ss, rs, on_shard)


def project(x, gain, wq, kvd, lgain, kvup, cos, sin):
    def out(c, t):
        return jax.ShapeDtypeStruct((SHARDS, OWN, c), t)

    outs = (out(WIDE, bf16), out(QCOLS, bf16), out(512, bf16), out(128, bf16), out(KVR, bf16), out(KVR, f32))
    return pl.pallas_call(
        project_kernel,
        out_shape=outs,
        in_specs=[vmem(), vmem(), anym(), anym(), vmem(), vmem(), vmem(), vmem()],
        out_specs=[vmem()] * 6,
        scratch_shapes=[
            VMEM((SHARDS, OWN, WIDE), bf16),
            VMEM((WIDE, QCOLS), bf16),
            VMEM((LATENT_ROWS, WIDE), bf16),
            DMA((11,)),
            DMA((11,)),
            DMA((3,)),
        ],
        compiler_params=pltpu.CompilerParams(
            collective_id=0, has_side_effects=True, vmem_limit_bytes=48 * MIB
        ),
        cost_estimate=pl.CostEstimate(flops=5 * 10**9, bytes_accessed=2 * 10**7, transcendentals=0),
        name="project",
    )(x, gain, wq, kvd, lgain, kvup, cos, sin)


KB = 256


def masked(s, key0, query0, prefix):
    keys = key0 + lax.broadcasted_iota(jnp.int32, s.shape, 0)
    rows = query0 + lax.broadcasted_iota(jnp.int32, s.shape, 1)
    return jnp.where((keys <= rows) | (keys < prefix), s, NEG)


def key_extent(query_block):
    return max(2, query_block + 1)


def head_lanes(shape, head):
    lane = lax.broadcasted_iota(jnp.int32, shape, 1)
    return (lane >= 64) if head else (lane < 64)


def head_query(q_ref, rows, head):
    rope = q_ref[rows, 256:QCOLS]
    rope = jnp.where(head_lanes(rope.shape, head), rope.astype(f32), 0.0).astype(bf16)
    return jnp.concatenate([q_ref[rows, head * 128 : head * 128 + 128], rope], axis=1)


def head_key(kvw_ref, kr_ref, rows, head):
    return jnp.concatenate([kvw_ref[rows, head * 256 : head * 256 + 128], kr_ref[rows, :]], axis=1)


def attend_kernel(prefix_ref, q_ref, kvw_ref, kr_ref, wo_ref, attn_ref, lse_ref, ot_ref, p_ref, s_scr):
    prefix = prefix_ref[0]
    for i in range(4):
        rows = pl.ds(i * KB, KB)
        for h in range(2):
            q = head_query(q_ref, rows, h)
            top = jnp.full((1, KB), NEG, f32)
            for k in range(key_extent(i)):
                keys = pl.ds(k * KB, KB)
                s = dot_nt(head_key(kvw_ref, kr_ref, keys, h), q)
                if k >= i:
                    s = masked(s, k * KB, i * KB, prefix)
                s_scr[keys, :] = s
                top = jnp.maximum(top, jnp.max(s, axis=0, keepdims=True))
            top = top * (SCALE * LOG2E)
            total = jnp.zeros((1, KB), f32)
            out = jnp.zeros((DV, KB), f32)
            for k in range(key_extent(i)):
                keys = pl.ds(k * KB, KB)
                p = jnp.exp2(s_scr[keys, :] * (SCALE * LOG2E) - top)
                total = total + jnp.sum(p, axis=0, keepdims=True)
                out = out + dot_tn(kvw_ref[keys, h * 256 + 128 : h * 256 + 256], p.astype(bf16))
            out = out / total
            lse_ref[h : h + 1, rows] = top + jnp.log2(total)
            ot_ref[h, :, rows] = out
            attn_ref[rows, h * 128 : h * 128 + 128] = out.T.astype(bf16)
        p_ref[rows, :] = dot(attn_ref[rows, :], wo_ref[...]).astype(bf16)


def attend(prefix, q, kvw, kr, wo):
    return pl.pallas_call(
        attend_kernel,
        out_shape=(
            jax.ShapeDtypeStruct((LENGTH, 256), bf16),
            jax.ShapeDtypeStruct((2, LENGTH), f32),
            jax.ShapeDtypeStruct((2, DV, LENGTH), f32),
            jax.ShapeDtypeStruct((LENGTH, WIDE), bf16),
        ),
        in_specs=[pl.BlockSpec(memory_space=pltpu.SMEM)] + [vmem()] * 4,
        out_specs=[vmem()] * 4,
        scratch_shapes=[VMEM((LENGTH, KB), f32)],
        compiler_params=pltpu.CompilerParams(vmem_limit_bytes=48 * MIB),
        cost_estimate=pl.CostEstimate(flops=25 * 10**8, bytes_accessed=10**7, transcendentals=2 * 10**6),
        name="attend",
    )(prefix, q, kvw, kr, wo)


def own_total(n, pv, bufs):
    m1, m2, m3 = bufs[8:]
    return pv[n["me"]].astype(f32) + m1[...].astype(f32) + m2[...].astype(f32) + m3[...].astype(f32)


def fetch_hidden_weights(sg, rt, eg, dst, zero_ref, sems, base):
    pieces = [(sg, 0, FS_OWN), (eg.at[0], 384, FE_OWN), (eg.at[1], 384 + FE_OWN, FE_OWN)]
    pieces += [(zero_ref, 736, 32), (rt if rt is not None else zero_ref, FS_OWN, 32)]
    copies = []
    for i, (src, at, count) in enumerate(pieces):
        c = pltpu.make_async_copy(src, dst.at[pl.ds(at, count)], sems.at[base + i])
        c.start()
        copies.append(c)
    return copies


def ffn_rows(mixed, grad, route, wg_ref, wu_ref, wd_ref):
    a = dot_nt(mixed, wg_ref[...])
    b = dot_nt(mixed, wu_ref[...])
    dm = dot_nt(grad, wd_ref[...])
    first = (route == 0).astype(f32)
    second = (route == 1).astype(f32)
    l0 = a[:, FS_OWN : FS_OWN + 1]
    l1 = a[:, FS_OWN + 1 : FS_OWN + 2]
    top = jnp.maximum(l0, l1)
    e0 = jnp.exp(l0 - top)
    e1 = jnp.exp(l1 - top)
    r0 = e0 / (e0 + e1)
    r1 = e1 / (e0 + e1)
    col = lax.broadcasted_iota(jnp.int32, (1, HID), 1)
    is_shared = col < 384
    in0 = (col >= 384) & (col < 384 + FE_OWN)
    in1 = (col >= 384 + FE_OWN) & (col < 384 + 2 * FE_OWN)
    gate = jnp.where(is_shared, 1.0, 0.0) + jnp.where(in0, first * r0, 0.0) + jnp.where(in1, second * r1, 0.0)
    sig = jax.nn.sigmoid(a)
    silu = a * sig
    act = silu * b
    m = (gate * act).astype(bf16)
    scaled = dm * gate
    down = dm * act
    g0 = first * jnp.sum(jnp.where(in0, down, 0.0), axis=1, keepdims=True)
    g1 = second * jnp.sum(jnp.where(in1, down, 0.0), axis=1, keepdims=True)
    mean = r0 * g0 + r1 * g1
    da = scaled * b * (sig * (1.0 + a * (1.0 - sig)))
    da = da + jnp.where(col == FS_OWN, r0 * (g0 - mean), 0.0) + jnp.where(col == FS_OWN + 1, r1 * (g1 - mean), 0.0)
    da = da.astype(bf16)
    db = (scaled * silu).astype(bf16)
    return m, da, db, dot(da, wg_ref[...]) + dot(db, wu_ref[...])


def hidden_ffn_kernel(
    p_ref, x_ref, gain_ref, grad_hbm, routes_ref, sg, su, sd, eg, eu, ed, rt_ref,
    hidden_ref, mixed_ref, m_ref, da_ref, db_ref, p2_ref, gsum_ref,
    pv, own, gall, wg_ref, wu_ref, wd_ref, zero_ref, *rest,
):
    bufs, (ss, rs, gs, gr, ls, ws) = rest[:11], rest[11:]
    n = neighbours()
    ready = load_partials(n, p_ref, pv, ls)
    zero_ref[...] = jnp.zeros_like(zero_ref)
    copies = fetch_hidden_weights(sg, rt_ref, eg, wg_ref, zero_ref, ws, 0)
    copies += fetch_hidden_weights(su, None, eu, wu_ref, zero_ref, ws, 5)
    copies += fetch_hidden_weights(sd, None, ed, wd_ref, zero_ref, ws, 10)
    gcopy = pltpu.make_async_copy(grad_hbm, gall, ws.at[15])
    gcopy.start()
    entry_barrier(ring_peers(n))
    reduce_ring(n, pv, ready, bufs, ss, rs)
    hidden = x_ref[...].astype(f32) + own_total(n, pv, bufs)
    hidden_ref[...] = hidden
    own[...] = (hidden * inverse_rms(hidden) * gain_ref[...].astype(f32)).astype(bf16)
    mixed_ref[n["me"]] = own[...]
    gsum_ref[...] = jnp.zeros_like(gsum_ref)
    waiting = []
    done = []

    def on_shard(slot):
        waiting.append(slot)
        if len(waiting) < 2:
            return
        if not done:
            for c in copies + [gcopy]:
                c.wait()
        done.append(1)
        pair = list(waiting)
        waiting.clear()
        mixed = jnp.concatenate([mixed_ref[s] for s in pair], axis=0)
        grad = jnp.concatenate([gall[s] for s in pair], axis=0)
        route = jnp.concatenate([routes_ref[s] for s in pair], axis=0)
        m, da, db, back = ffn_rows(mixed, grad, route, wg_ref, wu_ref, wd_ref)
        gsum_ref[...] += jnp.sum(back * mixed.astype(f32), axis=0, keepdims=True)
        back = back.astype(bf16)
        for i, s in enumerate(pair):
            part = slice(i * OWN, i * OWN + OWN)
            m_ref[s] = m[part]
            da_ref[s] = da[part]
            db_ref[s] = db[part]
            p2_ref[s] = back[part]

    gather_ring(n, own, mixed_ref, gs, gr, on_shard)


def hidden_ffn(p, x, gain, grad, routes, sg, su, sd, eg, eu, ed, rt):
    def out(c, t=bf16):
        return jax.ShapeDtypeStruct((SHARDS, OWN, c), t)

    row = jax.ShapeDtypeStruct((1, WIDE), f32)
    outs = (jax.ShapeDtypeStruct((OWN, WIDE), f32), out(WIDE), out(HID), out(HID), out(HID), out(WIDE), row)
    return pl.pallas_call(
        hidden_ffn_kernel,
        out_shape=outs,
        in_specs=[anym(), vmem(), vmem(), anym(), vmem()] + [anym()] * 7,
        out_specs=[vmem()] * 7,
        scratch_shapes=[
            VMEM((SHARDS, OWN, WIDE), bf16),
            VMEM((OWN, WIDE), bf16),
            VMEM((SHARDS, OWN, WIDE), bf16),
            VMEM((HID, WIDE), bf16),
            VMEM((HID, WIDE), bf16),
            VMEM((HID, WIDE), bf16),
            VMEM((32, WIDE), bf16),
        ]
        + reduce_scratch(WIDE)
        + [DMA((15,)), DMA((15,)), DMA((11,)), DMA((11,)), DMA((8,)), DMA((16,))],
        compiler_params=pltpu.CompilerParams(
            collective_id=1, has_side_effects=True, vmem_limit_bytes=60 * MIB
        ),
        cost_estimate=pl.CostEstimate(flops=16 * 10**9, bytes_accessed=3 * 10**7, transcendentals=10**6),
        name="hidden_ffn",
    )(p.reshape(SHARDS, OWN, WIDE), x, gain, grad, routes, sg, su, sd, eg, eu, ed, rt)


def rows_of(ref):
    return ref[...].reshape(LENGTH, ref.shape[-1])


BLOCKS = 9


def turn_kernel(
    p_ref, hidden_ref, grad_ref, gain_ref, mixed_ref, gall_ref, m_ref, da_ref, db_ref, sd, ed,
    hgrad_ref, low_ref, half_ref, router_ref, moe_hbm,
    pv, dw_scr, core_scr, moe_scr, wd_ref, zero_ref, *rest,
):
    bufs, (ss, rs, cs, cr, ls, ws, os) = rest[:11], rest[11:]
    n = neighbours()
    d = copies_of()
    ready = load_partials(n, p_ref, pv, ls)
    zero_ref[...] = jnp.zeros_like(zero_ref)
    copies = fetch_hidden_weights(sd, None, ed, wd_ref, zero_ref, ws, 0)
    entry_barrier(ring_peers(n), (d["core"],))
    stores = []
    crossed = []
    theirs = pl.multiple_of((1 - d["c"]) * OWN, OWN)
    mine = pl.multiple_of(d["c"] * OWN, OWN)

    def product(index, left, right, block):
        k = index * 3 + block
        left = left[:, :, pl.ds(block * 256, 256)].reshape(LENGTH, 256)
        dw_scr[k] = dot_tn(left, rows_of(right)).astype(bf16)
        c = dp_copy(dw_scr.at[k, pl.ds(theirs, OWN)], core_scr.at[k], cs.at[k], cr.at[k], d["core"])
        c.start()
        crossed.append((k, c))
        if k == 1:
            router_ref[...] = dw_scr[1, FS_OWN - 256 : FS_OWN - 240, :]

    def expert_sum(block):
        two = pl.ds(block * 2, 2)
        moe_scr[two] = dot(m_ref[two].reshape(256, HID), wd_ref[...]).astype(bf16).reshape(2, OWN, WIDE)
        c = pltpu.make_async_copy(moe_scr.at[two], moe_hbm.at[two], os.at[block])
        c.start()
        stores.append(c)

    def meet():
        k, c = crossed.pop(0)
        c.wait_recv()
        half_ref[k] = added(dw_scr[k, pl.ds(mine, OWN), :], core_scr[k])
        stores.append(c)

    jobs = [functools.partial(product, 2, m_ref, gall_ref, b) for b in range(3)]
    jobs += [functools.partial(product, 0, da_ref, mixed_ref, b) for b in range(3)]
    jobs += [functools.partial(product, 1, db_ref, mixed_ref, b) for b in range(3)]
    jobs += [functools.partial(expert_sum, b) for b in range(4)]
    plan = {0: 3, 1: 2, 2: 2, 3: 2, 4: 4}

    def work(point):
        if point == 4:
            for c in copies:
                c.wait()
        for _ in range(plan[point]):
            jobs.pop(0)()
        if point == 4:
            while crossed:
                meet()

    reduce_ring(n, pv, ready, bufs, ss, rs, work)
    total = own_total(n, pv, bufs)
    hidden = hidden_ref[...]
    inv = inverse_rms(hidden)
    unit = hidden * inv
    scaled = total * gain_ref[...].astype(f32)
    back = inv * (scaled - unit * jnp.mean(scaled * unit, axis=-1, keepdims=True))
    hgrad = grad_ref[...].astype(f32) + back
    hgrad_ref[...] = hgrad
    low_ref[...] = hgrad.astype(bf16)
    for c in stores[:4]:
        c.wait()
    for c in stores[4:]:
        c.wait_send()


def turn_back(p, hidden, grad, gain, mixed, gall, m, da, db, sd, ed):
    outs = (
        jax.ShapeDtypeStruct((OWN, WIDE), f32),
        jax.ShapeDtypeStruct((OWN, WIDE), bf16),
        jax.ShapeDtypeStruct((BLOCKS, OWN, WIDE), bf16),
        jax.ShapeDtypeStruct((16, WIDE), bf16),
        jax.ShapeDtypeStruct((SHARDS, OWN, WIDE), bf16),
    )
    return pl.pallas_call(
        turn_kernel,
        out_shape=outs,
        in_specs=[anym()] + [vmem()] * 8 + [anym()] * 2,
        out_specs=[vmem()] * 4 + [anym()],
        scratch_shapes=[
            VMEM((SHARDS, OWN, WIDE), bf16),
            VMEM((BLOCKS, 256, WIDE), bf16),
            VMEM((BLOCKS, OWN, WIDE), bf16),
            VMEM((SHARDS, OWN, WIDE), bf16),
            VMEM((HID, WIDE), bf16),
            VMEM((32, WIDE), bf16),
        ]
        + reduce_scratch(WIDE)
        + [DMA((15,)), DMA((15,)), DMA((BLOCKS,)), DMA((BLOCKS,)), DMA((8,)), DMA((5,)), DMA((4,))],
        compiler_params=pltpu.CompilerParams(
            collective_id=2, has_side_effects=True, vmem_limit_bytes=60 * MIB
        ),
        cost_estimate=pl.CostEstimate(flops=13 * 10**9, bytes_accessed=4 * 10**7, transcendentals=0),
        name="turn_back",
    )(p, hidden, grad, gain, mixed, gall, m, da, db, sd, ed)


QUARTER = 288


def gather_kernel(x_ref, half_ref, o_ref, sum_ref, got, ss, rs, ys, yr, ls):
    n = neighbours()
    d = copies_of()
    entry_barrier(ring_peers(n), (d["yp"], d["ym"]))
    local = pltpu.make_async_copy(x_ref, o_ref.at[n["me"]], ls.at[0])
    local.start()
    ysum = YSum(d, QUARTER // 2, half_ref, got, ys, yr)
    seen = []

    def on_shard(slot):
        seen.append(slot)
        step = {1: 0, 3: 1, 5: 2}.get(len(seen))
        if step is not None:
            ysum.step(step)

    gather_ring(n, x_ref, o_ref, ss, rs, on_shard)
    ysum.step(3)
    sum_ref[pl.ds(0, QUARTER // 2), :] = got[2, 0]
    sum_ref[pl.ds(QUARTER // 2, QUARTER // 2), :] = got[2, 1]
    ysum.close()
    local.wait()


def gather(x, half):
    return pl.pallas_call(
        gather_kernel,
        out_shape=(
            jax.ShapeDtypeStruct((SHARDS, OWN, WIDE), bf16),
            jax.ShapeDtypeStruct((QUARTER, WIDE), bf16),
        ),
        in_specs=[anym(), vmem()],
        out_specs=(anym(), vmem()),
        scratch_shapes=[
            VMEM((3, 2, QUARTER // 2, WIDE), bf16),
            DMA((11,)),
            DMA((11,)),
            DMA((6,)),
            DMA((6,)),
            DMA((1,)),
        ],
        compiler_params=pltpu.CompilerParams(
            collective_id=3, has_side_effects=True, vmem_limit_bytes=32 * MIB
        ),
        name="gather_grad",
    )(x, half)


LATE = 3072
PACK_COLS = 1280
EXT = WIDE + PACK_COLS


def attend_back_kernel(
    prefix_ref, hall_ref, wo_ref, q_ref, kvw_ref, kr_ref, lse_ref, ot_ref,
    kvup_ref, latent_ref, lgain_ref, cos_ref, sin_ref, wq_ref, kvd_hbm,
    normed_ref, lnorm_ref, attn_ref, gain_ref, fgain_ref, gsum_ref, router_ref, ysum_ref,
    p_ref, late_ref, quarter_ref,
    do_scr, dk_scr, dv_scr, jq_scr, jk_scr, kvg_scr, kvd_ref, far_scr, ls, xs, xr,
):
    prefix = prefix_ref[0]
    d = copies_of()
    entry_barrier((), (d["xo"],))
    cross = dp_copy(ysum_ref, far_scr, xs.at[0], xr.at[0], d["xo"])
    cross.start()
    copies = fetch_latent_weights(kvd_hbm, kvd_ref, ls)
    for i in range(4):
        rows = pl.ds(i * KB, KB)
        do_scr[rows, :] = dot_nt(hall_ref[rows, :], wo_ref[...]).astype(bf16)
    dk_scr[...] = jnp.zeros_like(dk_scr)
    dv_scr[...] = jnp.zeros_like(dv_scr)
    for i in range(4):
        rows = pl.ds(i * KB, KB)
        plain = []
        turned = jnp.zeros((KB, 128), f32)
        for h in range(2):
            q = head_query(q_ref, rows, h)
            do = do_scr[rows, h * 128 : h * 128 + 128]
            lse = lse_ref[h : h + 1, rows]
            delta = jnp.sum(do.astype(f32).T * ot_ref[h, :, rows], axis=0, keepdims=True)
            dq = jnp.zeros((KB, 256), f32)
            for k in range(key_extent(i)):
                keys = pl.ds(k * KB, KB)
                key = head_key(kvw_ref, kr_ref, keys, h)
                s = dot_nt(key, q)
                if k >= i:
                    s = masked(s, k * KB, i * KB, prefix)
                p = jnp.exp2(s * (SCALE * LOG2E) - lse)
                dp = dot_nt(kvw_ref[keys, h * 256 + 128 : h * 256 + 256], do)
                ds = (p * (dp - delta)).astype(bf16)
                dv_scr[h, keys, :] += dot(p.astype(bf16), do)
                dk_scr[h, keys, :] += dot(ds, q)
                dq = dq + dot_tn(ds, key)
            dq = dq * SCALE
            plain.append(dq[:, :128])
            turned = turned + jnp.where(head_lanes(turned.shape, h), dq[:, 128:], 0.0)
        turned = turn(turned, cos_ref[rows, :], -sin_ref[rows, :])
        j = jnp.concatenate([plain[0], turned[:, :64], plain[1], turned[:, 64:]], axis=1)
        jq_scr[rows, :] = j.astype(bf16)
    for c in copies:
        c.wait()
    gain_sum = jnp.zeros((1, WIDE), f32)
    lgain_sum = jnp.zeros((1, KVR), f32)
    for i in range(4):
        rows = pl.ds(i * KB, KB)
        for h in range(2):
            kvg_scr[rows, h * 256 : h * 256 + 128] = (dk_scr[h, rows, :128] * SCALE).astype(bf16)
            kvg_scr[rows, h * 256 + 128 : h * 256 + 256] = dv_scr[h, rows, :].astype(bf16)
        dkr = (dk_scr[0, rows, 128:] + dk_scr[1, rows, 128:]) * SCALE
        jk_scr[rows, KVR:] = turn(dkr, cos_ref[rows, :], -sin_ref[rows, :]).astype(bf16)
        dl = dot_nt(kvg_scr[rows, :], kvup_ref[...])
        latent = latent_ref[rows, :]
        inv = inverse_rms(latent)
        unit = latent * inv
        lgain_sum = lgain_sum + jnp.sum(dl * unit, axis=0, keepdims=True)
        scaled = dl * lgain_ref[...].astype(f32)
        back = inv * (scaled - unit * jnp.mean(scaled * unit, axis=-1, keepdims=True))
        jk_scr[rows, :KVR] = back.astype(bf16)
        into = dot_nt(jq_scr[rows, :], wq_ref[...]) + dot(jk_scr[rows, :], kvd_ref[...])
        gain_sum = gain_sum + jnp.sum(into * normed_ref[rows, :].astype(f32), axis=0, keepdims=True)
        into = into.astype(bf16)
        for t in range(2):
            p_ref[i * 2 + t, :, :WIDE] = into[t * OWN : t * OWN + OWN]
    late_ref[pl.ds(1536, KVR), :] = dot_tn(lnorm_ref[...], kvg_scr[...]).astype(bf16)
    for i in range(4):
        cols = pl.ds(i * 512, 512)
        late_ref[pl.ds(2048 + i * 256, 256), :] = dot_tn(attn_ref[...], hall_ref[:, cols]).astype(bf16)
        query = dot_tn(normed_ref[:, cols], jq_scr[...]).astype(bf16)
        for c in range(3):
            late_ref[pl.ds(c * 512, 512), i * 128 : i * 128 + 128] = query[:, c * 128 : c * 128 + 128]
    empty = jnp.zeros((1, 192), f32)
    lat = jnp.concatenate([v for t in range(SHARDS) for v in (lgain_sum[:, t * 64 : t * 64 + 64], empty)], axis=1)
    tail = jnp.concatenate(
        [
            gain_sum / gain_ref[...].astype(f32),
            gsum_ref[...] / fgain_ref[...].astype(f32),
            router_ref[:2, :].astype(f32),
            lat,
            jnp.zeros((59, WIDE), f32),
        ],
        axis=0,
    )
    for i in range(8):
        cols = pl.ds(i * KB, KB)
        down = dot_tn(jk_scr[...], normed_ref[:, cols])
        for c in range(4):
            at = WIDE + c * KB
            p_ref[i, :, at : at + KB] = down[c * OWN : c * OWN + OWN].astype(bf16)
        rest = jnp.concatenate(
            [down[KVR : KVR + DR] + down[KVR + DR :], tail[:, i * KB : i * KB + KB]], axis=0
        )
        p_ref[i, :, WIDE + 4 * KB :] = rest.astype(bf16)
    cross.wait_recv()
    quarter_ref[...] = added(ysum_ref[...], far_scr[...])
    cross.wait_send()


def attend_back(*args):
    return pl.pallas_call(
        attend_back_kernel,
        out_shape=(
            jax.ShapeDtypeStruct((SHARDS, OWN, EXT), bf16),
            jax.ShapeDtypeStruct((LATE, 512), bf16),
            jax.ShapeDtypeStruct((QUARTER, WIDE), bf16),
        ),
        in_specs=[pl.BlockSpec(memory_space=pltpu.SMEM)] + [vmem()] * 13 + [anym()] + [vmem()] * 8,
        out_specs=[vmem()] * 3,
        scratch_shapes=[
            VMEM((LENGTH, 256), bf16),
            VMEM((2, LENGTH, 256), f32),
            VMEM((2, LENGTH, DV), f32),
            VMEM((LENGTH, QCOLS), bf16),
            VMEM((LENGTH, LATENT_ROWS), bf16),
            VMEM((LENGTH, 512), bf16),
            VMEM((LATENT_ROWS, WIDE), bf16),
            VMEM((QUARTER, WIDE), bf16),
            DMA((2,)),
            DMA((1,)),
            DMA((1,)),
        ],
        compiler_params=pltpu.CompilerParams(
            collective_id=4, has_side_effects=True, vmem_limit_bytes=60 * MIB
        ),
        cost_estimate=pl.CostEstimate(flops=18 * 10**9, bytes_accessed=4 * 10**7, transcendentals=2 * 10**6),
        name="attend_back",
    )(*args)


def last_kernel(p_ref, x_ref, hgrad_ref, gain_ref, quarter_ref, out_ref, pack_ref, all_ref, pv, *rest):
    bufs, (ss, rs, ys, yr, ls) = rest[:11], rest[11:]
    n = neighbours()
    d = copies_of()
    ready = load_partials(n, p_ref, pv, ls)
    all_ref[d["y"]] = quarter_ref[...]
    entry_barrier(ring_peers(n), (d["yp"], d["ym"]))
    ygather = YGather(d, QUARTER // 2, all_ref, ys, yr)

    def work(point):
        if point == 0:
            ygather.step(0)
        if point == 4:
            ygather.step(1)

    reduce_ring(n, pv, ready, bufs, ss, rs, work)
    total = own_total(n, pv, bufs)
    pack_ref[...] = total[:, WIDE:].astype(bf16)
    total = total[:, :WIDE]
    x = x_ref[...].astype(f32)
    inv = inverse_rms(x)
    unit = x * inv
    scaled = total * gain_ref[...].astype(f32)
    back = inv * (scaled - unit * jnp.mean(scaled * unit, axis=-1, keepdims=True))
    out_ref[...] = (hgrad_ref[...] + back).astype(bf16)
    ygather.step(2)
    ygather.close()


def last(p, x, hgrad, gain, quarter):
    return pl.pallas_call(
        last_kernel,
        out_shape=(
            jax.ShapeDtypeStruct((OWN, WIDE), bf16),
            jax.ShapeDtypeStruct((OWN, PACK_COLS), bf16),
            jax.ShapeDtypeStruct((4, QUARTER, WIDE), bf16),
        ),
        in_specs=[anym()] + [vmem()] * 4,
        out_specs=[vmem()] * 3,
        scratch_shapes=[VMEM((SHARDS, OWN, EXT), bf16)]
        + reduce_scratch(EXT)
        + [DMA((15,)), DMA((15,)), DMA((4,)), DMA((4,)), DMA((8,))],
        compiler_params=pltpu.CompilerParams(
            collective_id=5, has_side_effects=True, vmem_limit_bytes=48 * MIB
        ),
        cost_estimate=pl.CostEstimate(flops=10**7, bytes_accessed=2 * 10**7, transcendentals=0),
        name="last",
    )(p, x, hgrad, gain, quarter)


LATE_HALF = 1792
LATE_PIECE = LATE_HALF // 8


def finish_kernel(
    late_hbm, pack_ref, all_ref,
    q_ref, kv_ref, o_ref, down_ref, tail_ref, sg, su, sd, eg, eu, ed,
    late, core_scr, half, got, near, far_scr, lall, full, wide, ls, cs, cr, ys, yr, xs, xr, gs, gr, os,
):
    d = copies_of()
    c = d["c"]
    load = pltpu.make_async_copy(late_hbm, late.at[pl.ds(0, LATE)], ls.at[0])
    load.start()
    for i in range(2):
        at = LATE + i * OWN
        late[at : at + OWN, :] = pack_ref[:, i * 512 : i * 512 + 512]
    late[LATE + 256 : LATE + 384, :256] = pack_ref[:, 1024:]
    late[LATE + 256 : LATE + 384, 256:] = jnp.zeros((OWN, 256), bf16)
    late[LATE + 384 :, :] = jnp.zeros((OWN, 512), bf16)
    entry_barrier((), (d["core"], d["yp"], d["ym"], d["xo"]))
    load.wait()
    theirs = pl.ds(pl.multiple_of((1 - c) * LATE_HALF, OWN), LATE_HALF)
    mine = pl.ds(pl.multiple_of(c * LATE_HALF, OWN), LATE_HALF)
    first = dp_copy(late.at[theirs], core_scr, cs.at[0], cr.at[0], d["core"])
    first.start()
    swap = dp_copy(all_ref, full.at[c], cs.at[1], cr.at[1], d["core"])
    swap.start()
    first.wait_recv()
    half[...] = added(late[mine, :], core_scr[...])
    ysum = YSum(d, LATE_PIECE, half, got, ys, yr)
    ysum.step(0)
    full[c] = all_ref[...]
    ysum.step(1)
    swap.wait_recv()
    stores = []

    def widen(k):
        for core in range(2):
            wide[pl.ds(k * 256 + core * OWN, OWN), :] = full[core, pl.ds(k * OWN, OWN), :].astype(f32)

    def put(start, count, dst):
        copy = pltpu.make_async_copy(wide.at[pl.ds(start, count)], dst, os.at[len(stores)])
        copy.start()
        stores.append(copy)

    def widen_third(index, shared, experts):
        for block in range(3):
            widen(index * 3 + block)
        base = index * HID
        put(base, FS_OWN, shared)
        put(base + 384, FE_OWN, experts.at[0])
        put(base + 384 + FE_OWN, FE_OWN, experts.at[1])

    widen_third(0, sg, eg)
    ysum.step(2)
    widen_third(1, su, eu)
    ysum.step(3)
    for way in range(2):
        near[pl.ds(way * LATE_PIECE, LATE_PIECE), :] = got[2, way]
    cross = dp_copy(near, far_scr, xs.at[0], xr.at[0], d["xo"])
    cross.start()
    widen_third(2, sd, ed)
    cross.wait_recv()
    lall[c, d["y"]] = added(near[...], far_scr[...])
    ygather = YGather(d, LATE_PIECE, lall.at[c], gs, gr)
    ygather.step(0)
    ygather.step(1)
    ygather.step(2)
    back = dp_copy(lall.at[c], lall.at[c], cs.at[2], cr.at[2], d["core"])
    back.start()
    back.wait_recv()

    def rows(start, count):
        core, at = divmod(start, LATE_HALF)
        assert at + count <= LATE_HALF
        quarter, at = divmod(at, 2 * LATE_PIECE)
        pieces = []
        while count:
            take = min(count, 2 * LATE_PIECE - at)
            pieces.append(lall[core, quarter, at : at + take, :].astype(f32))
            count -= take
            quarter, at = quarter + 1, 0
        return pieces[0] if len(pieces) == 1 else jnp.concatenate(pieces, axis=0)

    def late_rows(start, count):
        parts = []
        while count:
            take = min(count, LATE_HALF - start % LATE_HALF)
            parts.append(rows(start, take))
            start, count = start + take, count - take
        return parts[0] if len(parts) == 1 else jnp.concatenate(parts, axis=0)

    for k in range(3):
        block = late_rows(k * 512, 512)
        for i in range(4):
            q_ref[pl.ds(i * 512, 512), k * 128 : k * 128 + 128] = block[:, i * 128 : i * 128 + 128]
    kv_ref[...] = late_rows(1536, KVR)
    for i in range(4):
        o_ref[:, i * 512 : i * 512 + 512] = late_rows(2048 + i * 256, 256)
    for i in range(2):
        block = late_rows(LATE + i * OWN, OWN)
        down_ref[pl.ds(i * 256, OWN), :] = block[:, :256]
        down_ref[pl.ds(i * 256 + OWN, OWN), :] = block[:, 256:]
    block = late_rows(LATE + 256, OWN)
    down_ref[pl.ds(KVR, DR), :] = block[:DR, :256]
    tail_ref[...] = block[DR : DR + 16, :256]
    for copy in (first, swap, back, cross):
        copy.wait_send()
    ysum.close()
    ygather.close()
    for copy in stores:
        copy.wait()


def finish(late, pack, quarters):
    def out(*shape):
        return jax.ShapeDtypeStruct(shape, f32)

    shared, experts = out(FS_OWN, WIDE), out(2, FE_OWN, WIDE)
    return pl.pallas_call(
        finish_kernel,
        out_shape=(
            out(WIDE, QCOLS), out(KVR, 512), out(256, WIDE), out(576, 256), out(16, 256),
            shared, shared, shared, experts, experts, experts,
        ),
        in_specs=[anym(), vmem(), vmem()],
        out_specs=[vmem()] * 5 + [anym()] * 6,
        scratch_shapes=[
            VMEM((2 * LATE_HALF, 512), bf16),
            VMEM((LATE_HALF, 512), bf16),
            VMEM((LATE_HALF, 512), bf16),
            VMEM((3, 2, LATE_PIECE, 512), bf16),
            VMEM((2 * LATE_PIECE, 512), bf16),
            VMEM((2 * LATE_PIECE, 512), bf16),
            VMEM((2, 4, 2 * LATE_PIECE, 512), bf16),
            VMEM((2, BLOCKS * OWN, WIDE), bf16),
            VMEM((3 * HID, WIDE), f32),
            DMA((1,)),
            DMA((3,)),
            DMA((3,)),
            DMA((6,)),
            DMA((6,)),
            DMA((1,)),
            DMA((1,)),
            DMA((4,)),
            DMA((4,)),
            DMA((9,)),
        ],
        compiler_params=pltpu.CompilerParams(
            collective_id=6, has_side_effects=True, vmem_limit_bytes=60 * MIB
        ),
        cost_estimate=pl.CostEstimate(flops=10**7, bytes_accessed=3 * 10**7, transcendentals=0),
        name="finish",
    )(late, pack, quarters.reshape(BLOCKS * OWN, WIDE))


def rope_tables():
    half = DR // 2
    frequency = ROPE_BASE ** (-(np.arange(half, dtype=np.float64) * 2.0) / DR)
    angles = np.arange(LENGTH, dtype=np.float64)[:, None] * frequency[None, :]
    cos = np.cos(angles).astype(np.float32)
    sin = np.sin(angles).astype(np.float32)
    return np.concatenate([cos] * 4, axis=1), np.concatenate([-sin, sin, -sin, sin], axis=1)


def after(value, *others):
    return lax.optimization_barrier((value, *others))[0]


def flat(v):
    return v.reshape(LENGTH, v.shape[-1])


def body(
    layer_in, grad_out, routes, prefix, attn_gain, query_proj, kv_down, latent_gain, kv_up,
    out_proj, ffn_gain, router_proj, shared_gate, shared_up, shared_down, expert_gate, expert_up, expert_down,
):
    cos_np, sin_np = rope_tables()
    cos, sin = jnp.asarray(cos_np), jnp.asarray(sin_np)
    again, lgain, fgain = attn_gain[None], latent_gain[None], ffn_gain[None]
    kvd = kv_down.T
    sg, su = shared_gate.T, shared_up.T
    eg, eu = jnp.swapaxes(expert_gate, 1, 2), jnp.swapaxes(expert_up, 1, 2)
    rt = jnp.pad(router_proj.T, ((0, 30), (0, 0)))

    normed, q, kvw, kr, lnorm, latent = map(
        flat, project(layer_in, again, query_proj, kvd, lgain, kv_up, cos, sin)
    )
    grad_all = lax.all_gather(grad_out, "tensor", axis=0, tiled=True).reshape(SHARDS, OWN, WIDE)
    attn, lse, ot, p1 = attend(prefix, q, kvw, kr, out_proj)
    hidden, mixed, m, da, db, p2, gsum = hidden_ffn(
        p1, layer_in, fgain, grad_all, routes.reshape(SHARDS, OWN, 1),
        sg, su, shared_down, eg, eu, expert_down, rt,
    )
    hgrad, low, half, router_rows, moe = turn_back(
        p2, hidden, grad_out, fgain, mixed, grad_all, m, da, db, shared_down, expert_down
    )
    hall, ysum = gather(low, half.reshape(BLOCKS * OWN, WIDE))
    hall = flat(hall)
    moe = lax.psum_scatter(after(flat(moe), hall), "tensor", scatter_dimension=0, tiled=True)
    layer_out = (hidden + moe.astype(f32)).astype(bf16)
    p3, late, quarter = attend_back(
        prefix, hall, out_proj, q, kvw, kr, lse, ot, kv_up, latent, lgain, cos, sin, query_proj, kvd,
        normed, lnorm, attn, again, fgain, gsum, router_rows, ysum,
    )
    input_grad, pack, quarters = last(p3, layer_in, hgrad, again, quarter)
    dq, dkv, do, ddown, tail, dsg, dsu, dsd, deg, deu, ded = finish(late, pack, quarters)
    return (
        layer_out,
        input_grad,
        tail[0],
        dq,
        ddown.T,
        tail[4, : KVR // SHARDS],
        dkv,
        do,
        tail[1],
        tail[2:4].T,
        dsg.T,
        dsu.T,
        dsd,
        jnp.swapaxes(deg, 1, 2),
        jnp.swapaxes(deu, 1, 2),
        ded,
    )


def solution(mesh):
    placed = (
        P(("dp", "tensor"), None),
        P(("dp", "tensor"), None),
        P("dp", None),
        P("dp"),
        P(),
        P(None, "tensor"),
        P(),
        P(),
        P(None, "tensor"),
        P("tensor", None),
        P(),
        P(),
        P(None, "tensor"),
        P(None, "tensor"),
        P("tensor", None),
        P(None, None, "tensor"),
        P(None, None, "tensor"),
        P(None, "tensor", None),
    )
    return jax.shard_map(
        body,
        mesh=mesh,
        in_specs=placed,
        out_specs=(
            P(("dp", "tensor"), None),
            P(("dp", "tensor"), None),
            P("tensor"),
            P(None, "tensor"),
            P("tensor", None),
            P("tensor"),
            P(None, "tensor"),
            P("tensor", None),
            P("tensor"),
            P("tensor", None),
            P(None, "tensor"),
            P(None, "tensor"),
            P("tensor", None),
            P(None, None, "tensor"),
            P(None, None, "tensor"),
            P(None, "tensor", None),
        ),
        check_vma=False,
    )
```

```python
import functools

import jax
import jax.numpy as jnp
import numpy as np
from jax import lax
from jax.experimental import pallas as pl
from jax.experimental.pallas import tpu as pltpu
from jax.sharding import PartitionSpec as P

DN = 128
DR = 64
DV = 128
KVR = 512
EPS = 1e-06
ROPE_BASE = 10000.0
LOG2E = 1.4426950408889634
SCALE = (DN + DR) ** (-0.5)
NEG = -1e30
MIB = 2**20
MESH = pl.DeviceIdType.MESH
f32 = jnp.float32
bf16 = jnp.bfloat16
VMEM = pltpu.VMEM
DMA = pltpu.SemaphoreType.DMA

OWN = 128
SHARDS = 8
LENGTH = OWN * SHARDS
WIDE = 2048
FS_OWN = 352
FE_OWN = 176
HID = 768
QCOLS = 384
LATENT_ROWS = 640


def vmem():
    return pl.BlockSpec(memory_space=pltpu.VMEM)


def anym():
    return pl.BlockSpec(memory_space=pl.ANY)


def dot(a, b):
    return jnp.dot(a, b, preferred_element_type=f32)


def dot_nt(a, b):
    return lax.dot_general(a, b, (((1,), (1,)), ((), ())), preferred_element_type=f32)


def dot_tn(a, b):
    return lax.dot_general(a, b, (((0,), (0,)), ((), ())), preferred_element_type=f32)


def neighbours():
    t = lax.axis_index("tensor")
    x = t // 4
    z = t % 4
    zp = lax.rem(z + 1, 4)
    zm = lax.rem(z + 3, 4)
    z2 = lax.rem(z + 2, 4)
    own = x * 4
    far = (1 - x) * 4
    return dict(
        me=t, tp=own + zp, tm=own + zm, t2=own + z2, tx=far + z, xp=far + zp, xm=far + zm, x2=far + z2
    )


def copies_of():
    d = lax.axis_index("dp")
    c = lax.rem(d, 2)
    y = lax.rem(d // 2, 4)
    plane = d // 8
    here = plane * 8 + c
    return dict(
        c=c, y=y, core=d + 1 - 2 * c, y2=here + lax.rem(y + 2, 4) * 2, yp=here + lax.rem(y + 1, 4) * 2, ym=here + lax.rem(y + 3, 4) * 2,
        xo=(1 - plane) * 8 + y * 2 + c,
    )


def entry_barrier(tensor=(), dp=()):
    sem = pltpu.get_barrier_semaphore()
    for peer in tensor:
        pl.semaphore_signal(sem, inc=1, device_id={"tensor": peer}, device_id_type=MESH)
    for peer in dp:
        pl.semaphore_signal(sem, inc=1, device_id={"dp": peer}, device_id_type=MESH)
    pl.semaphore_wait(sem, len(tensor) + len(dp))


def ring_peers(n):
    return (n["tp"], n["tm"], n["tx"])


class YSum:
    def __init__(self, d, rows, a_ref, got, ss, rs):
        self.d, self.rows, self.a, self.got, self.ss, self.rs = d, rows, a_ref, got, ss, rs
        self.pending = None
        self.all = []

    def piece(self, way, hops):
        owner = lax.rem(self.d["y"] + ((3 - hops) if way == 0 else (1 + hops)) + 4, 4)
        start = pl.multiple_of((owner * 2 + way) * self.rows, 16)
        return pl.ds(start, self.rows)

    def step(self, s):
        if s:
            for c in self.pending:
                c.wait_recv()
            for way in range(2):
                here = self.piece(way, s)
                self.got[s - 1, way] = added(self.got[s - 1, way], self.a[here, :])
        if s == 3:
            return
        self.pending = []
        for way in range(2):
            src = self.a.at[self.piece(way, 0)] if s == 0 else self.got.at[s - 1, way]
            c = pltpu.make_async_remote_copy(
                src_ref=src,
                dst_ref=self.got.at[s, way],
                send_sem=self.ss.at[s * 2 + way],
                recv_sem=self.rs.at[s * 2 + way],
                device_id={"dp": self.d["yp"] if way == 0 else self.d["ym"]},
                device_id_type=MESH,
            )
            c.start()
            self.pending.append(c)
            self.all.append(c)

    def close(self):
        for c in self.all:
            c.wait_send()


class YGather:
    def __init__(self, d, rows, g_ref, ss, rs):
        self.d, self.rows, self.g, self.ss, self.rs = d, rows, g_ref, ss, rs
        self.all = []

    def send(self, i, slot, start, count, way):
        view = self.g.at[slot, pl.ds(start, count)]
        c = pltpu.make_async_remote_copy(
            src_ref=view,
            dst_ref=view,
            send_sem=self.ss.at[i],
            recv_sem=self.rs.at[i],
            device_id={"dp": self.d["yp"] if way == 0 else self.d["ym"]},
            device_id_type=MESH,
        )
        c.start()
        self.all.append(c)

    def step(self, s):
        y = self.d["y"]
        if s == 0:
            self.send(0, y, 0, 2 * self.rows, 0)
            self.send(1, y, 0, 2 * self.rows, 1)
        elif s == 1:
            self.all[0].wait_recv()
            self.send(2, lax.rem(y + 3, 4), 0, self.rows, 0)
            self.all[1].wait_recv()
            self.send(3, lax.rem(y + 1, 4), self.rows, self.rows, 1)
        else:
            self.all[2].wait_recv()
            self.all[3].wait_recv()

    def close(self):
        for c in self.all:
            c.wait_send()


def dp_copy(src, dst, ss, rs, peer):
    return pltpu.make_async_remote_copy(
        src_ref=src, dst_ref=dst, send_sem=ss, recv_sem=rs, device_id={"dp": peer}, device_id_type=MESH
    )


def sender(ss, rs):
    def send(i, src, dst, dev):
        return pltpu.make_async_remote_copy(
            src_ref=src,
            dst_ref=dst,
            send_sem=ss.at[i],
            recv_sem=rs.at[i],
            device_id={"tensor": dev},
            device_id_type=MESH,
        )

    return send


def gather_steps(n, x_ref, o_ref, ss, rs):
    send = sender(ss, rs)

    def s(i, src, slot, o, k, dev):
        return send(i, src, o_ref.at[slot, pl.ds(o, k)], dev)

    def part(slot, o, k):
        return o_ref.at[slot, pl.ds(o, k)]

    me, tp, tm, tx, t2, xp, xm, x2 = (n[k] for k in ("me", "tp", "tm", "tx", "t2", "xp", "xm", "x2"))
    s1a = s(0, x_ref.at[pl.ds(0, 64)], me, 0, 64, tp)
    s2a = s(1, x_ref.at[pl.ds(64, 64)], me, 64, 64, tm)
    s3 = s(2, x_ref, me, 0, 128, tx)
    s1b = s(11, x_ref.at[pl.ds(64, 64)], me, 64, 64, tp)
    s2b = s(12, x_ref.at[pl.ds(0, 64)], me, 0, 64, tm)
    for c in (s1a, s2a, s3, s1b, s2b):
        c.start()
    yield me
    s1a.wait_recv()
    s4 = s(3, part(tm, 0, 64), tm, 0, 64, tp)
    s6a = s(5, part(tm, 0, 64), tm, 0, 64, tx)
    s4.start()
    s6a.start()
    s2a.wait_recv()
    s5 = s(4, part(tp, 64, 64), tp, 64, 64, tm)
    s7a = s(6, part(tp, 64, 64), tp, 64, 64, tx)
    s5.start()
    s7a.start()
    s3.wait_recv()
    s8 = s(7, part(tx, 80, 48), tx, 80, 48, tp)
    s9 = s(8, part(tx, 0, 48), tx, 0, 48, tm)
    s8.start()
    s9.start()
    s1b.wait_recv()
    s6b = s(13, part(tm, 64, 16), tm, 64, 16, tx)
    s6b.start()
    s2b.wait_recv()
    s7b = s(14, part(tp, 48, 16), tp, 48, 16, tx)
    s7b.start()
    yield tm
    s6a.wait_recv()
    s10 = s(9, part(xm, 0, 64), xm, 0, 64, tp)
    s10.start()
    s7a.wait_recv()
    s11 = s(10, part(xp, 64, 64), xp, 64, 64, tm)
    s11.start()
    yield tp
    yield tx
    s4.wait_recv()
    s5.wait_recv()
    yield t2
    s8.wait_recv()
    s6b.wait_recv()
    yield xm
    s9.wait_recv()
    s7b.wait_recv()
    yield xp
    s10.wait_recv()
    s11.wait_recv()
    yield x2
    for c in (s1a, s1b, s2a, s2b, s3, s4, s5, s6a, s6b, s7a, s7b, s8, s9, s10, s11):
        c.wait_send()


def gather_ring(n, x_ref, o_ref, ss, rs, on_shard=None):
    for slot in gather_steps(n, x_ref, o_ref, ss, rs):
        if on_shard:
            on_shard(slot)


def reduce_steps(n, pv, ready, bufs, ss, rs):
    send = sender(ss, rs)
    me, tp, tm, tx, t2, xp, xm, x2 = (n[k] for k in ("me", "tp", "tm", "tx", "t2", "xp", "xm", "x2"))
    r10, r11, r8, r9, r6, r7, r4, r5, m1, m2, m3 = bufs

    def s(i, slot, o, k, dst, dev):
        return send(i, pv.at[slot, pl.ds(o, k)], dst, dev)

    def add(slot, o, k, buf):
        pv[slot, pl.ds(o, k)] = added(pv[slot, pl.ds(o, k)], buf[...])

    ready("x2")
    s10 = s(0, x2, 0, 64, r10, tm)
    s11 = s(1, x2, 64, 64, r11, tp)
    s10.start()
    s11.start()
    ready("tx")
    s3b = s(10, tx, 48, 32, m3.at[pl.ds(48, 32)], tx)
    s3b.start()
    ready("xm")
    ready("xp")
    s6b = s(15, xm, 64, 16, r6.at[pl.ds(64, 16)], tx)
    s7b = s(16, xp, 48, 16, r7.at[pl.ds(0, 16)], tx)
    s6b.start()
    s7b.start()
    ready("t2")
    s4 = s(2, t2, 0, 64, r4, tm)
    s5 = s(3, t2, 64, 64, r5, tp)
    s4.start()
    s5.start()
    s8 = s(4, xm, 80, 48, r8, tm)
    s9 = s(5, xp, 0, 48, r9, tp)
    s8.start()
    s9.start()
    ready("tm")
    ready("tp")
    s1b = s(11, tm, 80, 48, m1.at[pl.ds(80, 48)], tm)
    s2b = s(12, tp, 0, 48, m2.at[pl.ds(0, 48)], tp)
    s1b.start()
    s2b.start()
    yield
    s10.wait_recv()
    add(xm, 0, 64, r10)
    s6 = s(6, xm, 0, 64, r6.at[pl.ds(0, 64)], tx)
    s6.start()
    s11.wait_recv()
    add(xp, 64, 64, r11)
    s7 = s(7, xp, 64, 64, r7.at[pl.ds(16, 64)], tx)
    s7.start()
    yield
    s8.wait_recv()
    add(tx, 80, 48, r8)
    s9.wait_recv()
    add(tx, 0, 48, r9)
    s3a = s(13, tx, 80, 48, m3.at[pl.ds(80, 48)], tx)
    s3c = s(14, tx, 0, 48, m3.at[pl.ds(0, 48)], tx)
    s3a.start()
    s3c.start()
    yield
    s4.wait_recv()
    add(tm, 0, 64, r4)
    s6.wait_recv()
    s6b.wait_recv()
    add(tm, 0, 80, r6)
    s1 = s(8, tm, 0, 80, m1.at[pl.ds(0, 80)], tm)
    s1.start()
    yield
    s5.wait_recv()
    add(tp, 64, 64, r5)
    s7.wait_recv()
    s7b.wait_recv()
    add(tp, 48, 80, r7)
    s2 = s(9, tp, 48, 80, m2.at[pl.ds(48, 80)], tp)
    s2.start()
    yield
    ready("me")
    for c in (s3a, s3b, s3c, s1b, s2b, s1, s2):
        c.wait_recv()
    for c in (s1, s1b, s2, s2b, s3a, s3b, s3c, s4, s5, s6, s6b, s7, s7b, s8, s9, s10, s11):
        c.wait_send()


def reduce_ring(n, pv, ready, bufs, ss, rs, work=None):
    for point, _ in enumerate(reduce_steps(n, pv, ready, bufs, ss, rs)):
        if work:
            work(point)


def reduce_scratch(columns):
    rows = (64, 64, 48, 48, 80, 80, 64, 64, 128, 128, 128)
    return [VMEM((r, columns), bf16) for r in rows]


def added(a, b):
    return (a.astype(f32) + b.astype(f32)).astype(bf16)


def load_partials(n, p_ref, pv, ls):
    order = ("x2", "tx", "xm", "xp", "t2", "tm", "tp", "me")
    copies = {}
    for i, name in enumerate(order):
        copies[name] = pltpu.make_async_copy(p_ref.at[n[name]], pv.at[n[name]], ls.at[i])
        copies[name].start()
    return lambda name: copies[name].wait()


def inverse_rms(v):
    return lax.rsqrt(jnp.mean(v * v, axis=-1, keepdims=True) + EPS)


class Copies:
    def __init__(self, sems):
        self.sems, self.made = sems, []

    def start(self, src, dst):
        copy = pltpu.make_async_copy(src, dst, self.sems.at[len(self.made)])
        copy.start()
        self.made.append(copy)
        return copy

    def close(self):
        for copy in self.made:
            copy.wait()


def turn(v, cos, sin):
    lane = lax.broadcasted_iota(jnp.int32, v.shape, 1)
    low = lax.rem(lane, 64) < 32
    swapped = jnp.where(low, pltpu.roll(v, 96, 1), pltpu.roll(v, 32, 1))
    return v * cos + swapped * sin


def fetch_latent_weights(kvd_hbm, kvd_ref, sems):
    copies = [
        pltpu.make_async_copy(kvd_hbm, kvd_ref.at[pl.ds(0, KVR + DR)], sems.at[0]),
        pltpu.make_async_copy(kvd_hbm.at[pl.ds(KVR, DR)], kvd_ref.at[pl.ds(KVR + DR, DR)], sems.at[1]),
    ]
    for c in copies:
        c.start()
    return copies


def project_kernel(
    x_ref, grad_ref, gain_ref, wq_hbm, kvd_hbm, lgain_ref, kvup_ref, cos_ref, sin_ref,
    normed_out, q_ref, kvw_ref, kr_ref, lnorm_out, latent_out, gall_ref,
    xall, wq_ref, kvd_ref, normed_ref, lnorm_ref, latent_ref, ss, rs, gs, gr, ls, os,
):
    n = neighbours()
    wcopy = pltpu.make_async_copy(wq_hbm, wq_ref, ls.at[2])
    wcopy.start()
    copies = fetch_latent_weights(kvd_hbm, kvd_ref, ls)
    entry_barrier(ring_peers(n))

    def compute(slot, src):
        x = src.astype(f32)
        normed = (x * inverse_rms(x) * gain_ref[...].astype(f32)).astype(bf16)
        normed_ref[slot] = normed
        raw = dot(normed, wq_ref[...])
        rows = pl.ds(pl.multiple_of(slot * OWN, OWN), OWN)
        cos = cos_ref[rows, :]
        sin = sin_ref[rows, :]
        q_ref[slot, :, :128] = raw[:, :128].astype(bf16)
        q_ref[slot, :, 128:256] = raw[:, 192:320].astype(bf16)
        rope = jnp.concatenate([raw[:, 128:192], raw[:, 320:384]], axis=1)
        q_ref[slot, :, 256:] = turn(rope, cos, sin).astype(bf16)
        raw = dot_nt(normed, kvd_ref[...])
        latent = raw[:, :KVR]
        latent_ref[slot] = latent
        lnorm = (latent * inverse_rms(latent) * lgain_ref[...].astype(f32)).astype(bf16)
        lnorm_ref[slot] = lnorm
        kr_ref[slot] = turn(raw[:, KVR:], cos, sin).astype(bf16)
        kvw_ref[slot] = dot(lnorm, kvup_ref[...]).astype(bf16)
        for src, dst in ((normed_ref, normed_out), (lnorm_ref, lnorm_out), (latent_ref, latent_out)):
            stores.start(src.at[slot], dst.at[slot])

    stores = Copies(os)
    second = gather_steps(n, grad_ref, gall_ref, gs, gr)
    local = pltpu.make_async_copy(grad_ref, gall_ref.at[n["me"]], ls.at[3])
    for k, slot in enumerate(gather_steps(n, x_ref, xall, ss, rs)):
        if k == 0:
            local.start()
            for c in copies + [wcopy]:
                c.wait()
            compute(slot, x_ref[...])
            continue
        if k == 1:
            next(second)
        if k == 4:
            next(second)
        if k == 7:
            next(second)
        compute(slot, xall[slot])
    for slot in second:
        pass
    local.wait()
    stores.close()


def project(x, grad, gain, wq, kvd, lgain, kvup, cos, sin):
    def out(c, t):
        return jax.ShapeDtypeStruct((SHARDS, OWN, c), t)

    outs = (out(WIDE, bf16), out(QCOLS, bf16), out(512, bf16), out(128, bf16), out(KVR, bf16), out(KVR, f32))
    outs += (out(WIDE, bf16),)
    return pl.pallas_call(
        project_kernel,
        out_shape=outs,
        in_specs=[vmem(), anym(), vmem(), anym(), anym(), vmem(), vmem(), vmem(), vmem()],
        out_specs=[anym()] + [vmem()] * 3 + [anym()] * 3,
        scratch_shapes=[
            VMEM((SHARDS, OWN, WIDE), bf16),
            VMEM((WIDE, QCOLS), bf16),
            VMEM((LATENT_ROWS, WIDE), bf16),
            VMEM((SHARDS, OWN, WIDE), bf16),
            VMEM((SHARDS, OWN, KVR), bf16),
            VMEM((SHARDS, OWN, KVR), f32),
            DMA((17,)),
            DMA((17,)),
            DMA((17,)),
            DMA((17,)),
            DMA((4,)),
            DMA((24,)),
        ],
        compiler_params=pltpu.CompilerParams(
            collective_id=0, has_side_effects=True, vmem_limit_bytes=48 * MIB
        ),
        cost_estimate=pl.CostEstimate(flops=5 * 10**9, bytes_accessed=2 * 10**7, transcendentals=0),
        name="project",
    )(x, grad, gain, wq, kvd, lgain, kvup, cos, sin)


KB = 256


def masked(s, key0, query0, prefix):
    keys = key0 + lax.broadcasted_iota(jnp.int32, s.shape, 0)
    rows = query0 + lax.broadcasted_iota(jnp.int32, s.shape, 1)
    return jnp.where((keys <= rows) | (keys < prefix), s, NEG)


def key_extent(query_block):
    return max(2, query_block + 1)


def head_lanes(shape, head):
    lane = lax.broadcasted_iota(jnp.int32, shape, 1)
    return (lane >= 64) if head else (lane < 64)


def head_query(q_ref, rows, head):
    rope = q_ref[rows, 256:QCOLS]
    rope = jnp.where(head_lanes(rope.shape, head), rope.astype(f32), 0.0).astype(bf16)
    return jnp.concatenate([q_ref[rows, head * 128 : head * 128 + 128], rope], axis=1)


def head_key(kvw_ref, kr_ref, rows, head):
    return jnp.concatenate([kvw_ref[rows, head * 256 : head * 256 + 128], kr_ref[rows, :]], axis=1)


def attend_kernel(prefix_ref, q_ref, kvw_ref, kr_ref, wo_ref, attn_ref, lse_ref, ot_ref, p_out, s_scr, p_ref, os):
    prefix = prefix_ref[0]
    stores = Copies(os)
    for i in range(4):
        rows = pl.ds(i * KB, KB)
        for h in range(2):
            q = head_query(q_ref, rows, h)
            top = jnp.full((1, KB), NEG, f32)
            for k in range(key_extent(i)):
                keys = pl.ds(k * KB, KB)
                s = dot_nt(head_key(kvw_ref, kr_ref, keys, h), q)
                if k >= i:
                    s = masked(s, k * KB, i * KB, prefix)
                s_scr[keys, :] = s
                top = jnp.maximum(top, jnp.max(s, axis=0, keepdims=True))
            top = top * (SCALE * LOG2E)
            total = jnp.zeros((1, KB), f32)
            out = jnp.zeros((DV, KB), f32)
            for k in range(key_extent(i)):
                keys = pl.ds(k * KB, KB)
                p = jnp.exp2(s_scr[keys, :] * (SCALE * LOG2E) - top)
                total = total + jnp.sum(p, axis=0, keepdims=True)
                out = out + dot_tn(kvw_ref[keys, h * 256 + 128 : h * 256 + 256], p.astype(bf16))
            out = out / total
            lse_ref[h : h + 1, rows] = top + jnp.log2(total)
            ot_ref[h, :, rows] = out
            attn_ref[rows, h * 128 : h * 128 + 128] = out.T.astype(bf16)
        p_ref[rows, :] = dot(attn_ref[rows, :], wo_ref[...]).astype(bf16)
        stores.start(p_ref.at[rows], p_out.at[rows])
    stores.close()


def attend(prefix, q, kvw, kr, wo):
    return pl.pallas_call(
        attend_kernel,
        out_shape=(
            jax.ShapeDtypeStruct((LENGTH, 256), bf16),
            jax.ShapeDtypeStruct((2, LENGTH), f32),
            jax.ShapeDtypeStruct((2, DV, LENGTH), f32),
            jax.ShapeDtypeStruct((LENGTH, WIDE), bf16),
        ),
        in_specs=[pl.BlockSpec(memory_space=pltpu.SMEM)] + [vmem()] * 4,
        out_specs=[vmem()] * 3 + [anym()],
        scratch_shapes=[VMEM((LENGTH, KB), f32), VMEM((LENGTH, WIDE), bf16), DMA((4,))],
        compiler_params=pltpu.CompilerParams(vmem_limit_bytes=48 * MIB),
        cost_estimate=pl.CostEstimate(flops=25 * 10**8, bytes_accessed=10**7, transcendentals=2 * 10**6),
        name="attend",
    )(prefix, q, kvw, kr, wo)


def own_total(n, pv, bufs):
    m1, m2, m3 = bufs[8:]
    return pv[n["me"]].astype(f32) + m1[...].astype(f32) + m2[...].astype(f32) + m3[...].astype(f32)


def fetch_hidden_weights(sg, rt, eg, dst, zero_ref, sems, base):
    pieces = [(sg, 0, FS_OWN), (eg.at[0], 384, FE_OWN), (eg.at[1], 384 + FE_OWN, FE_OWN)]
    pieces += [(zero_ref, 736, 32), (rt if rt is not None else zero_ref, FS_OWN, 32)]
    copies = []
    for i, (src, at, count) in enumerate(pieces):
        c = pltpu.make_async_copy(src, dst.at[pl.ds(at, count)], sems.at[base + i])
        c.start()
        copies.append(c)
    return copies


def ffn_rows(mixed, dm, route, wg_ref, wu_ref):
    a = dot_nt(mixed, wg_ref[...])
    b = dot_nt(mixed, wu_ref[...])
    first = (route == 0).astype(f32)
    second = (route == 1).astype(f32)
    l0 = a[:, FS_OWN : FS_OWN + 1]
    l1 = a[:, FS_OWN + 1 : FS_OWN + 2]
    top = jnp.maximum(l0, l1)
    e0 = jnp.exp(l0 - top)
    e1 = jnp.exp(l1 - top)
    r0 = e0 / (e0 + e1)
    r1 = e1 / (e0 + e1)
    col = lax.broadcasted_iota(jnp.int32, (1, HID), 1)
    is_shared = col < 384
    in0 = (col >= 384) & (col < 384 + FE_OWN)
    in1 = (col >= 384 + FE_OWN) & (col < 384 + 2 * FE_OWN)
    gate = jnp.where(is_shared, 1.0, 0.0) + jnp.where(in0, first * r0, 0.0) + jnp.where(in1, second * r1, 0.0)
    sig = jax.nn.sigmoid(a)
    silu = a * sig
    act = silu * b
    m = (gate * act).astype(bf16)
    scaled = dm * gate
    down = dm * act
    g0 = first * jnp.sum(jnp.where(in0, down, 0.0), axis=1, keepdims=True)
    g1 = second * jnp.sum(jnp.where(in1, down, 0.0), axis=1, keepdims=True)
    mean = r0 * g0 + r1 * g1
    da = scaled * b * (sig * (1.0 + a * (1.0 - sig)))
    da = da + jnp.where(col == FS_OWN, r0 * (g0 - mean), 0.0) + jnp.where(col == FS_OWN + 1, r1 * (g1 - mean), 0.0)
    da = da.astype(bf16)
    db = (scaled * silu).astype(bf16)
    return m, da, db, dot(da, wg_ref[...]) + dot(db, wu_ref[...])


def hidden_ffn_kernel(
    p_ref, x_ref, gain_ref, grad_hbm, routes_ref, sg, su, sd, eg, eu, ed, rt_ref,
    hidden_ref, mixed_out, m_out, da_out, db_out, p2_out, gsum_ref,
    mixed_ref, m_ref, da_ref, db_ref, p2_ref, os, pv, own, gall, dm_scr, wg_ref, wu_ref, wd_ref, zero_ref, *rest,
):
    bufs, (ss, rs, gs, gr, ls, ws) = rest[:11], rest[11:]
    n = neighbours()
    ready = load_partials(n, p_ref, pv, ls)
    zero_ref[...] = jnp.zeros_like(zero_ref)
    copies = fetch_hidden_weights(sg, rt_ref, eg, wg_ref, zero_ref, ws, 0)
    copies += fetch_hidden_weights(su, None, eu, wu_ref, zero_ref, ws, 5)
    copies += fetch_hidden_weights(sd, None, ed, wd_ref, zero_ref, ws, 10)
    gcopy = pltpu.make_async_copy(grad_hbm, gall, ws.at[15])
    gcopy.start()
    entry_barrier(ring_peers(n))

    def work(point):
        if point == 0:
            for c in copies + [gcopy]:
                c.wait()
        if point < 4:
            two = pl.ds(point * 2, 2)
            dm_scr[two] = dot_nt(gall[two].reshape(256, WIDE), wd_ref[...]).reshape(2, OWN, HID)

    reduce_ring(n, pv, ready, bufs, ss, rs, work)
    hidden = x_ref[...].astype(f32) + own_total(n, pv, bufs)
    hidden_ref[...] = hidden
    own[...] = (hidden * inverse_rms(hidden) * gain_ref[...].astype(f32)).astype(bf16)
    mixed_ref[n["me"]] = own[...]
    gsum_ref[...] = jnp.zeros_like(gsum_ref)
    waiting = []

    def on_shard(slot):
        waiting.append(slot)
        if len(waiting) < 2:
            return
        pair = list(waiting)
        waiting.clear()
        mixed = jnp.concatenate([mixed_ref[s] for s in pair], axis=0)
        dm = jnp.concatenate([dm_scr[s] for s in pair], axis=0)
        route = jnp.concatenate([routes_ref[s] for s in pair], axis=0)
        m, da, db, back = ffn_rows(mixed, dm, route, wg_ref, wu_ref)
        gsum_ref[...] += jnp.sum(back * mixed.astype(f32), axis=0, keepdims=True)
        back = back.astype(bf16)
        for i, s in enumerate(pair):
            part = slice(i * OWN, i * OWN + OWN)
            m_ref[s] = m[part]
            da_ref[s] = da[part]
            db_ref[s] = db[part]
            p2_ref[s] = back[part]
            for src, dst in (
                (mixed_ref, mixed_out), (m_ref, m_out), (da_ref, da_out), (db_ref, db_out), (p2_ref, p2_out)
            ):
                stores.start(src.at[s], dst.at[s])

    stores = Copies(os)
    gather_ring(n, own, mixed_ref, gs, gr, on_shard)
    stores.close()


def hidden_ffn(p, x, gain, grad, routes, sg, su, sd, eg, eu, ed, rt):
    def out(c, t=bf16):
        return jax.ShapeDtypeStruct((SHARDS, OWN, c), t)

    row = jax.ShapeDtypeStruct((1, WIDE), f32)
    outs = (jax.ShapeDtypeStruct((OWN, WIDE), f32), out(WIDE), out(HID), out(HID), out(HID), out(WIDE), row)
    return pl.pallas_call(
        hidden_ffn_kernel,
        out_shape=outs,
        in_specs=[anym(), vmem(), vmem(), anym(), vmem()] + [anym()] * 7,
        out_specs=[vmem()] + [anym()] * 5 + [vmem()],
        scratch_shapes=[
            VMEM((SHARDS, OWN, WIDE), bf16),
            VMEM((SHARDS, OWN, HID), bf16),
            VMEM((SHARDS, OWN, HID), bf16),
            VMEM((SHARDS, OWN, HID), bf16),
            VMEM((SHARDS, OWN, WIDE), bf16),
            DMA((40,)),
            VMEM((SHARDS, OWN, WIDE), bf16),
            VMEM((OWN, WIDE), bf16),
            VMEM((SHARDS, OWN, WIDE), bf16),
            VMEM((SHARDS, OWN, HID), f32),
            VMEM((HID, WIDE), bf16),
            VMEM((HID, WIDE), bf16),
            VMEM((HID, WIDE), bf16),
            VMEM((32, WIDE), bf16),
        ]
        + reduce_scratch(WIDE)
        + [DMA((17,)), DMA((17,)), DMA((17,)), DMA((17,)), DMA((8,)), DMA((16,))],
        compiler_params=pltpu.CompilerParams(
            collective_id=1, has_side_effects=True, vmem_limit_bytes=60 * MIB
        ),
        cost_estimate=pl.CostEstimate(flops=16 * 10**9, bytes_accessed=3 * 10**7, transcendentals=10**6),
        name="hidden_ffn",
    )(p.reshape(SHARDS, OWN, WIDE), x, gain, grad, routes, sg, su, sd, eg, eu, ed, rt)


def rows_of(ref):
    return ref[...].reshape(LENGTH, ref.shape[-1])


BLOCKS = 9


def turn_kernel(
    p_ref, hidden_ref, grad_ref, gain_ref, mixed_hbm, gall_hbm, m_hbm, da_hbm, db_hbm, sd, ed,
    hgrad_ref, low_ref, half_out, router_ref, moe_hbm,
    mixed_ref, gall_ref, m_ref, da_ref, db_ref, half_ref, hs, hos, pv, dw_scr, core_scr, moe_scr, wd_ref, zero_ref, *rest,
):
    bufs, (ss, rs, cs, cr, ls, ws, os) = rest[:11], rest[11:]
    n = neighbours()
    d = copies_of()
    ready = load_partials(n, p_ref, pv, ls)
    zero_ref[...] = jnp.zeros_like(zero_ref)
    loads = Copies(hs)
    for src, dst in ((m_hbm, m_ref), (gall_hbm, gall_ref), (da_hbm, da_ref), (mixed_hbm, mixed_ref), (db_hbm, db_ref)):
        loads.start(src, dst)
    copies = fetch_hidden_weights(sd, None, ed, wd_ref, zero_ref, ws, 0)
    halves = Copies(hos)
    entry_barrier(ring_peers(n), (d["core"],))
    stores = []
    crossed = []
    sent = []
    theirs = pl.multiple_of((1 - d["c"]) * OWN, OWN)
    mine = pl.multiple_of(d["c"] * OWN, OWN)

    def product(index, left, right, block):
        k = index * 3 + block
        if block == 0:
            for c in {2: loads.made[:2], 0: loads.made[2:4], 1: loads.made[4:]}[index]:
                c.wait()
        left = left[:, :, pl.ds(block * 256, 256)].reshape(LENGTH, 256)
        dw_scr[k] = dot_tn(left, rows_of(right)).astype(bf16)
        c = dp_copy(dw_scr.at[k, pl.ds(theirs, OWN)], core_scr.at[k], cs.at[k], cr.at[k], d["core"])
        c.start()
        crossed.append((k, c))
        if len(crossed) > 2:
            meet()
        if k == 1:
            router_ref[...] = dw_scr[1, FS_OWN - 256 : FS_OWN - 240, :]

    def expert_sum(block):
        two = pl.ds(block * 2, 2)
        moe_scr[two] = dot(m_ref[two].reshape(256, HID), wd_ref[...]).astype(bf16).reshape(2, OWN, WIDE)
        c = pltpu.make_async_copy(moe_scr.at[two], moe_hbm.at[two], os.at[block])
        c.start()
        stores.append(c)

    def meet():
        k, c = crossed.pop(0)
        c.wait_recv()
        half_ref[k] = added(dw_scr[k, pl.ds(mine, OWN), :], core_scr[k])
        halves.start(half_ref.at[k], half_out.at[k])
        sent.append(c)

    jobs = [functools.partial(product, 2, m_ref, gall_ref, b) for b in range(3)]
    jobs += [functools.partial(product, 0, da_ref, mixed_ref, b) for b in range(3)]
    jobs += [functools.partial(product, 1, db_ref, mixed_ref, b) for b in range(3)]
    jobs += [functools.partial(expert_sum, b) for b in range(4)]
    plan = {0: 3, 1: 2, 2: 2, 3: 2, 4: 4}

    def work(point):
        if point == 4:
            for c in copies:
                c.wait()
        for _ in range(plan[point]):
            jobs.pop(0)()
        if point == 4:
            while crossed:
                meet()

    reduce_ring(n, pv, ready, bufs, ss, rs, work)
    total = own_total(n, pv, bufs)
    hidden = hidden_ref[...]
    inv = inverse_rms(hidden)
    unit = hidden * inv
    scaled = total * gain_ref[...].astype(f32)
    back = inv * (scaled - unit * jnp.mean(scaled * unit, axis=-1, keepdims=True))
    hgrad = grad_ref[...].astype(f32) + back
    hgrad_ref[...] = hgrad
    low_ref[...] = hgrad.astype(bf16)
    for c in stores:
        c.wait()
    for c in sent:
        c.wait_send()
    halves.close()


def turn_back(p, hidden, grad, gain, mixed, gall, m, da, db, sd, ed):
    outs = (
        jax.ShapeDtypeStruct((OWN, WIDE), f32),
        jax.ShapeDtypeStruct((OWN, WIDE), bf16),
        jax.ShapeDtypeStruct((BLOCKS, OWN, WIDE), bf16),
        jax.ShapeDtypeStruct((16, WIDE), bf16),
        jax.ShapeDtypeStruct((SHARDS, OWN, WIDE), bf16),
    )
    return pl.pallas_call(
        turn_kernel,
        out_shape=outs,
        in_specs=[anym()] + [vmem()] * 3 + [anym()] * 7,
        out_specs=[vmem(), vmem(), anym(), vmem(), anym()],
        scratch_shapes=[
            VMEM((SHARDS, OWN, WIDE), bf16),
            VMEM((SHARDS, OWN, WIDE), bf16),
            VMEM((SHARDS, OWN, HID), bf16),
            VMEM((SHARDS, OWN, HID), bf16),
            VMEM((SHARDS, OWN, HID), bf16),
            VMEM((BLOCKS, OWN, WIDE), bf16),
            DMA((5,)),
            DMA((BLOCKS,)),
            VMEM((SHARDS, OWN, WIDE), bf16),
            VMEM((BLOCKS, 256, WIDE), bf16),
            VMEM((BLOCKS, OWN, WIDE), bf16),
            VMEM((SHARDS, OWN, WIDE), bf16),
            VMEM((HID, WIDE), bf16),
            VMEM((32, WIDE), bf16),
        ]
        + reduce_scratch(WIDE)
        + [DMA((17,)), DMA((17,)), DMA((BLOCKS,)), DMA((BLOCKS,)), DMA((8,)), DMA((5,)), DMA((4,))],
        compiler_params=pltpu.CompilerParams(
            collective_id=2, has_side_effects=True, vmem_limit_bytes=60 * MIB
        ),
        cost_estimate=pl.CostEstimate(flops=13 * 10**9, bytes_accessed=4 * 10**7, transcendentals=0),
        name="turn_back",
    )(p, hidden, grad, gain, mixed, gall, m, da, db, sd, ed)


QUARTER = 288


def gather_kernel(x_ref, half_hbm, o_ref, sum_ref, half_ref, got, ss, rs, ys, yr, ls):
    n = neighbours()
    d = copies_of()
    load = pltpu.make_async_copy(half_hbm, half_ref, ls.at[1])
    load.start()
    entry_barrier(ring_peers(n), (d["yp"], d["ym"]))
    local = pltpu.make_async_copy(x_ref, o_ref.at[n["me"]], ls.at[0])
    local.start()
    ysum = YSum(d, QUARTER // 2, half_ref, got, ys, yr)
    seen = []

    def on_shard(slot):
        seen.append(slot)
        step = {1: 0, 2: 1, 4: 2}.get(len(seen))
        if step == 0:
            load.wait()
        if step is not None:
            ysum.step(step)

    gather_ring(n, x_ref, o_ref, ss, rs, on_shard)
    ysum.step(3)
    sum_ref[pl.ds(0, QUARTER // 2), :] = got[2, 0]
    sum_ref[pl.ds(QUARTER // 2, QUARTER // 2), :] = got[2, 1]
    ysum.close()
    local.wait()


def gather(x, half):
    return pl.pallas_call(
        gather_kernel,
        out_shape=(
            jax.ShapeDtypeStruct((SHARDS, OWN, WIDE), bf16),
            jax.ShapeDtypeStruct((QUARTER, WIDE), bf16),
        ),
        in_specs=[anym(), anym()],
        out_specs=(anym(), vmem()),
        scratch_shapes=[
            VMEM((BLOCKS * OWN, WIDE), bf16),
            VMEM((3, 2, QUARTER // 2, WIDE), bf16),
            DMA((17,)),
            DMA((17,)),
            DMA((6,)),
            DMA((6,)),
            DMA((2,)),
        ],
        compiler_params=pltpu.CompilerParams(
            collective_id=3, has_side_effects=True, vmem_limit_bytes=32 * MIB
        ),
        name="gather_grad",
    )(x, half)


LATE = 3072
PACK_COLS = 1280
EXT = WIDE + PACK_COLS


def attend_back_kernel(
    prefix_ref, hall_hbm, wo_ref, q_ref, kvw_ref, kr_ref, lse_ref, ot_ref,
    kvup_ref, latent_hbm, lgain_ref, cos_ref, sin_ref, wq_hbm, kvd_hbm,
    normed_hbm, lnorm_hbm, attn_ref, gain_ref, fgain_ref, gsum_ref, router_ref, ysum_ref,
    p_out, late_out, all_ref,
    hall_ref, latent_ref, wq_ref, normed_ref, lnorm_ref, p_ref, late_ref, hs, os, do_scr, dk_scr, dv_scr, jq_scr, jk_scr, kvg_scr, kvd_ref, far_scr, quarter, ls, xs, xr, ys, yr,
):
    prefix = prefix_ref[0]
    d = copies_of()
    loads = Copies(hs)
    for i in range(4):
        loads.start(hall_hbm.at[pl.ds(i * KB, KB)], hall_ref.at[pl.ds(i * KB, KB)])
    for src, dst in ((latent_hbm, latent_ref), (wq_hbm, wq_ref), (normed_hbm, normed_ref), (lnorm_hbm, lnorm_ref)):
        loads.start(src, dst)
    stores = Copies(os)
    entry_barrier((), (d["xo"], d["yp"], d["ym"]))
    half = QUARTER // 2
    parts = [pl.ds(0, half), pl.ds(half, half)]
    crosses = [dp_copy(ysum_ref.at[r], far_scr.at[r], xs.at[k], xr.at[k], d["xo"]) for k, r in enumerate(parts)]
    for cross in crosses:
        cross.start()
    spread = []

    def meet(k):
        crosses[k].wait_recv()
        quarter[parts[k], :] = added(ysum_ref[parts[k], :], far_scr[parts[k], :])
        for way, peer in enumerate((d["yp"], d["ym"])):
            i = k * 2 + way
            copy = dp_copy(quarter.at[parts[k]], all_ref.at[d["y"], parts[k]], ys.at[i], yr.at[i], peer)
            copy.start()
            spread.append(copy)
        stores.start(quarter.at[parts[k]], all_ref.at[d["y"], parts[k]])

    copies = fetch_latent_weights(kvd_hbm, kvd_ref, ls)
    for i in range(4):
        rows = pl.ds(i * KB, KB)
        loads.made[i].wait()
        do_scr[rows, :] = dot_nt(hall_ref[rows, :], wo_ref[...]).astype(bf16)
    dk_scr[...] = jnp.zeros_like(dk_scr)
    dv_scr[...] = jnp.zeros_like(dv_scr)
    for i in range(4):
        rows = pl.ds(i * KB, KB)
        plain = []
        turned = jnp.zeros((KB, 128), f32)
        for h in range(2):
            q = head_query(q_ref, rows, h)
            do = do_scr[rows, h * 128 : h * 128 + 128]
            lse = lse_ref[h : h + 1, rows]
            delta = jnp.sum(do.astype(f32).T * ot_ref[h, :, rows], axis=0, keepdims=True)
            dq = jnp.zeros((KB, 256), f32)
            for k in range(key_extent(i)):
                keys = pl.ds(k * KB, KB)
                key = head_key(kvw_ref, kr_ref, keys, h)
                s = dot_nt(key, q)
                if k >= i:
                    s = masked(s, k * KB, i * KB, prefix)
                p = jnp.exp2(s * (SCALE * LOG2E) - lse)
                dp = dot_nt(kvw_ref[keys, h * 256 + 128 : h * 256 + 256], do)
                ds = (p * (dp - delta)).astype(bf16)
                dv_scr[h, keys, :] += dot(p.astype(bf16), do)
                dk_scr[h, keys, :] += dot(ds, q)
                dq = dq + dot_tn(ds, key)
            dq = dq * SCALE
            plain.append(dq[:, :128])
            turned = turned + jnp.where(head_lanes(turned.shape, h), dq[:, 128:], 0.0)
        turned = turn(turned, cos_ref[rows, :], -sin_ref[rows, :])
        j = jnp.concatenate([plain[0], turned[:, :64], plain[1], turned[:, 64:]], axis=1)
        jq_scr[rows, :] = j.astype(bf16)
    meet(0)
    for c in copies + loads.made[4:]:
        c.wait()
    gain_sum = jnp.zeros((1, WIDE), f32)
    lgain_sum = jnp.zeros((1, KVR), f32)
    for i in range(4):
        rows = pl.ds(i * KB, KB)
        for h in range(2):
            kvg_scr[rows, h * 256 : h * 256 + 128] = (dk_scr[h, rows, :128] * SCALE).astype(bf16)
            kvg_scr[rows, h * 256 + 128 : h * 256 + 256] = dv_scr[h, rows, :].astype(bf16)
        dkr = (dk_scr[0, rows, 128:] + dk_scr[1, rows, 128:]) * SCALE
        jk_scr[rows, KVR:] = turn(dkr, cos_ref[rows, :], -sin_ref[rows, :]).astype(bf16)
        dl = dot_nt(kvg_scr[rows, :], kvup_ref[...])
        latent = latent_ref[rows, :]
        inv = inverse_rms(latent)
        unit = latent * inv
        lgain_sum = lgain_sum + jnp.sum(dl * unit, axis=0, keepdims=True)
        scaled = dl * lgain_ref[...].astype(f32)
        back = inv * (scaled - unit * jnp.mean(scaled * unit, axis=-1, keepdims=True))
        jk_scr[rows, :KVR] = back.astype(bf16)
        into = dot_nt(jq_scr[rows, :], wq_ref[...]) + dot(jk_scr[rows, :], kvd_ref[...])
        gain_sum = gain_sum + jnp.sum(into * normed_ref[rows, :].astype(f32), axis=0, keepdims=True)
        into = into.astype(bf16)
        for t in range(2):
            p_ref[i * 2 + t, :, :WIDE] = into[t * OWN : t * OWN + OWN]
    meet(1)
    late_ref[pl.ds(1536, KVR), :] = dot_tn(lnorm_ref[...], kvg_scr[...]).astype(bf16)
    for i in range(4):
        cols = pl.ds(i * 512, 512)
        late_ref[pl.ds(2048 + i * 256, 256), :] = dot_tn(attn_ref[...], hall_ref[:, cols]).astype(bf16)
        query = dot_tn(normed_ref[:, cols], jq_scr[...]).astype(bf16)
        for c in range(3):
            late_ref[pl.ds(c * 512, 512), i * 128 : i * 128 + 128] = query[:, c * 128 : c * 128 + 128]
    stores.start(late_ref, late_out)
    empty = jnp.zeros((1, 192), f32)
    lat = jnp.concatenate([v for t in range(SHARDS) for v in (lgain_sum[:, t * 64 : t * 64 + 64], empty)], axis=1)
    tail = jnp.concatenate(
        [
            gain_sum / gain_ref[...].astype(f32),
            gsum_ref[...] / fgain_ref[...].astype(f32),
            router_ref[:2, :].astype(f32),
            lat,
            jnp.zeros((59, WIDE), f32),
        ],
        axis=0,
    )
    for i in range(8):
        cols = pl.ds(i * KB, KB)
        down = dot_tn(jk_scr[...], normed_ref[:, cols])
        for c in range(4):
            at = WIDE + c * KB
            p_ref[i, :, at : at + KB] = down[c * OWN : c * OWN + OWN].astype(bf16)
        rest = jnp.concatenate(
            [down[KVR : KVR + DR] + down[KVR + DR :], tail[:, i * KB : i * KB + KB]], axis=0
        )
        p_ref[i, :, WIDE + 4 * KB :] = rest.astype(bf16)
        stores.start(p_ref.at[i], p_out.at[i])
    for copy in spread:
        copy.wait()
    for cross in crosses:
        cross.wait_send()
    stores.close()


def attend_back(*args):
    return pl.pallas_call(
        attend_back_kernel,
        out_shape=(
            jax.ShapeDtypeStruct((SHARDS, OWN, EXT), bf16),
            jax.ShapeDtypeStruct((LATE, 512), bf16),
            jax.ShapeDtypeStruct((4, QUARTER, WIDE), bf16),
        ),
        in_specs=[pl.BlockSpec(memory_space=pltpu.SMEM), anym()]
        + [vmem()] * 7
        + [anym()]
        + [vmem()] * 3
        + [anym()] * 4
        + [vmem()] * 6,
        out_specs=[anym()] * 3,
        scratch_shapes=[
            VMEM((LENGTH, WIDE), bf16),
            VMEM((LENGTH, KVR), f32),
            VMEM((WIDE, QCOLS), bf16),
            VMEM((LENGTH, WIDE), bf16),
            VMEM((LENGTH, KVR), bf16),
            VMEM((SHARDS, OWN, EXT), bf16),
            VMEM((LATE, 512), bf16),
            DMA((8,)),
            DMA((11,)),
            VMEM((LENGTH, 256), bf16),
            VMEM((2, LENGTH, 256), f32),
            VMEM((2, LENGTH, DV), f32),
            VMEM((LENGTH, QCOLS), bf16),
            VMEM((LENGTH, LATENT_ROWS), bf16),
            VMEM((LENGTH, 512), bf16),
            VMEM((LATENT_ROWS, WIDE), bf16),
            VMEM((QUARTER, WIDE), bf16),
            VMEM((QUARTER, WIDE), bf16),
            DMA((2,)),
            DMA((2,)),
            DMA((2,)),
            DMA((4,)),
            DMA((4,)),
        ],
        compiler_params=pltpu.CompilerParams(
            collective_id=4, has_side_effects=True, vmem_limit_bytes=60 * MIB
        ),
        cost_estimate=pl.CostEstimate(flops=18 * 10**9, bytes_accessed=4 * 10**7, transcendentals=2 * 10**6),
        name="attend_back",
    )(*args)


LATE_HALF = LATE // 2
LATE_PIECE = LATE_HALF // 8


def last_kernel(
    p_ref, x_ref, hgrad_ref, gain_ref, all_ref, late_hbm,
    out_ref, pack_ref, opposite_ref, lquarter_ref,
    pv, kept, core_scr, half, got, near, far, *rest,
):
    bufs, (ss, rs, gs, gr, ys, yr, xs, xr, ls) = rest[:11], rest[11:]
    n = neighbours()
    d = copies_of()
    ready = load_partials(n, p_ref, pv, ls)
    theirs = pl.ds(pl.multiple_of((1 - d["c"]) * LATE_HALF, OWN), LATE_HALF)
    mine = pl.ds(pl.multiple_of(d["c"] * LATE_HALF, OWN), LATE_HALF)
    load = pltpu.make_async_copy(late_hbm.at[mine], kept, ls.at[8])
    load.start()
    entry_barrier(ring_peers(n), (d["core"], d["yp"], d["ym"], d["xo"]))
    first = dp_copy(late_hbm.at[theirs], core_scr, xs.at[0], xr.at[0], d["core"])
    first.start()
    ysum = YSum(d, LATE_PIECE, half, got, ys, yr)
    y = d["y"]
    onward = []
    for way, (slot, peer) in enumerate(((lax.rem(y + 3, 4), d["yp"]), (lax.rem(y + 1, 4), d["ym"]))):
        rows = pl.ds(way * (QUARTER // 2), QUARTER // 2)
        onward.append(dp_copy(all_ref.at[slot, rows], opposite_ref.at[rows], gs.at[way], gr.at[way], peer))

    def work(point):
        if point == 0:
            load.wait()
            first.wait_recv()
            half[...] = added(kept[...], core_scr[...])
            ysum.step(0)
        elif point == 1:
            ysum.step(1)
        elif point == 2:
            ysum.step(2)
            for copy in onward:
                copy.start()
        elif point == 3:
            ysum.step(3)
            for way in range(2):
                near[pl.ds(way * LATE_PIECE, LATE_PIECE), :] = got[2, way]
            cross.start()

    cross = dp_copy(near, far, xs.at[1], xr.at[1], d["xo"])
    reduce_ring(n, pv, ready, bufs, ss, rs, work)
    total = own_total(n, pv, bufs)
    pack_ref[...] = total[:, WIDE:].astype(bf16)
    total = total[:, :WIDE]
    x = x_ref[...].astype(f32)
    inv = inverse_rms(x)
    unit = x * inv
    scaled = total * gain_ref[...].astype(f32)
    back = inv * (scaled - unit * jnp.mean(scaled * unit, axis=-1, keepdims=True))
    out_ref[...] = (hgrad_ref[...] + back).astype(bf16)
    cross.wait_recv()
    lquarter_ref[...] = added(near[...], far[...])
    for copy in onward:
        copy.wait()
    first.wait_send()
    cross.wait_send()
    ysum.close()


def last(p, x, hgrad, gain, quarters, late):
    return pl.pallas_call(
        last_kernel,
        out_shape=(
            jax.ShapeDtypeStruct((OWN, WIDE), bf16),
            jax.ShapeDtypeStruct((OWN, PACK_COLS), bf16),
            jax.ShapeDtypeStruct((QUARTER, WIDE), bf16),
            jax.ShapeDtypeStruct((2 * LATE_PIECE, 512), bf16),
        ),
        in_specs=[anym()] + [vmem()] * 3 + [anym()] * 2,
        out_specs=[vmem(), vmem(), anym(), vmem()],
        scratch_shapes=[
            VMEM((SHARDS, OWN, EXT), bf16),
            VMEM((LATE_HALF, 512), bf16),
            VMEM((LATE_HALF, 512), bf16),
            VMEM((LATE_HALF, 512), bf16),
            VMEM((3, 2, LATE_PIECE, 512), bf16),
            VMEM((2 * LATE_PIECE, 512), bf16),
            VMEM((2 * LATE_PIECE, 512), bf16),
        ]
        + reduce_scratch(EXT)
        + [DMA((17,)), DMA((17,)), DMA((2,)), DMA((2,)), DMA((6,)), DMA((6,)), DMA((2,)), DMA((2,)), DMA((9,))],
        compiler_params=pltpu.CompilerParams(
            collective_id=5, has_side_effects=True, vmem_limit_bytes=56 * MIB
        ),
        cost_estimate=pl.CostEstimate(flops=10**7, bytes_accessed=2 * 10**7, transcendentals=0),
        name="last",
    )(p, x, hgrad, gain, quarters, late)


def finish_kernel(
    lquarter_ref, pack_ref, all_ref, opposite_ref, moe_ref, hidden_ref,
    other, lall, packs, out_ref,
    core_scr, by_y, near, far, cs, cr, ys, yr, xs, xr, gs, gr, ls, pv, *rest,
):
    bufs, (ss, rs, ms) = rest[:11], rest[11:]
    n = neighbours()
    d = copies_of()
    c, y = d["c"], d["y"]
    ready = load_partials(n, moe_ref, pv, ms)
    local = pltpu.make_async_copy(lquarter_ref, lall.at[c, y], ls.at[0])
    local.start()
    entry_barrier(ring_peers(n), (d["core"], d["yp"], d["ym"], d["y2"], d["xo"]))
    theirs = pl.ds(pl.multiple_of((1 - c) * 64, 64), 64)
    mine = pl.ds(pl.multiple_of(c * 64, 64), 64)
    first = dp_copy(pack_ref.at[theirs], core_scr, cs.at[0], cr.at[0], d["core"])
    first.start()
    swaps = []
    for k in (0, 1, 3):
        slot = lax.rem(y + k, 4)
        swaps.append(dp_copy(all_ref.at[slot], other.at[slot], cs.at[3 + k], cr.at[3 + k], d["core"]))
    swaps.append(dp_copy(opposite_ref, other.at[lax.rem(y + 2, 4)], cs.at[5], cr.at[5], d["core"]))
    ring = reduce_steps(n, pv, ready, bufs, ss, rs)
    next(ring)
    for copy in swaps:
        copy.start()
    first.wait_recv()
    by_y[y] = added(pack_ref[mine, :], core_scr[...])
    spread = [
        dp_copy(by_y.at[y], by_y.at[y], ys.at[i], yr.at[i], d[peer]) for i, peer in enumerate(("y2", "yp", "ym"))
    ]
    for copy in spread:
        copy.start()
    ygather = YGather(d, LATE_PIECE, lall.at[c], gs, gr)
    local.wait()
    ygather.step(0)
    next(ring)
    for copy in spread:
        copy.wait_recv()
    total = by_y[0].astype(f32) + by_y[1].astype(f32) + by_y[2].astype(f32) + by_y[3].astype(f32)
    near[...] = total.astype(bf16)
    cross = dp_copy(near, far, xs.at[0], xr.at[0], d["xo"])
    cross.start()
    next(ring)
    ygather.step(1)
    next(ring)
    cross.wait_recv()
    packs[c] = added(near[...], far[...])
    pback = dp_copy(packs.at[c], packs.at[c], cs.at[2], cr.at[2], d["core"])
    pback.start()
    ygather.step(2)
    back = dp_copy(lall.at[c], lall.at[c], cs.at[1], cr.at[1], d["core"])
    back.start()
    next(ring)
    next(ring, None)
    out_ref[...] = (hidden_ref[...] + own_total(n, pv, bufs)).astype(bf16)
    for copy in (pback, back, *swaps):
        copy.wait_recv()
    for copy in (first, pback, back, cross, *spread, *swaps):
        copy.wait_send()
    ygather.close()


def finish(lquarter, pack, quarters, opposite, moe, hidden):
    return pl.pallas_call(
        finish_kernel,
        out_shape=(
            jax.ShapeDtypeStruct((4, QUARTER, WIDE), bf16),
            jax.ShapeDtypeStruct((2, 4, 2 * LATE_PIECE, 512), bf16),
            jax.ShapeDtypeStruct((2, 64, PACK_COLS), bf16),
            jax.ShapeDtypeStruct((OWN, WIDE), bf16),
        ),
        in_specs=[vmem(), vmem(), anym(), anym(), anym(), vmem()],
        out_specs=[anym(), anym(), vmem(), vmem()],
        scratch_shapes=[
            VMEM((64, PACK_COLS), bf16),
            VMEM((4, 64, PACK_COLS), bf16),
            VMEM((64, PACK_COLS), bf16),
            VMEM((64, PACK_COLS), bf16),
            DMA((7,)),
            DMA((7,)),
            DMA((3,)),
            DMA((3,)),
            DMA((1,)),
            DMA((1,)),
            DMA((4,)),
            DMA((4,)),
            DMA((1,)),
            VMEM((SHARDS, OWN, WIDE), bf16),
        ]
        + reduce_scratch(WIDE)
        + [DMA((17,)), DMA((17,)), DMA((8,))],
        compiler_params=pltpu.CompilerParams(
            collective_id=6, has_side_effects=True, vmem_limit_bytes=48 * MIB
        ),
        cost_estimate=pl.CostEstimate(flops=10**7, bytes_accessed=3 * 10**7, transcendentals=0),
        name="finish",
    )(lquarter, pack, quarters, opposite, moe, hidden)


def widen_kernel(
    own_hbm, opposite_hbm, other_hbm, lall_hbm, pack_ref, q_ref, kv_ref, o_ref, down_ref, tail_ref, sg, su, sd, eg, eu, ed,
    wide, full_ref, lall_ref, os, hs,
):
    stores = []
    loads = Copies(hs)
    d = copies_of()
    c, y = d["c"], d["y"]
    for k in range(4):
        slot = lax.rem(y + k, 4)
        rows = pl.ds(pl.multiple_of(slot * QUARTER, 32), QUARTER)
        loads.start(opposite_hbm if k == 2 else own_hbm.at[slot], full_ref.at[c, rows])
    loads.start(other_hbm, full_ref.at[1 - c])
    loads.start(lall_hbm, lall_ref)

    def put(start, count, dst):
        copy = pltpu.make_async_copy(wide.at[pl.ds(start, count)], dst, os.at[len(stores)])
        copy.start()
        stores.append(copy)

    for index, (shared, experts) in enumerate(((sg, eg), (su, eu), (sd, ed))):
        base = index * HID
        if index == 0:
            for copy in loads.made[:5]:
                copy.wait()
        for k in range(index * 3, index * 3 + 3):
            for core in range(2):
                wide[pl.ds(k * 256 + core * OWN, OWN), :] = full_ref[core, pl.ds(k * OWN, OWN), :].astype(f32)
        put(base, FS_OWN, shared)
        put(base + 384, FE_OWN, experts.at[0])
        put(base + 384 + FE_OWN, FE_OWN, experts.at[1])
    loads.made[5].wait()
    for k in range(3):
        for i in range(4):
            block = lall_ref[0, pl.ds(k * 512, 512), i * 128 : i * 128 + 128]
            q_ref[pl.ds(i * 512, 512), k * 128 : k * 128 + 128] = block.astype(f32)
    kv_ref[...] = lall_ref[1, pl.ds(0, KVR), :].astype(f32)
    for i in range(4):
        o_ref[:, i * 512 : i * 512 + 512] = lall_ref[1, pl.ds(512 + i * 256, 256), :].astype(f32)
    for j in range(4):
        down_ref[pl.ds(j * OWN, OWN), :] = pack_ref[:, j * KB : j * KB + KB].astype(f32)
    down_ref[pl.ds(KVR, DR), :] = pack_ref[:DR, 4 * KB :].astype(f32)
    tail_ref[...] = pack_ref[DR : DR + 16, 4 * KB :].astype(f32)
    for copy in stores:
        copy.wait()


def widen(own, opposite, other, lall, packs):
    def out(*shape):
        return jax.ShapeDtypeStruct(shape, f32)

    shared, experts = out(FS_OWN, WIDE), out(2, FE_OWN, WIDE)
    return pl.pallas_call(
        widen_kernel,
        out_shape=(
            out(WIDE, QCOLS), out(KVR, 512), out(256, WIDE), out(576, 256), out(16, 256),
            shared, shared, shared, experts, experts, experts,
        ),
        in_specs=[anym()] * 4 + [vmem()],
        out_specs=[vmem()] * 5 + [anym()] * 6,
        scratch_shapes=[
            VMEM((3 * HID, WIDE), f32),
            VMEM((2, BLOCKS * OWN, WIDE), bf16),
            VMEM((2, LATE_HALF, 512), bf16),
            DMA((9,)),
            DMA((6,)),
        ],
        compiler_params=pltpu.CompilerParams(vmem_limit_bytes=60 * MIB),
        cost_estimate=pl.CostEstimate(flops=10**7, bytes_accessed=4 * 10**7, transcendentals=0),
        name="widen",
    )(own, opposite, other.reshape(BLOCKS * OWN, WIDE), lall.reshape(2, LATE_HALF, 512), packs.reshape(OWN, PACK_COLS))


def rope_tables():
    half = DR // 2
    frequency = ROPE_BASE ** (-(np.arange(half, dtype=np.float64) * 2.0) / DR)
    angles = np.arange(LENGTH, dtype=np.float64)[:, None] * frequency[None, :]
    cos = np.cos(angles).astype(np.float32)
    sin = np.sin(angles).astype(np.float32)
    return np.concatenate([cos] * 4, axis=1), np.concatenate([-sin, sin, -sin, sin], axis=1)


def after(value, *others):
    return lax.optimization_barrier((value, *others))[0]


def flat(v):
    return v.reshape(LENGTH, v.shape[-1])


def body(
    layer_in, grad_out, routes, prefix, attn_gain, query_proj, kv_down, latent_gain, kv_up,
    out_proj, ffn_gain, router_proj, shared_gate, shared_up, shared_down, expert_gate, expert_up, expert_down,
):
    cos_np, sin_np = rope_tables()
    cos, sin = jnp.asarray(cos_np), jnp.asarray(sin_np)
    again, lgain, fgain = attn_gain[None], latent_gain[None], ffn_gain[None]
    kvd = kv_down.T
    sg, su = shared_gate.T, shared_up.T
    eg, eu = jnp.swapaxes(expert_gate, 1, 2), jnp.swapaxes(expert_up, 1, 2)
    rt = jnp.pad(router_proj.T, ((0, 30), (0, 0)))

    *projected, grad_all = project(layer_in, grad_out, again, query_proj, kvd, lgain, kv_up, cos, sin)
    normed, q, kvw, kr, lnorm, latent = map(flat, projected)
    attn, lse, ot, p1 = attend(prefix, q, kvw, kr, out_proj)
    hidden, mixed, m, da, db, p2, gsum = hidden_ffn(
        p1, layer_in, fgain, grad_all, routes.reshape(SHARDS, OWN, 1),
        sg, su, shared_down, eg, eu, expert_down, rt,
    )
    hgrad, low, half, router_rows, moe = turn_back(
        p2, hidden, grad_out, fgain, mixed, grad_all, m, da, db, shared_down, expert_down
    )
    hall, ysum = gather(low, half.reshape(BLOCKS * OWN, WIDE))
    hall = flat(hall)
    p3, late, quarters = attend_back(
        prefix, hall, out_proj, q, kvw, kr, lse, ot, kv_up, latent, lgain, cos, sin, query_proj, kvd,
        normed, lnorm, attn, again, fgain, gsum, router_rows, ysum,
    )
    input_grad, pack, opposite, lquarter = last(p3, layer_in, hgrad, again, quarters, late)
    other, lall, packs, layer_out = finish(lquarter, pack, quarters, opposite, moe, hidden)
    dq, dkv, do, ddown, tail, dsg, dsu, dsd, deg, deu, ded = widen(quarters, opposite, other, lall, packs)
    return (
        layer_out,
        input_grad,
        tail[0],
        dq,
        ddown.T,
        tail[4, : KVR // SHARDS],
        dkv,
        do,
        tail[1],
        tail[2:4].T,
        dsg.T,
        dsu.T,
        dsd,
        jnp.swapaxes(deg, 1, 2),
        jnp.swapaxes(deu, 1, 2),
        ded,
    )


def solution(mesh):
    placed = (
        P(("dp", "tensor"), None),
        P(("dp", "tensor"), None),
        P("dp", None),
        P("dp"),
        P(),
        P(None, "tensor"),
        P(),
        P(),
        P(None, "tensor"),
        P("tensor", None),
        P(),
        P(),
        P(None, "tensor"),
        P(None, "tensor"),
        P("tensor", None),
        P(None, None, "tensor"),
        P(None, None, "tensor"),
        P(None, "tensor", None),
    )
    return jax.shard_map(
        body,
        mesh=mesh,
        in_specs=placed,
        out_specs=(
            P(("dp", "tensor"), None),
            P(("dp", "tensor"), None),
            P("tensor"),
            P(None, "tensor"),
            P("tensor", None),
            P("tensor"),
            P(None, "tensor"),
            P("tensor", None),
            P("tensor"),
            P("tensor", None),
            P(None, "tensor"),
            P(None, "tensor"),
            P("tensor", None),
            P(None, None, "tensor"),
            P(None, None, "tensor"),
            P(None, "tensor", None),
        ),
        check_vma=False,
    )
```

```python
import functools

import jax
import jax.numpy as jnp
import numpy as np
from jax import lax
from jax.experimental import pallas as pl
from jax.experimental.pallas import tpu as pltpu
from jax.sharding import PartitionSpec as P

DN = 128
DR = 64
DV = 128
KVR = 512
EPS = 1e-06
ROPE_BASE = 10000.0
LOG2E = 1.4426950408889634
SCALE = (DN + DR) ** (-0.5)
NEG = -1e30
MIB = 2**20
MESH = pl.DeviceIdType.MESH
f32 = jnp.float32
bf16 = jnp.bfloat16
VMEM = pltpu.VMEM
DMA = pltpu.SemaphoreType.DMA

OWN = 128
SHARDS = 8
LENGTH = OWN * SHARDS
WIDE = 2048
FS_OWN = 352
FE_OWN = 176
HID = 768
QCOLS = 384
LATENT_ROWS = 640


def vmem():
    return pl.BlockSpec(memory_space=pltpu.VMEM)


def anym():
    return pl.BlockSpec(memory_space=pltpu.HBM)


def dot(a, b):
    return jnp.dot(a, b, preferred_element_type=f32)


def dot_nt(a, b):
    return lax.dot_general(a, b, (((1,), (1,)), ((), ())), preferred_element_type=f32)


def dot_tn(a, b):
    return lax.dot_general(a, b, (((0,), (0,)), ((), ())), preferred_element_type=f32)


def neighbours():
    t = lax.axis_index("tensor")
    x = t // 4
    z = t % 4
    zp = lax.rem(z + 1, 4)
    zm = lax.rem(z + 3, 4)
    z2 = lax.rem(z + 2, 4)
    own = x * 4
    far = (1 - x) * 4
    return dict(
        me=t, tp=own + zp, tm=own + zm, t2=own + z2, tx=far + z, xp=far + zp, xm=far + zm, x2=far + z2
    )


def copies_of():
    d = lax.axis_index("dp")
    c = lax.rem(d, 2)
    y = lax.rem(d // 2, 4)
    plane = d // 8
    here = plane * 8 + c
    return dict(
        c=c, y=y, core=d + 1 - 2 * c, y2=here + lax.rem(y + 2, 4) * 2, yp=here + lax.rem(y + 1, 4) * 2, ym=here + lax.rem(y + 3, 4) * 2,
        xo=(1 - plane) * 8 + y * 2 + c,
    )


def entry_barrier(tensor=(), dp=()):
    sem = pltpu.get_barrier_semaphore()
    for peer in tensor:
        pl.semaphore_signal(sem, inc=1, device_id={"tensor": peer}, device_id_type=MESH)
    for peer in dp:
        pl.semaphore_signal(sem, inc=1, device_id={"dp": peer}, device_id_type=MESH)
    pl.semaphore_wait(sem, len(tensor) + len(dp))


def ring_peers(n):
    return (n["tp"], n["tm"], n["tx"])


class YSum:
    def __init__(self, d, rows, a_ref, base, got, ss, rs, sem):
        self.d, self.rows, self.a, self.base, self.got = d, rows, a_ref, base, got
        self.ss, self.rs, self.sem = ss, rs, sem
        self.pending = None
        self.all = []

    def piece(self, way, hops):
        owner = lax.rem(self.d["y"] + ((3 - hops) if way == 0 else (1 + hops)) + 4, 4)
        start = pl.multiple_of(self.base + (owner * 2 + way) * self.rows, 16)
        return pl.ds(start, self.rows)

    def step(self, s):
        if s:
            for c in self.pending:
                c.wait_recv()
            for way in range(2):
                here = self.piece(way, s)
                self.got[s - 1, way] = added(self.got[s - 1, way], self.a[here, :])
        if s == 3:
            return
        self.pending = []
        for way in range(2):
            src = self.a.at[self.piece(way, 0)] if s == 0 else self.got.at[s - 1, way]
            c = pltpu.make_async_remote_copy(
                src_ref=src,
                dst_ref=self.got.at[s, way],
                send_sem=self.ss.at[self.sem + s * 2 + way],
                recv_sem=self.rs.at[self.sem + s * 2 + way],
                device_id={"dp": self.d["yp"] if way == 0 else self.d["ym"]},
                device_id_type=MESH,
            )
            c.start()
            self.pending.append(c)
            self.all.append(c)

    def close(self):
        for c in self.all:
            c.wait_send()


class YGather:
    def __init__(self, d, rows, g_ref, ss, rs):
        self.d, self.rows, self.g, self.ss, self.rs = d, rows, g_ref, ss, rs
        self.all = []

    def send(self, i, slot, start, count, way):
        view = self.g.at[slot, pl.ds(start, count)]
        copy = dp_copy(view, view, self.ss.at[i], self.rs.at[i], self.d["yp"] if way == 0 else self.d["ym"])
        copy.start()
        self.all.append(copy)

    def step(self, s):
        y = self.d["y"]
        if s == 0:
            self.send(0, y, 0, 2 * self.rows, 0)
            self.send(1, y, 0, 2 * self.rows, 1)
        elif s == 1:
            self.all[0].wait_recv()
            self.send(2, lax.rem(y + 3, 4), 0, self.rows, 0)
            self.all[1].wait_recv()
            self.send(3, lax.rem(y + 1, 4), self.rows, self.rows, 1)
        else:
            self.all[2].wait_recv()
            self.all[3].wait_recv()


def y_spread(d, ref, ss, rs, sem):
    mine = ref.at[d["y"]]
    return [
        dp_copy(mine, mine, ss.at[sem + i], rs.at[sem + i], d[peer]) for i, peer in enumerate(("y2", "yp", "ym"))
    ]


def y_deal(d, ref, rows, got, ss, rs, sem):
    y = d["y"]
    copies = []
    for i, (hops, peer) in enumerate(((2, "y2"), (1, "yp"), (3, "ym"))):
        start = pl.multiple_of(lax.rem(y + hops, 4) * rows, 16)
        src = ref.at[pl.ds(start, rows)]
        copies.append(dp_copy(src, got.at[y], ss.at[sem + i], rs.at[sem + i], d[peer]))
    return copies


def dp_copy(src, dst, ss, rs, peer):
    return pltpu.make_async_remote_copy(
        src_ref=src, dst_ref=dst, send_sem=ss, recv_sem=rs, device_id={"dp": peer}, device_id_type=MESH
    )


def sender(ss, rs):
    def send(i, src, dst, dev):
        return pltpu.make_async_remote_copy(
            src_ref=src,
            dst_ref=dst,
            send_sem=ss.at[i],
            recv_sem=rs.at[i],
            device_id={"tensor": dev},
            device_id_type=MESH,
        )

    return send


def gather_steps(n, x_ref, o_ref, ss, rs):
    send = sender(ss, rs)

    def s(i, src, slot, o, k, dev):
        return send(i, src, o_ref.at[slot, pl.ds(o, k)], dev)

    def part(slot, o, k):
        return o_ref.at[slot, pl.ds(o, k)]

    me, tp, tm, tx, t2, xp, xm, x2 = (n[k] for k in ("me", "tp", "tm", "tx", "t2", "xp", "xm", "x2"))
    s1a = s(0, x_ref.at[pl.ds(0, 64)], me, 0, 64, tp)
    s2a = s(1, x_ref.at[pl.ds(64, 64)], me, 64, 64, tm)
    s3 = s(2, x_ref, me, 0, 128, tx)
    s1b = s(11, x_ref.at[pl.ds(64, 64)], me, 64, 64, tp)
    s2b = s(12, x_ref.at[pl.ds(0, 64)], me, 0, 64, tm)
    for c in (s1a, s2a, s3, s1b, s2b):
        c.start()
    yield me
    s1a.wait_recv()
    s4 = s(3, part(tm, 0, 64), tm, 0, 64, tp)
    s6a = s(5, part(tm, 0, 64), tm, 0, 64, tx)
    s4.start()
    s6a.start()
    s2a.wait_recv()
    s5 = s(4, part(tp, 64, 64), tp, 64, 64, tm)
    s7a = s(6, part(tp, 64, 64), tp, 64, 64, tx)
    s5.start()
    s7a.start()
    s3.wait_recv()
    s8 = s(7, part(tx, 80, 48), tx, 80, 48, tp)
    s9 = s(8, part(tx, 0, 48), tx, 0, 48, tm)
    s8.start()
    s9.start()
    s1b.wait_recv()
    s6b = s(13, part(tm, 64, 16), tm, 64, 16, tx)
    s6b.start()
    s2b.wait_recv()
    s7b = s(14, part(tp, 48, 16), tp, 48, 16, tx)
    s7b.start()
    yield tm
    s6a.wait_recv()
    s10 = s(9, part(xm, 0, 64), xm, 0, 64, tp)
    s10.start()
    s7a.wait_recv()
    s11 = s(10, part(xp, 64, 64), xp, 64, 64, tm)
    s11.start()
    yield tp
    yield tx
    s4.wait_recv()
    s5.wait_recv()
    yield t2
    s8.wait_recv()
    s6b.wait_recv()
    yield xm
    s9.wait_recv()
    s7b.wait_recv()
    yield xp
    s10.wait_recv()
    s11.wait_recv()
    yield x2
    for c in (s1a, s1b, s2a, s2b, s3, s4, s5, s6a, s6b, s7a, s7b, s8, s9, s10, s11):
        c.wait_send()


def gather_ring(n, x_ref, o_ref, ss, rs, on_shard=None):
    for slot in gather_steps(n, x_ref, o_ref, ss, rs):
        if on_shard:
            on_shard(slot)


def reduce_steps(n, pv, ready, bufs, ss, rs):
    send = sender(ss, rs)
    me, tp, tm, tx, t2, xp, xm, x2 = (n[k] for k in ("me", "tp", "tm", "tx", "t2", "xp", "xm", "x2"))
    r10, r11, r8, r9, r6, r7, r4, r5, m1, m2, m3 = bufs

    def s(i, slot, o, k, dst, dev):
        return send(i, pv.at[slot, pl.ds(o, k)], dst, dev)

    def add(slot, o, k, buf):
        pv[slot, pl.ds(o, k)] = added(pv[slot, pl.ds(o, k)], buf[...])

    ready("x2")
    s10 = s(0, x2, 0, 64, r10, tm)
    s11 = s(1, x2, 64, 64, r11, tp)
    s10.start()
    s11.start()
    ready("tx")
    s3b = s(10, tx, 48, 32, m3.at[pl.ds(48, 32)], tx)
    s3b.start()
    ready("xm")
    ready("xp")
    s6b = s(15, xm, 64, 16, r6.at[pl.ds(64, 16)], tx)
    s7b = s(16, xp, 48, 16, r7.at[pl.ds(0, 16)], tx)
    s6b.start()
    s7b.start()
    ready("t2")
    s4 = s(2, t2, 0, 64, r4, tm)
    s5 = s(3, t2, 64, 64, r5, tp)
    s4.start()
    s5.start()
    s8 = s(4, xm, 80, 48, r8, tm)
    s9 = s(5, xp, 0, 48, r9, tp)
    s8.start()
    s9.start()
    ready("tm")
    ready("tp")
    s1b = s(11, tm, 80, 48, m1.at[pl.ds(80, 48)], tm)
    s2b = s(12, tp, 0, 48, m2.at[pl.ds(0, 48)], tp)
    s1b.start()
    s2b.start()
    yield
    s10.wait_recv()
    add(xm, 0, 64, r10)
    s6 = s(6, xm, 0, 64, r6.at[pl.ds(0, 64)], tx)
    s6.start()
    s11.wait_recv()
    add(xp, 64, 64, r11)
    s7 = s(7, xp, 64, 64, r7.at[pl.ds(16, 64)], tx)
    s7.start()
    yield
    s8.wait_recv()
    add(tx, 80, 48, r8)
    s9.wait_recv()
    add(tx, 0, 48, r9)
    s3a = s(13, tx, 80, 48, m3.at[pl.ds(80, 48)], tx)
    s3c = s(14, tx, 0, 48, m3.at[pl.ds(0, 48)], tx)
    s3a.start()
    s3c.start()
    yield
    s4.wait_recv()
    add(tm, 0, 64, r4)
    s6.wait_recv()
    s6b.wait_recv()
    add(tm, 0, 80, r6)
    s1 = s(8, tm, 0, 80, m1.at[pl.ds(0, 80)], tm)
    s1.start()
    yield
    s5.wait_recv()
    add(tp, 64, 64, r5)
    s7.wait_recv()
    s7b.wait_recv()
    add(tp, 48, 80, r7)
    s2 = s(9, tp, 48, 80, m2.at[pl.ds(48, 80)], tp)
    s2.start()
    yield
    ready("me")
    for c in (s3a, s3b, s3c, s1b, s2b, s1, s2):
        c.wait_recv()
    for c in (s1, s1b, s2, s2b, s3a, s3b, s3c, s4, s5, s6, s6b, s7, s7b, s8, s9, s10, s11):
        c.wait_send()


def reduce_ring(n, pv, ready, bufs, ss, rs, work=None):
    for point, _ in enumerate(reduce_steps(n, pv, ready, bufs, ss, rs)):
        if work:
            work(point)


def reduce_scratch(columns):
    rows = (64, 64, 48, 48, 80, 80, 64, 64, 128, 128, 128)
    return [VMEM((r, columns), bf16) for r in rows]


def added(a, b):
    return (a.astype(f32) + b.astype(f32)).astype(bf16)


def load_partials(n, p_ref, pv, ls):
    order = ("x2", "tx", "xm", "xp", "t2", "tm", "tp", "me")
    copies = {}
    for i, name in enumerate(order):
        copies[name] = pltpu.make_async_copy(p_ref.at[n[name]], pv.at[n[name]], ls.at[i])
        copies[name].start()
    return lambda name: copies[name].wait()


def inverse_rms(v):
    return lax.rsqrt(jnp.mean(v * v, axis=-1, keepdims=True) + EPS)


class Copies:
    def __init__(self, sems):
        self.sems, self.made = sems, []

    def start(self, src, dst):
        copy = pltpu.make_async_copy(src, dst, self.sems.at[len(self.made)])
        copy.start()
        self.made.append(copy)
        return copy

    def close(self):
        for copy in self.made:
            copy.wait()


def turn(v, cos, sin):
    lane = lax.broadcasted_iota(jnp.int32, v.shape, 1)
    low = lax.rem(lane, 64) < 32
    swapped = jnp.where(low, pltpu.roll(v, 96, 1), pltpu.roll(v, 32, 1))
    return v * cos + swapped * sin


def fetch_latent_weights(kvd_hbm, kvd_ref, sems):
    copies = [
        pltpu.make_async_copy(kvd_hbm, kvd_ref.at[pl.ds(0, KVR + DR)], sems.at[0]),
        pltpu.make_async_copy(kvd_hbm.at[pl.ds(KVR, DR)], kvd_ref.at[pl.ds(KVR + DR, DR)], sems.at[1]),
    ]
    for c in copies:
        c.start()
    return copies


def project_kernel(
    x_hbm, grad_ref, gain_ref, wq_hbm, kvd_hbm, lgain_ref, kvup_hbm, cos_hbm, sin_hbm,
    normed_out, q_ref, kvw_ref, kr_ref, lnorm_out, latent_out, gall_ref,
    xall, wq_ref, kvd_ref, normed_ref, lnorm_ref, latent_ref, x_ref, kvup_ref, cos_ref, sin_ref,
    ss, rs, gs, gr, ls, os, hs,
):
    n = neighbours()
    loads = Copies(hs)
    entry_barrier(ring_peers(n))

    def compute(slot, src):
        x = src.astype(f32)
        normed = (x * inverse_rms(x) * gain_ref[...].astype(f32)).astype(bf16)
        normed_ref[slot] = normed
        raw = dot(normed, wq_ref[...])
        rows = pl.ds(pl.multiple_of(slot * OWN, OWN), OWN)
        cos = cos_ref[rows, :]
        sin = sin_ref[rows, :]
        q_ref[slot, :, :128] = raw[:, :128].astype(bf16)
        q_ref[slot, :, 128:256] = raw[:, 192:320].astype(bf16)
        rope = jnp.concatenate([raw[:, 128:192], raw[:, 320:384]], axis=1)
        q_ref[slot, :, 256:] = turn(rope, cos, sin).astype(bf16)
        raw = dot_nt(normed, kvd_ref[...])
        latent = raw[:, :KVR]
        latent_ref[slot] = latent
        lnorm = (latent * inverse_rms(latent) * lgain_ref[...].astype(f32)).astype(bf16)
        lnorm_ref[slot] = lnorm
        kr_ref[slot] = turn(raw[:, KVR:], cos, sin).astype(bf16)
        kvw_ref[slot] = dot(lnorm, kvup_ref[...]).astype(bf16)
        for src, dst in ((normed_ref, normed_out), (lnorm_ref, lnorm_out), (latent_ref, latent_out)):
            stores.start(src.at[slot], dst.at[slot])

    stores = Copies(os)
    second = gather_steps(n, grad_ref, gall_ref, gs, gr)
    local = pltpu.make_async_copy(grad_ref, gall_ref.at[n["me"]], ls.at[3])
    for k, slot in enumerate(gather_steps(n, x_hbm, xall, ss, rs)):
        if k == 0:
            loads.start(x_hbm, x_ref)
            loads.start(wq_hbm, wq_ref)
            copies = fetch_latent_weights(kvd_hbm, kvd_ref, ls)
            for src, dst in ((kvup_hbm, kvup_ref), (cos_hbm, cos_ref), (sin_hbm, sin_ref)):
                loads.start(src, dst)
            local.start()
            loads.close()
            for c in copies:
                c.wait()
            compute(slot, x_ref[...])
            continue
        if k == 1:
            next(second)
        if k == 4:
            next(second)
        if k == 7:
            next(second)
        compute(slot, xall[slot])
    for slot in second:
        pass
    local.wait()
    stores.close()


def project(x, grad, gain, wq, kvd, lgain, kvup, cos, sin):
    def out(c, t):
        return jax.ShapeDtypeStruct((SHARDS, OWN, c), t)

    outs = (out(WIDE, bf16), out(QCOLS, bf16), out(512, bf16), out(128, bf16), out(KVR, bf16), out(KVR, f32))
    outs += (out(WIDE, bf16),)
    return pl.pallas_call(
        project_kernel,
        out_shape=outs,
        in_specs=[anym(), anym(), vmem(), anym(), anym(), vmem(), anym(), anym(), anym()],
        out_specs=[anym()] + [vmem()] * 3 + [anym()] * 3,
        scratch_shapes=[
            VMEM((SHARDS, OWN, WIDE), bf16),
            VMEM((WIDE, QCOLS), bf16),
            VMEM((LATENT_ROWS, WIDE), bf16),
            VMEM((SHARDS, OWN, WIDE), bf16),
            VMEM((SHARDS, OWN, KVR), bf16),
            VMEM((SHARDS, OWN, KVR), f32),
            VMEM((OWN, WIDE), bf16),
            VMEM((KVR, 512), bf16),
            VMEM((LENGTH, 128), f32),
            VMEM((LENGTH, 128), f32),
            DMA((17,)),
            DMA((17,)),
            DMA((17,)),
            DMA((17,)),
            DMA((4,)),
            DMA((24,)),
            DMA((5,)),
        ],
        compiler_params=pltpu.CompilerParams(
            collective_id=0, has_side_effects=True, vmem_limit_bytes=60 * MIB
        ),
        cost_estimate=pl.CostEstimate(flops=5 * 10**9, bytes_accessed=2 * 10**7, transcendentals=0),
        name="project",
    )(x, grad, gain, wq, kvd, lgain, kvup, cos, sin)


KB = 256


def masked(s, key0, query0, prefix):
    keys = key0 + lax.broadcasted_iota(jnp.int32, s.shape, 0)
    rows = query0 + lax.broadcasted_iota(jnp.int32, s.shape, 1)
    return jnp.where((keys <= rows) | (keys < prefix), s, NEG)


def key_extent(query_block):
    return max(2, query_block + 1)


def head_lanes(shape, head):
    lane = lax.broadcasted_iota(jnp.int32, shape, 1)
    return (lane >= 64) if head else (lane < 64)


def head_query(q_ref, rows, head):
    rope = q_ref[rows, 256:QCOLS]
    rope = jnp.where(head_lanes(rope.shape, head), rope.astype(f32), 0.0).astype(bf16)
    return jnp.concatenate([q_ref[rows, head * 128 : head * 128 + 128], rope], axis=1)


def head_key(kvw_ref, kr_ref, rows, head):
    return jnp.concatenate([kvw_ref[rows, head * 256 : head * 256 + 128], kr_ref[rows, :]], axis=1)


def attend_kernel(prefix_ref, q_ref, kvw_ref, kr_ref, wo_ref, attn_ref, lse_ref, ot_ref, p_out, s_scr, p_ref, os):
    prefix = prefix_ref[0]
    stores = Copies(os)
    for i in range(4):
        rows = pl.ds(i * KB, KB)
        for h in range(2):
            q = head_query(q_ref, rows, h)
            top = jnp.full((1, KB), NEG, f32)
            for k in range(key_extent(i)):
                keys = pl.ds(k * KB, KB)
                s = dot_nt(head_key(kvw_ref, kr_ref, keys, h), q)
                if k >= i:
                    s = masked(s, k * KB, i * KB, prefix)
                s_scr[keys, :] = s
                top = jnp.maximum(top, jnp.max(s, axis=0, keepdims=True))
            top = top * (SCALE * LOG2E)
            total = jnp.zeros((1, KB), f32)
            out = jnp.zeros((DV, KB), f32)
            for k in range(key_extent(i)):
                keys = pl.ds(k * KB, KB)
                p = jnp.exp2(s_scr[keys, :] * (SCALE * LOG2E) - top)
                total = total + jnp.sum(p, axis=0, keepdims=True)
                out = out + dot_tn(kvw_ref[keys, h * 256 + 128 : h * 256 + 256], p.astype(bf16))
            out = out / total
            lse_ref[h : h + 1, rows] = top + jnp.log2(total)
            ot_ref[h, :, rows] = out
            attn_ref[rows, h * 128 : h * 128 + 128] = out.T.astype(bf16)
        p_ref[rows, :] = dot(attn_ref[rows, :], wo_ref[...]).astype(bf16)
        stores.start(p_ref.at[rows], p_out.at[rows])
    stores.close()


def attend(prefix, q, kvw, kr, wo):
    return pl.pallas_call(
        attend_kernel,
        out_shape=(
            jax.ShapeDtypeStruct((LENGTH, 256), bf16),
            jax.ShapeDtypeStruct((2, LENGTH), f32),
            jax.ShapeDtypeStruct((2, DV, LENGTH), f32),
            jax.ShapeDtypeStruct((LENGTH, WIDE), bf16),
        ),
        in_specs=[pl.BlockSpec(memory_space=pltpu.SMEM)] + [vmem()] * 4,
        out_specs=[vmem()] * 3 + [anym()],
        scratch_shapes=[VMEM((LENGTH, KB), f32), VMEM((LENGTH, WIDE), bf16), DMA((4,))],
        compiler_params=pltpu.CompilerParams(vmem_limit_bytes=60 * MIB),
        cost_estimate=pl.CostEstimate(flops=25 * 10**8, bytes_accessed=10**7, transcendentals=2 * 10**6),
        name="attend",
    )(prefix, q, kvw, kr, wo)


def own_total(n, pv, bufs):
    m1, m2, m3 = bufs[8:]
    return pv[n["me"]].astype(f32) + m1[...].astype(f32) + m2[...].astype(f32) + m3[...].astype(f32)


def fetch_hidden_weights(sg, eg, dst, zero_ref, sems, base):
    pieces = [(sg, 0, FS_OWN), (eg.at[0], 384, FE_OWN), (eg.at[1], 384 + FE_OWN, FE_OWN)]
    pieces += [(zero_ref, 736, 32), (zero_ref, FS_OWN, 32)]
    copies = []
    for i, (src, at, count) in enumerate(pieces):
        c = pltpu.make_async_copy(src, dst.at[pl.ds(at, count)], sems.at[base + i])
        c.start()
        copies.append(c)
    return copies


def ffn_rows(mixed, dm, route, wg_ref, wu_ref):
    a = dot_nt(mixed, wg_ref[...])
    b = dot_nt(mixed, wu_ref[...])
    first = (route == 0.0).astype(f32)
    second = (route == 1.0).astype(f32)
    l0 = a[:, FS_OWN : FS_OWN + 1]
    l1 = a[:, FS_OWN + 1 : FS_OWN + 2]
    top = jnp.maximum(l0, l1)
    e0 = jnp.exp(l0 - top)
    e1 = jnp.exp(l1 - top)
    r0 = e0 / (e0 + e1)
    r1 = e1 / (e0 + e1)
    col = lax.broadcasted_iota(jnp.int32, (1, HID), 1)
    is_shared = col < 384
    in0 = (col >= 384) & (col < 384 + FE_OWN)
    in1 = (col >= 384 + FE_OWN) & (col < 384 + 2 * FE_OWN)
    gate = jnp.where(is_shared, 1.0, 0.0) + jnp.where(in0, first * r0, 0.0) + jnp.where(in1, second * r1, 0.0)
    sig = jax.nn.sigmoid(a)
    silu = a * sig
    act = silu * b
    m = (gate * act).astype(bf16)
    scaled = dm * gate
    down = dm * act
    g0 = first * jnp.sum(jnp.where(in0, down, 0.0), axis=1, keepdims=True)
    g1 = second * jnp.sum(jnp.where(in1, down, 0.0), axis=1, keepdims=True)
    mean = r0 * g0 + r1 * g1
    da = scaled * b * (sig * (1.0 + a * (1.0 - sig)))
    da = da + jnp.where(col == FS_OWN, r0 * (g0 - mean), 0.0) + jnp.where(col == FS_OWN + 1, r1 * (g1 - mean), 0.0)
    da = da.astype(bf16)
    db = (scaled * silu).astype(bf16)
    return m, da, db, dot(da, wg_ref[...]) + dot(db, wu_ref[...])


def hidden_ffn_kernel(
    p_ref, x_ref, gain_ref, grad_hbm, routes_ref, sg, su, sd, eg, eu, ed, rt_ref,
    hidden_ref, mixed_out, m_out, da_out, db_out, p2_out, gsum_ref,
    mixed_ref, m_ref, da_ref, db_ref, p2_ref, os, pv, own, gall, dm_scr, wg_ref, wu_ref, wd_ref, zero_ref, *rest,
):
    bufs, (ss, rs, gs, gr, ls, ws) = rest[:11], rest[11:]
    n = neighbours()
    ready = load_partials(n, p_ref, pv, ls)
    zero_ref[...] = jnp.zeros_like(zero_ref)
    gcopy = pltpu.make_async_copy(grad_hbm, gall, ws.at[15])
    copies = []
    entry_barrier(ring_peers(n))

    def work(point):
        if point == 0:
            copies.extend(fetch_hidden_weights(sd, ed, wd_ref, zero_ref, ws, 10))
            gcopy.start()
            copies.extend(fetch_hidden_weights(sg, eg, wg_ref, zero_ref, ws, 0))
            copies.extend(fetch_hidden_weights(su, eu, wu_ref, zero_ref, ws, 5))
            for c in copies[:5] + [gcopy]:
                c.wait()
        if point == 4:
            for c in copies[5:]:
                c.wait()
            router = jnp.concatenate([rt_ref[...].astype(f32), jnp.zeros((30, WIDE), f32)], axis=0)
            wg_ref[pl.ds(FS_OWN, 32), :] = router.astype(bf16)
        if point < 4:
            two = pl.ds(point * 2, 2)
            dm_scr[two] = dot_nt(gall[two].reshape(256, WIDE), wd_ref[...]).reshape(2, OWN, HID)

    reduce_ring(n, pv, ready, bufs, ss, rs, work)
    hidden = x_ref[...].astype(f32) + own_total(n, pv, bufs)
    hidden_ref[...] = hidden
    own[...] = (hidden * inverse_rms(hidden) * gain_ref[...].astype(f32)).astype(bf16)
    mixed_ref[n["me"]] = own[...]
    gsum_ref[...] = jnp.zeros_like(gsum_ref)
    waiting = []
    by_token = routes_ref[...].astype(f32).T

    def on_shard(slot):
        waiting.append(slot)
        if len(waiting) < 2:
            return
        pair = list(waiting)
        waiting.clear()
        mixed = jnp.concatenate([mixed_ref[s] for s in pair], axis=0)
        dm = jnp.concatenate([dm_scr[s] for s in pair], axis=0)
        shard = lax.broadcasted_iota(jnp.int32, (OWN, SHARDS), 1)
        route = jnp.concatenate(
            [jnp.sum(jnp.where(shard == s, by_token, 0.0), axis=1, keepdims=True) for s in pair], axis=0
        )
        m, da, db, back = ffn_rows(mixed, dm, route, wg_ref, wu_ref)
        gsum_ref[...] += jnp.sum(back * mixed.astype(f32), axis=0, keepdims=True)
        back = back.astype(bf16)
        for i, s in enumerate(pair):
            part = slice(i * OWN, i * OWN + OWN)
            m_ref[s] = m[part]
            da_ref[s] = da[part]
            db_ref[s] = db[part]
            p2_ref[s] = back[part]
            for src, dst in (
                (mixed_ref, mixed_out), (m_ref, m_out), (da_ref, da_out), (db_ref, db_out), (p2_ref, p2_out)
            ):
                stores.start(src.at[s], dst.at[s])

    stores = Copies(os)
    gather_ring(n, own, mixed_ref, gs, gr, on_shard)
    stores.close()


def hidden_ffn(p, x, gain, grad, routes, sg, su, sd, eg, eu, ed, rt):
    def out(c, t=bf16):
        return jax.ShapeDtypeStruct((SHARDS, OWN, c), t)

    row = jax.ShapeDtypeStruct((1, WIDE), f32)
    outs = (jax.ShapeDtypeStruct((OWN, WIDE), f32), out(WIDE), out(HID), out(HID), out(HID), out(WIDE), row)
    return pl.pallas_call(
        hidden_ffn_kernel,
        out_shape=outs,
        in_specs=[anym(), vmem(), vmem(), anym(), vmem()] + [anym()] * 6 + [vmem()],
        out_specs=[vmem()] + [anym()] * 5 + [vmem()],
        scratch_shapes=[
            VMEM((SHARDS, OWN, WIDE), bf16),
            VMEM((SHARDS, OWN, HID), bf16),
            VMEM((SHARDS, OWN, HID), bf16),
            VMEM((SHARDS, OWN, HID), bf16),
            VMEM((SHARDS, OWN, WIDE), bf16),
            DMA((40,)),
            VMEM((SHARDS, OWN, WIDE), bf16),
            VMEM((OWN, WIDE), bf16),
            VMEM((SHARDS, OWN, WIDE), bf16),
            VMEM((SHARDS, OWN, HID), f32),
            VMEM((HID, WIDE), bf16),
            VMEM((HID, WIDE), bf16),
            VMEM((HID, WIDE), bf16),
            VMEM((32, WIDE), bf16),
        ]
        + reduce_scratch(WIDE)
        + [DMA((17,)), DMA((17,)), DMA((17,)), DMA((17,)), DMA((8,)), DMA((16,))],
        compiler_params=pltpu.CompilerParams(
            collective_id=1, has_side_effects=True, vmem_limit_bytes=60 * MIB
        ),
        cost_estimate=pl.CostEstimate(flops=16 * 10**9, bytes_accessed=3 * 10**7, transcendentals=10**6),
        name="hidden_ffn",
    )(p.reshape(SHARDS, OWN, WIDE), x, gain, grad, routes, sg, su, sd, eg, eu, ed, rt)


def rows_of(ref):
    return ref[...].reshape(LENGTH, ref.shape[-1])


BLOCKS = 9


QUARTER = 288


def turn_kernel(
    p_ref, hidden_ref, grad_ref, gain_ref, mixed_hbm, gall_hbm, m_hbm, da_hbm, db_hbm, sd, ed,
    hgrad_ref, hall_ref, sum_ref, router_ref, moe_hbm,
    mixed_ref, gall_ref, m_ref, da_ref, db_ref, half_ref, hs, pv, low, dw_scr, core_scr, moe_scr, wd_ref, zero_ref,
    got, *rest,
):
    bufs, (ss, rs, gs, gr, cs, cr, ys, yr, ls, ws, os) = rest[:11], rest[11:]
    n = neighbours()
    d = copies_of()
    ready = load_partials(n, p_ref, pv, ls)
    zero_ref[...] = jnp.zeros_like(zero_ref)
    loads = Copies(hs)
    copies = []
    entry_barrier(ring_peers(n), (d["core"], d["yp"], d["ym"]))
    stores = Copies(os)
    crossed = []
    sent = []
    theirs = pl.multiple_of((1 - d["c"]) * OWN, OWN)
    mine = pl.multiple_of(d["c"] * OWN, OWN)
    sums = [YSum(d, 48, half_ref, 384 * k, got.at[k], ys, yr, 6 * k) for k in range(3)]

    def product(index, left, right, block):
        k = index * 3 + block
        if block == 0:
            for c in {2: loads.made[:2], 0: loads.made[2:4], 1: loads.made[4:]}[index]:
                c.wait()
        left = left[:, :, pl.ds(block * 256, 256)].reshape(LENGTH, 256)
        dw_scr[k] = dot_tn(left, rows_of(right)).astype(bf16)
        c = dp_copy(dw_scr.at[k, pl.ds(theirs, OWN)], core_scr.at[k], cs.at[k], cr.at[k], d["core"])
        c.start()
        crossed.append((k, c))
        if k == 1:
            router_ref[...] = dw_scr[1, FS_OWN - 256 : FS_OWN - 240, :]

    def expert_sum(block):
        two = pl.ds(block * 2, 2)
        moe_scr[two] = dot(m_ref[two].reshape(256, HID), wd_ref[...]).astype(bf16).reshape(2, OWN, WIDE)
        stores.start(moe_scr.at[two], moe_hbm.at[two])

    def meet():
        k, c = crossed.pop(0)
        c.wait_recv()
        half_ref[pl.ds(k * OWN, OWN), :] = added(dw_scr[k, pl.ds(mine, OWN), :], core_scr[k])
        sent.append(c)

    jobs = [functools.partial(product, 2, m_ref, gall_ref, b) for b in range(3)]
    jobs += [functools.partial(product, 0, da_ref, mixed_ref, b) for b in range(3)]
    jobs += [functools.partial(product, 1, db_ref, mixed_ref, b) for b in range(3)]
    plan = {0: 3, 1: 2, 2: 2, 3: 1, 4: 1}

    def work(point):
        if point == 0:
            for src, dst in (
                (m_hbm, m_ref), (gall_hbm, gall_ref), (da_hbm, da_ref), (mixed_hbm, mixed_ref), (db_hbm, db_ref)
            ):
                loads.start(src, dst)
            copies.extend(fetch_hidden_weights(sd, ed, wd_ref, zero_ref, ws, 0))
        if point == 1:
            meet_all(2)
        for _ in range(plan[point]):
            jobs.pop(0)()
        if point == 2:
            while len(crossed) > 1:
                meet()
            sums[0].step(0)
        elif point == 3:
            sums[2].step(1)
        elif point == 4:
            meet_all(1)
            sums[0].step(1)

    def meet_all(part):
        while crossed:
            meet()
        sums[part].step(0)

    reduce_ring(n, pv, ready, bufs, ss, rs, work)
    total = own_total(n, pv, bufs)
    hidden = hidden_ref[...]
    inv = inverse_rms(hidden)
    unit = hidden * inv
    scaled = total * gain_ref[...].astype(f32)
    back = inv * (scaled - unit * jnp.mean(scaled * unit, axis=-1, keepdims=True))
    hgrad = grad_ref[...].astype(f32) + back
    hgrad_ref[...] = hgrad
    low[...] = hgrad.astype(bf16)
    for k, _ in enumerate(gather_steps(n, low, hall_ref, gs, gr)):
        if k == 0:
            stores.start(low, hall_ref.at[n["me"]])
            for c in copies:
                c.wait()
            expert_sum(0)
            expert_sum(1)
            sums[2].step(2)
            sums[1].step(1)
        elif k == 1:
            expert_sum(2)
            expert_sum(3)
            sums[0].step(2)
        elif k == 3:
            sums[1].step(2)
            sums[2].step(3)
        elif k == 5:
            sums[0].step(3)
    sums[1].step(3)
    for k in range(3):
        for way in range(2):
            sum_ref[pl.ds(k * 96 + way * 48, 48), :] = got[k, 2, way]
        sums[k].close()
    stores.close()
    for c in sent:
        c.wait_send()


def turn_back(p, hidden, grad, gain, mixed, gall, m, da, db, sd, ed):
    outs = (
        jax.ShapeDtypeStruct((OWN, WIDE), f32),
        jax.ShapeDtypeStruct((SHARDS, OWN, WIDE), bf16),
        jax.ShapeDtypeStruct((QUARTER, WIDE), bf16),
        jax.ShapeDtypeStruct((16, WIDE), bf16),
        jax.ShapeDtypeStruct((SHARDS, OWN, WIDE), bf16),
    )
    return pl.pallas_call(
        turn_kernel,
        out_shape=outs,
        in_specs=[anym()] + [vmem()] * 3 + [anym()] * 7,
        out_specs=[vmem(), anym(), vmem(), vmem(), anym()],
        scratch_shapes=[
            VMEM((SHARDS, OWN, WIDE), bf16),
            VMEM((SHARDS, OWN, WIDE), bf16),
            VMEM((SHARDS, OWN, HID), bf16),
            VMEM((SHARDS, OWN, HID), bf16),
            VMEM((SHARDS, OWN, HID), bf16),
            VMEM((BLOCKS * OWN, WIDE), bf16),
            DMA((5,)),
            VMEM((SHARDS, OWN, WIDE), bf16),
            VMEM((OWN, WIDE), bf16),
            VMEM((BLOCKS, 256, WIDE), bf16),
            VMEM((BLOCKS, OWN, WIDE), bf16),
            VMEM((SHARDS, OWN, WIDE), bf16),
            VMEM((HID, WIDE), bf16),
            VMEM((32, WIDE), bf16),
            VMEM((3, 3, 2, 48, WIDE), bf16),
        ]
        + reduce_scratch(WIDE)
        + [DMA((17,))] * 4
        + [DMA((BLOCKS,)), DMA((BLOCKS,)), DMA((18,)), DMA((18,)), DMA((8,)), DMA((5,)), DMA((5,))],
        compiler_params=pltpu.CompilerParams(
            collective_id=2, has_side_effects=True, vmem_limit_bytes=60 * MIB
        ),
        cost_estimate=pl.CostEstimate(flops=13 * 10**9, bytes_accessed=4 * 10**7, transcendentals=0),
        name="turn_back",
    )(p, hidden, grad, gain, mixed, gall, m, da, db, sd, ed)


LATE = 3072
PACK_COLS = 1280


def attend_back_kernel(
    prefix_ref, hall_hbm, wo_ref, q_ref, kvw_ref, kr_ref, lse_ref, ot_ref,
    kvup_ref, latent_hbm, lgain_ref, cos_ref, sin_ref, wq_hbm, kvd_hbm,
    normed_hbm, gain_ref, fgain_ref, gsum_ref, router_ref, ysum_ref,
    p_out, all_ref, jq_out, jk_out, kvg_out, tail_ref,
    hall_ref, latent_ref, wq_ref, normed_ref, p_ref, hs, os, do_scr, dk_scr, dv_scr, jq_scr, jk_scr, kvg_scr, kvd_ref, far_scr, quarter, ls, xs, xr, ys, yr,
):
    prefix = prefix_ref[0]
    d = copies_of()
    loads = Copies(hs)
    for i in range(4):
        loads.start(hall_hbm.at[pl.ds(i * KB, KB)], hall_ref.at[pl.ds(i * KB, KB)])
    for src, dst in ((latent_hbm, latent_ref), (wq_hbm, wq_ref), (normed_hbm, normed_ref)):
        loads.start(src, dst)
    stores = Copies(os)
    entry_barrier((), (d["xo"], d["yp"], d["ym"]))
    half = QUARTER // 2
    parts = [pl.ds(0, half), pl.ds(half, half)]
    crosses = [dp_copy(ysum_ref.at[r], far_scr.at[r], xs.at[k], xr.at[k], d["xo"]) for k, r in enumerate(parts)]
    for cross in crosses:
        cross.start()
    spread = []

    def meet(k):
        crosses[k].wait_recv()
        quarter[parts[k], :] = added(ysum_ref[parts[k], :], far_scr[parts[k], :])
        if k == 0:
            for i, peer in enumerate((d["yp"], d["ym"])):
                copy = dp_copy(quarter.at[parts[k]], all_ref.at[d["y"], parts[k]], ys.at[i], yr.at[i], peer)
                copy.start()
                spread.append(copy)
        stores.start(quarter.at[parts[k]], all_ref.at[d["y"], parts[k]])

    copies = fetch_latent_weights(kvd_hbm, kvd_ref, ls)
    for i in range(4):
        rows = pl.ds(i * KB, KB)
        loads.made[i].wait()
        do_scr[rows, :] = dot_nt(hall_ref[rows, :], wo_ref[...]).astype(bf16)
    dk_scr[...] = jnp.zeros_like(dk_scr)
    dv_scr[...] = jnp.zeros_like(dv_scr)
    for i in range(4):
        rows = pl.ds(i * KB, KB)
        plain = []
        turned = jnp.zeros((KB, 128), f32)
        for h in range(2):
            q = head_query(q_ref, rows, h)
            do = do_scr[rows, h * 128 : h * 128 + 128]
            lse = lse_ref[h : h + 1, rows]
            delta = jnp.sum(do.astype(f32).T * ot_ref[h, :, rows], axis=0, keepdims=True)
            dq = jnp.zeros((KB, 256), f32)
            for k in range(key_extent(i)):
                keys = pl.ds(k * KB, KB)
                key = head_key(kvw_ref, kr_ref, keys, h)
                s = dot_nt(key, q)
                if k >= i:
                    s = masked(s, k * KB, i * KB, prefix)
                p = jnp.exp2(s * (SCALE * LOG2E) - lse)
                dp = dot_nt(kvw_ref[keys, h * 256 + 128 : h * 256 + 256], do)
                ds = (p * (dp - delta)).astype(bf16)
                dv_scr[h, keys, :] += dot(p.astype(bf16), do)
                dk_scr[h, keys, :] += dot(ds, q)
                dq = dq + dot_tn(ds, key)
            dq = dq * SCALE
            plain.append(dq[:, :128])
            turned = turned + jnp.where(head_lanes(turned.shape, h), dq[:, 128:], 0.0)
        turned = turn(turned, cos_ref[rows, :], -sin_ref[rows, :])
        j = jnp.concatenate([plain[0], turned[:, :64], plain[1], turned[:, 64:]], axis=1)
        jq_scr[rows, :] = j.astype(bf16)
    meet(0)
    for c in copies + loads.made[4:]:
        c.wait()
    gain_sum = jnp.zeros((1, WIDE), f32)
    lgain_sum = jnp.zeros((1, KVR), f32)
    for i in range(4):
        rows = pl.ds(i * KB, KB)
        for h in range(2):
            kvg_scr[rows, h * 256 : h * 256 + 128] = (dk_scr[h, rows, :128] * SCALE).astype(bf16)
            kvg_scr[rows, h * 256 + 128 : h * 256 + 256] = dv_scr[h, rows, :].astype(bf16)
        dkr = (dk_scr[0, rows, 128:] + dk_scr[1, rows, 128:]) * SCALE
        jk_scr[rows, KVR:] = turn(dkr, cos_ref[rows, :], -sin_ref[rows, :]).astype(bf16)
        dl = dot_nt(kvg_scr[rows, :], kvup_ref[...])
        latent = latent_ref[rows, :]
        inv = inverse_rms(latent)
        unit = latent * inv
        lgain_sum = lgain_sum + jnp.sum(dl * unit, axis=0, keepdims=True)
        scaled = dl * lgain_ref[...].astype(f32)
        back = inv * (scaled - unit * jnp.mean(scaled * unit, axis=-1, keepdims=True))
        jk_scr[rows, :KVR] = back.astype(bf16)
        into = dot_nt(jq_scr[rows, :], wq_ref[...]) + dot(jk_scr[rows, :], kvd_ref[...])
        gain_sum = gain_sum + jnp.sum(into * normed_ref[rows, :].astype(f32), axis=0, keepdims=True)
        into = into.astype(bf16)
        for t in range(2):
            p_ref[i * 2 + t] = into[t * OWN : t * OWN + OWN]
        stores.start(p_ref.at[pl.ds(i * 2, 2)], p_out.at[pl.ds(i * 2, 2)])
        for src, dst in ((jq_scr, jq_out), (jk_scr, jk_out), (kvg_scr, kvg_out)):
            stores.start(src.at[rows], dst.at[rows])
    empty = jnp.zeros((1, 192), f32)
    lat = jnp.concatenate([v for t in range(SHARDS) for v in (lgain_sum[:, t * 64 : t * 64 + 64], empty)], axis=1)
    tail_ref[...] = jnp.concatenate(
        [
            gain_sum / gain_ref[...].astype(f32),
            gsum_ref[...] / fgain_ref[...].astype(f32),
            router_ref[:2, :].astype(f32),
            lat,
            jnp.zeros((3, WIDE), f32),
        ],
        axis=0,
    )
    meet(1)
    for copy in spread:
        copy.wait()
    for cross in crosses:
        cross.wait_send()
    stores.close()


def attend_back(*args):
    return pl.pallas_call(
        attend_back_kernel,
        out_shape=(
            jax.ShapeDtypeStruct((SHARDS, OWN, WIDE), bf16),
            jax.ShapeDtypeStruct((4, QUARTER, WIDE), bf16),
            jax.ShapeDtypeStruct((LENGTH, QCOLS), bf16),
            jax.ShapeDtypeStruct((LENGTH, LATENT_ROWS), bf16),
            jax.ShapeDtypeStruct((LENGTH, 512), bf16),
            jax.ShapeDtypeStruct((8, WIDE), f32),
        ),
        in_specs=[pl.BlockSpec(memory_space=pltpu.SMEM), anym()]
        + [vmem()] * 7
        + [anym()]
        + [vmem()] * 3
        + [anym()] * 3
        + [vmem()] * 5,
        out_specs=[anym()] * 5 + [vmem()],
        scratch_shapes=[
            VMEM((LENGTH, WIDE), bf16),
            VMEM((LENGTH, KVR), f32),
            VMEM((WIDE, QCOLS), bf16),
            VMEM((LENGTH, WIDE), bf16),
            VMEM((SHARDS, OWN, WIDE), bf16),
            DMA((8,)),
            DMA((18,)),
            VMEM((LENGTH, 256), bf16),
            VMEM((2, LENGTH, 256), f32),
            VMEM((2, LENGTH, DV), f32),
            VMEM((LENGTH, QCOLS), bf16),
            VMEM((LENGTH, LATENT_ROWS), bf16),
            VMEM((LENGTH, 512), bf16),
            VMEM((LATENT_ROWS, WIDE), bf16),
            VMEM((QUARTER, WIDE), bf16),
            VMEM((QUARTER, WIDE), bf16),
            DMA((2,)),
            DMA((2,)),
            DMA((2,)),
            DMA((2,)),
            DMA((2,)),
        ],
        compiler_params=pltpu.CompilerParams(
            collective_id=4, has_side_effects=True, vmem_limit_bytes=60 * MIB
        ),
        cost_estimate=pl.CostEstimate(flops=18 * 10**9, bytes_accessed=4 * 10**7, transcendentals=2 * 10**6),
        name="attend_back",
    )(*args)


LATE_HALF = LATE // 2
LATE_PIECE = LATE_HALF // 8


def half_pieces(y, all_ref, second_ref, opposite_ref):
    half = QUARTER // 2
    below, above = lax.rem(y + 3, 4), lax.rem(y + 1, 4)

    def view(ref, lead, offset=0):
        return lambda start, count: ref.at[lead, pl.ds(start - offset, count)]

    return (
        (view(all_ref, y), y, 0, QUARTER),
        (view(all_ref, below), below, 0, half),
        (view(all_ref, above), above, 0, half),
        (view(second_ref, 0, half), below, half, half),
        (view(second_ref, 1, half), above, half, half),
        (lambda start, count: opposite_ref.at[pl.ds(start, count)], lax.rem(y + 2, 4), 0, QUARTER),
    )


def last_kernel(
    p_ref, x_ref, hgrad_ref, gain_ref, tail_ref, hidden_ref, all_ref, moe_ref,
    normed_hbm, hall_hbm, jq_hbm, jk_hbm, kvg_hbm, attn_hbm, lnorm_hbm,
    out_ref, moved_ref, second_ref, opposite_ref, other, lall, packs,
    normed_ref, hall_ref, jq_ref, jk_ref, kvg_ref, attn_ref, lnorm_ref, hs,
    pv, pack_pv, moe_pv, pack, late, core_scr, half, got, near, far,
    pack_core, by_y, pack_near, pack_far, *rest,
):
    bufs, pack_bufs, moe_bufs = rest[:11], rest[11:22], rest[22:33]
    ss, rs, ps, pr, ms, mr, ys, yr, xs, xr, gs, gr, cs, cr, zs, zr, ls, mls = rest[33:]
    n = neighbours()
    d = copies_of()
    c, y = d["c"], d["y"]
    ready = load_partials(n, p_ref, pv, ls)
    loads = Copies(hs)
    theirs = pl.ds(pl.multiple_of((1 - c) * LATE_HALF, OWN), LATE_HALF)
    mine = pl.ds(pl.multiple_of(c * LATE_HALF, OWN), LATE_HALF)
    pack_theirs = pl.ds(pl.multiple_of((1 - c) * 64, 64), 64)
    pack_mine = pl.ds(pl.multiple_of(c * 64, 64), 64)
    entry_barrier(ring_peers(n), (d["core"], d["yp"], d["ym"], d["y2"], d["xo"]))
    first = dp_copy(late.at[theirs], core_scr, cs.at[0], cr.at[0], d["core"])
    cross = dp_copy(near, far, xs.at[0], xr.at[0], d["xo"])
    rows0, rows1 = pl.ds(0, QUARTER // 2), pl.ds(QUARTER // 2, QUARTER // 2)
    below = lax.rem(y + 3, 4)
    spread = [
        dp_copy(all_ref.at[y, rows1], second_ref.at[0], gs.at[0], gr.at[0], d["yp"]),
        dp_copy(all_ref.at[y, rows1], second_ref.at[1], gs.at[1], gr.at[1], d["ym"]),
    ]
    onward = [
        dp_copy(all_ref.at[below, rows0], opposite_ref.at[rows0], gs.at[2], gr.at[2], d["yp"]),
        dp_copy(second_ref.at[1], opposite_ref.at[rows1], gs.at[3], gr.at[3], d["ym"]),
    ]
    ring = reduce_steps(n, pv, ready, bufs, ss, rs)
    next(ring)
    for src, dst in (
        (jk_hbm, jk_ref), (normed_hbm, normed_ref), (jq_hbm, jq_ref), (lnorm_hbm, lnorm_ref), (kvg_hbm, kvg_ref),
        (attn_hbm, attn_ref), (hall_hbm, hall_ref),
    ):
        loads.start(src, dst)
    moe_ready = load_partials(n, moe_ref, moe_pv, mls)
    for copy in spread:
        copy.start()
    for copy in loads.made[:2]:
        copy.wait()
    blank = jnp.zeros((56, KB), f32)
    for i in range(8):
        cols = pl.ds(i * KB, KB)
        down = dot_tn(jk_ref[...], normed_ref[:, cols])
        for k in range(4):
            pack_pv[i, :, k * KB : k * KB + KB] = down[k * OWN : k * OWN + OWN].astype(bf16)
        rope = down[KVR : KVR + DR] + down[KVR + DR :]
        end = jnp.concatenate([rope, tail_ref[:, i * KB : i * KB + KB], blank], axis=0)
        pack_pv[i, :, 4 * KB :] = end.astype(bf16)
    pack_ring = reduce_steps(n, pack_pv, lambda name: None, pack_bufs, ps, pr)
    next(pack_ring)
    next(ring)
    for copy in loads.made[2:]:
        copy.wait()
    late[pl.ds(1536, KVR), :] = dot_tn(lnorm_ref[...], kvg_ref[...]).astype(bf16)
    for i in range(4):
        cols = pl.ds(i * 512, 512)
        late[pl.ds(2048 + i * 256, 256), :] = dot_tn(attn_ref[...], hall_ref[:, cols]).astype(bf16)
        query = dot_tn(normed_ref[:, cols], jq_ref[...]).astype(bf16)
        for k in range(3):
            late[pl.ds(k * 512, 512), i * 128 : i * 128 + 128] = query[:, k * 128 : k * 128 + 128]
    first.start()
    next(ring)
    first.wait_recv()
    half[...] = added(late[mine, :], core_scr[...])
    deal = y_deal(d, half, 2 * LATE_PIECE, got, ys, yr, 0)
    for copy in deal:
        copy.start()
    next(ring)
    next(pack_ring)
    next(ring)
    next(pack_ring)
    next(pack_ring)
    next(pack_ring)
    for copy in deal:
        copy.wait_recv()
    own_rows = pl.ds(pl.multiple_of(y * (2 * LATE_PIECE), 16), 2 * LATE_PIECE)
    total = half[own_rows, :].astype(f32)
    for hops in (1, 2, 3):
        total = total + got[lax.rem(y + hops, 4)].astype(f32)
    near[...] = total.astype(bf16)
    cross.start()
    for copy in spread:
        copy.wait_recv()
    for copy in onward:
        copy.start()
    moe_ring = reduce_steps(n, moe_pv, moe_ready, moe_bufs, ms, mr)
    next(moe_ring)
    next(ring, None)
    total = own_total(n, pv, bufs)
    x = x_ref[...].astype(f32)
    inv = inverse_rms(x)
    unit = x * inv
    scaled = total * gain_ref[...].astype(f32)
    back = inv * (scaled - unit * jnp.mean(scaled * unit, axis=-1, keepdims=True))
    out_ref[...] = (hgrad_ref[...] + back).astype(bf16)
    next(pack_ring, None)
    pack[...] = own_total(n, pack_pv, pack_bufs).astype(bf16)
    pack_first = dp_copy(pack.at[pack_theirs], pack_core, cs.at[1], cr.at[1], d["core"])
    pack_first.start()
    cross.wait_recv()
    lall[c, y] = added(near[...], far[...])
    pack_first.wait_recv()
    by_y[y] = added(pack[pack_mine, :], pack_core[...])
    pack_spread = y_spread(d, by_y, gs, gr, 4)
    for copy in pack_spread:
        copy.start()
    ygather = YGather(d, LATE_PIECE, lall.at[c], zs, zr)
    ygather.step(0)
    next(moe_ring)
    for copy in onward:
        copy.wait_recv()
    swaps = []
    for i, (view, slot, start, count) in enumerate(half_pieces(y, all_ref, second_ref, opposite_ref)):
        rows = pl.ds(start, count)
        swaps.append(dp_copy(view(start, count), other.at[slot, rows], cs.at[4 + i], cr.at[4 + i], d["core"]))
        swaps[-1].start()
    for copy in pack_spread:
        copy.wait_recv()
    total = by_y[0].astype(f32) + by_y[1].astype(f32) + by_y[2].astype(f32) + by_y[3].astype(f32)
    pack_near[...] = total.astype(bf16)
    pack_cross = dp_copy(pack_near, pack_far, xs.at[1], xr.at[1], d["xo"])
    pack_cross.start()
    next(moe_ring)
    next(moe_ring)
    next(moe_ring)
    ygather.step(1)
    pack_cross.wait_recv()
    packs[c] = added(pack_near[...], pack_far[...])
    pack_back = dp_copy(packs.at[c], packs.at[c], cs.at[3], cr.at[3], d["core"])
    pack_back.start()
    ygather.step(2)
    late_back = dp_copy(lall.at[c], lall.at[c], cs.at[2], cr.at[2], d["core"])
    late_back.start()
    next(moe_ring, None)
    moved_ref[...] = (hidden_ref[...] + own_total(n, moe_pv, moe_bufs)).astype(bf16)
    for copy in (pack_back, late_back, *swaps):
        copy.wait_recv()
    for copy in (first, cross, pack_first, pack_cross, pack_back, late_back):
        copy.wait_send()
    for copy in (*spread, *onward, *deal, *pack_spread, *ygather.all, *swaps):
        copy.wait_send()


def last(p, x, hgrad, gain, tail, hidden, quarters, moe, normed, hall, jq, jk, kvg, attn, lnorm):
    return pl.pallas_call(
        last_kernel,
        out_shape=(
            jax.ShapeDtypeStruct((OWN, WIDE), bf16),
            jax.ShapeDtypeStruct((OWN, WIDE), bf16),
            jax.ShapeDtypeStruct((2, QUARTER // 2, WIDE), bf16),
            jax.ShapeDtypeStruct((QUARTER, WIDE), bf16),
            jax.ShapeDtypeStruct((4, QUARTER, WIDE), bf16),
            jax.ShapeDtypeStruct((2, 4, 2 * LATE_PIECE, 512), bf16),
            jax.ShapeDtypeStruct((2, 64, PACK_COLS), bf16),
        ),
        in_specs=[anym()] + [vmem()] * 5 + [anym()] * 9,
        out_specs=[vmem(), vmem(), anym(), anym(), anym(), vmem(), vmem()],
        scratch_shapes=[
            VMEM((LENGTH, WIDE), bf16),
            VMEM((LENGTH, WIDE), bf16),
            VMEM((LENGTH, QCOLS), bf16),
            VMEM((LENGTH, LATENT_ROWS), bf16),
            VMEM((LENGTH, 512), bf16),
            VMEM((LENGTH, 256), bf16),
            VMEM((LENGTH, KVR), bf16),
            DMA((7,)),
            VMEM((SHARDS, OWN, WIDE), bf16),
            VMEM((SHARDS, OWN, PACK_COLS), bf16),
            VMEM((SHARDS, OWN, WIDE), bf16),
            VMEM((OWN, PACK_COLS), bf16),
            VMEM((LATE, 512), bf16),
            VMEM((LATE_HALF, 512), bf16),
            VMEM((LATE_HALF, 512), bf16),
            VMEM((4, 2 * LATE_PIECE, 512), bf16),
            VMEM((2 * LATE_PIECE, 512), bf16),
            VMEM((2 * LATE_PIECE, 512), bf16),
            VMEM((64, PACK_COLS), bf16),
            VMEM((4, 64, PACK_COLS), bf16),
            VMEM((64, PACK_COLS), bf16),
            VMEM((64, PACK_COLS), bf16),
        ]
        + reduce_scratch(WIDE)
        + reduce_scratch(PACK_COLS)
        + reduce_scratch(WIDE)
        + [DMA((17,))] * 6
        + [DMA((3,)), DMA((3,)), DMA((2,)), DMA((2,)), DMA((7,)), DMA((7,)), DMA((10,)), DMA((10,))]
        + [DMA((4,)), DMA((4,)), DMA((8,)), DMA((8,))],
        compiler_params=pltpu.CompilerParams(
            collective_id=5, has_side_effects=True, vmem_limit_bytes=60 * MIB
        ),
        cost_estimate=pl.CostEstimate(flops=6 * 10**9, bytes_accessed=2 * 10**7, transcendentals=0),
        name="last",
    )(p, x, hgrad, gain, tail, hidden, quarters, moe, normed, hall, jq, jk, kvg, attn, lnorm)


def widen_kernel(
    own_hbm, second_hbm, opposite_hbm, other_hbm, lall_hbm, pack_ref,
    q_ref, kv_ref, o_ref, down_ref, again_ref, fgain_ref, router_ref, lgain_ref, sg, su, sd, eg, eu, ed,
    wide, full_ref, lall_ref, os, hs,
):
    stores = []
    loads = Copies(hs)
    d = copies_of()
    c, y = d["c"], d["y"]

    def place(view, slot, start, count, core):
        for k in range(3):
            low, high = max(start, 96 * k), min(start + count, 96 * k + 96)
            if low < high:
                at = pl.multiple_of(384 * k + 96 * slot + (low - 96 * k), 16)
                loads.start(view(low, high - low), full_ref.at[core, pl.ds(at, high - low)])

    for view, slot, start, count in half_pieces(y, own_hbm, second_hbm, opposite_hbm):
        place(view, slot, start, count, c)
    for slot in range(4):
        place(lambda start, count, slot=slot: other_hbm.at[slot, pl.ds(start, count)], slot, 0, QUARTER, 1 - c)
    loads.start(lall_hbm, lall_ref)

    def put(start, count, dst):
        copy = pltpu.make_async_copy(wide.at[pl.ds(start, count)], dst, os.at[len(stores)])
        copy.start()
        stores.append(copy)

    for index, (shared, experts) in enumerate(((sg, eg), (su, eu), (sd, ed))):
        base = index * HID
        if index == 0:
            for copy in loads.made[:-1]:
                copy.wait()
        for k in range(index * 3, index * 3 + 3):
            for core in range(2):
                wide[pl.ds(k * 256 + core * OWN, OWN), :] = full_ref[core, pl.ds(k * OWN, OWN), :].astype(f32)
        put(base, FS_OWN, shared)
        put(base + 384, FE_OWN, experts.at[0])
        put(base + 384 + FE_OWN, FE_OWN, experts.at[1])
    loads.made[-1].wait()
    for k in range(3):
        for i in range(4):
            block = lall_ref[0, pl.ds(k * 512, 512), i * 128 : i * 128 + 128]
            q_ref[pl.ds(i * 512, 512), k * 128 : k * 128 + 128] = block.astype(f32)
    kv_ref[...] = lall_ref[1, pl.ds(0, KVR), :].astype(f32)
    for i in range(4):
        o_ref[:, i * 512 : i * 512 + 512] = lall_ref[1, pl.ds(512 + i * 256, 256), :].astype(f32)
    for j in range(4):
        down_ref[pl.ds(j * OWN, OWN), :] = pack_ref[:, j * KB : j * KB + KB].astype(f32)
    down_ref[pl.ds(KVR, DR), :] = pack_ref[:DR, 4 * KB :].astype(f32)
    tail = pack_ref[DR : DR + 16, 4 * KB :].astype(f32)
    again_ref[...] = tail[0:1]
    fgain_ref[...] = tail[1:2]
    router_ref[...] = tail[2:4]
    lgain_ref[...] = tail[4:5, :64]
    for copy in stores:
        copy.wait()


def widen(own, second, opposite, other, lall, packs):
    def out(*shape):
        return jax.ShapeDtypeStruct(shape, f32)

    shared, experts = out(FS_OWN, WIDE), out(2, FE_OWN, WIDE)
    return pl.pallas_call(
        widen_kernel,
        out_shape=(
            out(WIDE, QCOLS), out(KVR, 512), out(256, WIDE), out(576, 256),
            out(1, 256), out(1, 256), out(2, 256), out(1, 64), shared, shared, shared, experts, experts, experts,
        ),
        in_specs=[anym()] * 5 + [vmem()],
        out_specs=[vmem()] * 8 + [anym()] * 6,
        scratch_shapes=[
            VMEM((3 * HID, WIDE), f32),
            VMEM((2, BLOCKS * OWN, WIDE), bf16),
            VMEM((2, LATE_HALF, 512), bf16),
            DMA((9,)),
            DMA((27,)),
        ],
        compiler_params=pltpu.CompilerParams(vmem_limit_bytes=60 * MIB),
        cost_estimate=pl.CostEstimate(flops=10**7, bytes_accessed=4 * 10**7, transcendentals=0),
        name="widen",
    )(own, second, opposite, other, lall.reshape(2, LATE_HALF, 512), packs.reshape(OWN, PACK_COLS))


def rope_tables():
    half = DR // 2
    frequency = ROPE_BASE ** (-(np.arange(half, dtype=np.float64) * 2.0) / DR)
    angles = np.arange(LENGTH, dtype=np.float64)[:, None] * frequency[None, :]
    cos = np.cos(angles).astype(np.float32)
    sin = np.sin(angles).astype(np.float32)
    return np.concatenate([cos] * 4, axis=1), np.concatenate([-sin, sin, -sin, sin], axis=1)


def after(value, *others):
    return lax.optimization_barrier((value, *others))[0]


def flat(v):
    return v.reshape(LENGTH, v.shape[-1])


def body(
    layer_in, grad_out, routes, prefix, attn_gain, query_proj, kv_down, latent_gain, kv_up,
    out_proj, ffn_gain, router_proj, shared_gate, shared_up, shared_down, expert_gate, expert_up, expert_down,
):
    cos_np, sin_np = rope_tables()
    cos, sin = jnp.asarray(cos_np), jnp.asarray(sin_np)
    again, lgain, fgain = attn_gain[None], latent_gain[None], ffn_gain[None]
    kvd = kv_down.T
    sg, su = shared_gate.T, shared_up.T
    eg, eu = jnp.swapaxes(expert_gate, 1, 2), jnp.swapaxes(expert_up, 1, 2)
    rt = router_proj.T

    *projected, grad_all = project(layer_in, grad_out, again, query_proj, kvd, lgain, kv_up, cos, sin)
    normed, q, kvw, kr, lnorm, latent = map(flat, projected)
    attn, lse, ot, p1 = attend(prefix, q, kvw, kr, out_proj)
    hidden, mixed, m, da, db, p2, gsum = hidden_ffn(
        p1, layer_in, fgain, grad_all, routes.reshape(SHARDS, OWN),
        sg, su, shared_down, eg, eu, expert_down, rt,
    )
    hgrad, hall, ysum, router_rows, moe = turn_back(
        p2, hidden, grad_out, fgain, mixed, grad_all, m, da, db, shared_down, expert_down
    )
    hall = flat(hall)
    p3, quarters, jq, jk, kvg, tail = attend_back(
        prefix, hall, out_proj, q, kvw, kr, lse, ot, kv_up, latent, lgain, cos, sin, query_proj, kvd,
        normed, again, fgain, gsum, router_rows, ysum,
    )
    input_grad, layer_out, second, opposite, other, lall, packs = last(
        p3, layer_in, hgrad, again, tail, hidden, quarters, moe, normed, hall, jq, jk, kvg, attn, lnorm
    )
    dq, dkv, do, ddown, dag, dfg, drouter, dlg, dsg, dsu, dsd, deg, deu, ded = widen(
        quarters, second, opposite, other, lall, packs
    )
    return (
        layer_out,
        input_grad,
        dag.reshape(256),
        dq,
        ddown.T,
        dlg.reshape(64),
        dkv,
        do,
        dfg.reshape(256),
        drouter.T,
        dsg.T,
        dsu.T,
        dsd,
        jnp.swapaxes(deg, 1, 2),
        jnp.swapaxes(deu, 1, 2),
        ded,
    )


def solution(mesh):
    placed = (
        P(("dp", "tensor"), None),
        P(("dp", "tensor"), None),
        P("dp", None),
        P("dp"),
        P(),
        P(None, "tensor"),
        P(),
        P(),
        P(None, "tensor"),
        P("tensor", None),
        P(),
        P(),
        P(None, "tensor"),
        P(None, "tensor"),
        P("tensor", None),
        P(None, None, "tensor"),
        P(None, None, "tensor"),
        P(None, "tensor", None),
    )
    return jax.shard_map(
        body,
        mesh=mesh,
        in_specs=placed,
        out_specs=(
            P(("dp", "tensor"), None),
            P(("dp", "tensor"), None),
            P("tensor"),
            P(None, "tensor"),
            P("tensor", None),
            P("tensor"),
            P(None, "tensor"),
            P("tensor", None),
            P("tensor"),
            P("tensor", None),
            P(None, "tensor"),
            P(None, "tensor"),
            P("tensor", None),
            P(None, None, "tensor"),
            P(None, None, "tensor"),
            P(None, "tensor", None),
        ),
        check_vma=False,
    )
```

```python
import functools

import jax
import jax.numpy as jnp
import numpy as np
from jax import lax
from jax.experimental import pallas as pl
from jax.experimental.pallas import tpu as pltpu
from jax.sharding import PartitionSpec as P

DN = 128
DR = 64
DV = 128
KVR = 512
EPS = 1e-06
ROPE_BASE = 10000.0
LOG2E = 1.4426950408889634
SCALE = (DN + DR) ** (-0.5)
NEG = -1e30
MIB = 2**20
MESH = pl.DeviceIdType.MESH
f32 = jnp.float32
bf16 = jnp.bfloat16
VMEM = pltpu.VMEM
DMA = pltpu.SemaphoreType.DMA

OWN = 128
SHARDS = 8
LENGTH = OWN * SHARDS
WIDE = 2048
FS_OWN = 352
FE_OWN = 176
HID = 768
QCOLS = 384
LATENT_ROWS = 640


def vmem():
    return pl.BlockSpec(memory_space=pltpu.VMEM)


def anym():
    return pl.BlockSpec(memory_space=pltpu.HBM)


def row(ref):
    v = ref[...].astype(f32)
    return jnp.concatenate([v[i : i + 1] for i in range(v.shape[0])], axis=1)


def dot(a, b):
    return jnp.dot(a, b, preferred_element_type=f32)


def dot_nt(a, b):
    return lax.dot_general(a, b, (((1,), (1,)), ((), ())), preferred_element_type=f32)


def dot_tn(a, b):
    return lax.dot_general(a, b, (((0,), (0,)), ((), ())), preferred_element_type=f32)


def neighbours():
    t = lax.axis_index("tensor")
    x = t // 4
    z = t % 4
    zp = lax.rem(z + 1, 4)
    zm = lax.rem(z + 3, 4)
    z2 = lax.rem(z + 2, 4)
    own = x * 4
    far = (1 - x) * 4
    return dict(
        me=t, tp=own + zp, tm=own + zm, t2=own + z2, tx=far + z, xp=far + zp, xm=far + zm, x2=far + z2
    )


def copies_of():
    d = lax.axis_index("dp")
    c = lax.rem(d, 2)
    y = lax.rem(d // 2, 4)
    plane = d // 8
    here = plane * 8 + c
    return dict(
        c=c, y=y, core=d + 1 - 2 * c, y2=here + lax.rem(y + 2, 4) * 2, yp=here + lax.rem(y + 1, 4) * 2, ym=here + lax.rem(y + 3, 4) * 2,
        xo=(1 - plane) * 8 + y * 2 + c,
    )


def entry_barrier(tensor=(), dp=()):
    sem = pltpu.get_barrier_semaphore()
    for peer in tensor:
        pl.semaphore_signal(sem, inc=1, device_id={"tensor": peer}, device_id_type=MESH)
    for peer in dp:
        pl.semaphore_signal(sem, inc=1, device_id={"dp": peer}, device_id_type=MESH)
    pl.semaphore_wait(sem, len(tensor) + len(dp))


def ring_peers(n):
    return (n["tp"], n["tm"], n["tx"])


class YSum:
    def __init__(self, d, rows, a_ref, base, got, ss, rs, sem):
        self.d, self.rows, self.a, self.base, self.got = d, rows, a_ref, base, got
        self.ss, self.rs, self.sem = ss, rs, sem
        self.pending = None
        self.all = []

    def piece(self, way, hops):
        owner = lax.rem(self.d["y"] + ((3 - hops) if way == 0 else (1 + hops)) + 4, 4)
        start = pl.multiple_of(self.base + (owner * 2 + way) * self.rows, 16)
        return pl.ds(start, self.rows)

    def step(self, s):
        if s:
            for c in self.pending:
                c.wait_recv()
            for way in range(2):
                here = self.piece(way, s)
                self.got[s - 1, way] = added(self.got[s - 1, way], self.a[here, :])
        if s == 3:
            return
        self.pending = []
        for way in range(2):
            src = self.a.at[self.piece(way, 0)] if s == 0 else self.got.at[s - 1, way]
            c = pltpu.make_async_remote_copy(
                src_ref=src,
                dst_ref=self.got.at[s, way],
                send_sem=self.ss.at[self.sem + s * 2 + way],
                recv_sem=self.rs.at[self.sem + s * 2 + way],
                device_id={"dp": self.d["yp"] if way == 0 else self.d["ym"]},
                device_id_type=MESH,
            )
            c.start()
            self.pending.append(c)
            self.all.append(c)

    def close(self):
        for c in self.all:
            c.wait_send()


class YGather:
    def __init__(self, d, rows, g_ref, ss, rs):
        self.d, self.rows, self.g, self.ss, self.rs = d, rows, g_ref, ss, rs
        self.all = []

    def send(self, i, slot, start, count, way):
        view = self.g.at[slot, pl.ds(start, count)]
        copy = dp_copy(view, view, self.ss.at[i], self.rs.at[i], self.d["yp"] if way == 0 else self.d["ym"])
        copy.start()
        self.all.append(copy)

    def step(self, s):
        y = self.d["y"]
        if s == 0:
            self.send(0, y, 0, 2 * self.rows, 0)
            self.send(1, y, 0, 2 * self.rows, 1)
        elif s == 1:
            self.all[0].wait_recv()
            self.send(2, lax.rem(y + 3, 4), 0, self.rows, 0)
            self.all[1].wait_recv()
            self.send(3, lax.rem(y + 1, 4), self.rows, self.rows, 1)
        else:
            self.all[2].wait_recv()
            self.all[3].wait_recv()


def y_spread(d, ref, ss, rs, sem):
    mine = ref.at[d["y"]]
    return [
        dp_copy(mine, mine, ss.at[sem + i], rs.at[sem + i], d[peer]) for i, peer in enumerate(("y2", "yp", "ym"))
    ]


def y_deal(d, ref, rows, got, ss, rs, sem):
    y = d["y"]
    copies = []
    for i, (hops, peer) in enumerate(((2, "y2"), (1, "yp"), (3, "ym"))):
        start = pl.multiple_of(lax.rem(y + hops, 4) * rows, 16)
        src = ref.at[pl.ds(start, rows)]
        copies.append(dp_copy(src, got.at[y], ss.at[sem + i], rs.at[sem + i], d[peer]))
    return copies


def dp_copy(src, dst, ss, rs, peer):
    return pltpu.make_async_remote_copy(
        src_ref=src, dst_ref=dst, send_sem=ss, recv_sem=rs, device_id={"dp": peer}, device_id_type=MESH
    )


def sender(ss, rs):
    def send(i, src, dst, dev):
        return pltpu.make_async_remote_copy(
            src_ref=src,
            dst_ref=dst,
            send_sem=ss.at[i],
            recv_sem=rs.at[i],
            device_id={"tensor": dev},
            device_id_type=MESH,
        )

    return send


def gather_steps(n, x_ref, o_ref, ss, rs):
    send = sender(ss, rs)

    def s(i, src, slot, o, k, dev):
        return send(i, src, o_ref.at[slot, pl.ds(o, k)], dev)

    def part(slot, o, k):
        return o_ref.at[slot, pl.ds(o, k)]

    me, tp, tm, tx, t2, xp, xm, x2 = (n[k] for k in ("me", "tp", "tm", "tx", "t2", "xp", "xm", "x2"))
    s1a = s(0, x_ref.at[pl.ds(0, 64)], me, 0, 64, tp)
    s2a = s(1, x_ref.at[pl.ds(64, 64)], me, 64, 64, tm)
    s3 = s(2, x_ref, me, 0, 128, tx)
    s1b = s(11, x_ref.at[pl.ds(64, 64)], me, 64, 64, tp)
    s2b = s(12, x_ref.at[pl.ds(0, 64)], me, 0, 64, tm)
    for c in (s1a, s2a, s3, s1b, s2b):
        c.start()
    yield me
    s1a.wait_recv()
    s4 = s(3, part(tm, 0, 64), tm, 0, 64, tp)
    s6a = s(5, part(tm, 0, 64), tm, 0, 64, tx)
    s4.start()
    s6a.start()
    s2a.wait_recv()
    s5 = s(4, part(tp, 64, 64), tp, 64, 64, tm)
    s7a = s(6, part(tp, 64, 64), tp, 64, 64, tx)
    s5.start()
    s7a.start()
    s3.wait_recv()
    s8 = s(7, part(tx, 80, 48), tx, 80, 48, tp)
    s9 = s(8, part(tx, 0, 48), tx, 0, 48, tm)
    s8.start()
    s9.start()
    s1b.wait_recv()
    s6b = s(13, part(tm, 64, 16), tm, 64, 16, tx)
    s6b.start()
    s2b.wait_recv()
    s7b = s(14, part(tp, 48, 16), tp, 48, 16, tx)
    s7b.start()
    yield tm
    s6a.wait_recv()
    s10 = s(9, part(xm, 0, 64), xm, 0, 64, tp)
    s10.start()
    s7a.wait_recv()
    s11 = s(10, part(xp, 64, 64), xp, 64, 64, tm)
    s11.start()
    yield tp
    yield tx
    s4.wait_recv()
    s5.wait_recv()
    yield t2
    s8.wait_recv()
    s6b.wait_recv()
    yield xm
    s9.wait_recv()
    s7b.wait_recv()
    yield xp
    s10.wait_recv()
    s11.wait_recv()
    yield x2
    for c in (s1a, s1b, s2a, s2b, s3, s4, s5, s6a, s6b, s7a, s7b, s8, s9, s10, s11):
        c.wait_send()


def gather_ring(n, x_ref, o_ref, ss, rs, on_shard=None):
    for slot in gather_steps(n, x_ref, o_ref, ss, rs):
        if on_shard:
            on_shard(slot)


def reduce_steps(n, pv, ready, bufs, ss, rs):
    send = sender(ss, rs)
    me, tp, tm, tx, t2, xp, xm, x2 = (n[k] for k in ("me", "tp", "tm", "tx", "t2", "xp", "xm", "x2"))
    r10, r11, r8, r9, r6, r7, r4, r5, m1, m2, m3 = bufs

    def s(i, slot, o, k, dst, dev):
        return send(i, pv.at[slot, pl.ds(o, k)], dst, dev)

    def add(slot, o, k, buf):
        pv[slot, pl.ds(o, k)] = added(pv[slot, pl.ds(o, k)], buf[...])

    ready("x2")
    s10 = s(0, x2, 0, 64, r10, tm)
    s11 = s(1, x2, 64, 64, r11, tp)
    s10.start()
    s11.start()
    ready("tx")
    s3b = s(10, tx, 48, 32, m3.at[pl.ds(48, 32)], tx)
    s3b.start()
    ready("xm")
    ready("xp")
    s6b = s(15, xm, 64, 16, r6.at[pl.ds(64, 16)], tx)
    s7b = s(16, xp, 48, 16, r7.at[pl.ds(0, 16)], tx)
    s6b.start()
    s7b.start()
    ready("t2")
    s4 = s(2, t2, 0, 64, r4, tm)
    s5 = s(3, t2, 64, 64, r5, tp)
    s4.start()
    s5.start()
    s8 = s(4, xm, 80, 48, r8, tm)
    s9 = s(5, xp, 0, 48, r9, tp)
    s8.start()
    s9.start()
    ready("tm")
    ready("tp")
    s1b = s(11, tm, 80, 48, m1.at[pl.ds(80, 48)], tm)
    s2b = s(12, tp, 0, 48, m2.at[pl.ds(0, 48)], tp)
    s1b.start()
    s2b.start()
    yield
    s10.wait_recv()
    add(xm, 0, 64, r10)
    s6 = s(6, xm, 0, 64, r6.at[pl.ds(0, 64)], tx)
    s6.start()
    s11.wait_recv()
    add(xp, 64, 64, r11)
    s7 = s(7, xp, 64, 64, r7.at[pl.ds(16, 64)], tx)
    s7.start()
    yield
    s8.wait_recv()
    add(tx, 80, 48, r8)
    s9.wait_recv()
    add(tx, 0, 48, r9)
    s3a = s(13, tx, 80, 48, m3.at[pl.ds(80, 48)], tx)
    s3c = s(14, tx, 0, 48, m3.at[pl.ds(0, 48)], tx)
    s3a.start()
    s3c.start()
    yield
    s4.wait_recv()
    add(tm, 0, 64, r4)
    s6.wait_recv()
    s6b.wait_recv()
    add(tm, 0, 80, r6)
    s1 = s(8, tm, 0, 80, m1.at[pl.ds(0, 80)], tm)
    s1.start()
    yield
    s5.wait_recv()
    add(tp, 64, 64, r5)
    s7.wait_recv()
    s7b.wait_recv()
    add(tp, 48, 80, r7)
    s2 = s(9, tp, 48, 80, m2.at[pl.ds(48, 80)], tp)
    s2.start()
    yield
    ready("me")
    for c in (s3a, s3b, s3c, s1b, s2b, s1, s2):
        c.wait_recv()
    for c in (s1, s1b, s2, s2b, s3a, s3b, s3c, s4, s5, s6, s6b, s7, s7b, s8, s9, s10, s11):
        c.wait_send()


def reduce_ring(n, pv, ready, bufs, ss, rs, work=None):
    for point, _ in enumerate(reduce_steps(n, pv, ready, bufs, ss, rs)):
        if work:
            work(point)


def reduce_scratch(columns):
    rows = (64, 64, 48, 48, 80, 80, 64, 64, 128, 128, 128)
    return [VMEM((r, columns), bf16) for r in rows]


def added(a, b):
    return (a.astype(f32) + b.astype(f32)).astype(bf16)


def load_partials(n, p_ref, pv, ls):
    order = ("x2", "tx", "xm", "xp", "t2", "tm", "tp", "me")
    copies = {}
    for i, name in enumerate(order):
        copies[name] = pltpu.make_async_copy(p_ref.at[n[name]], pv.at[n[name]], ls.at[i])
        copies[name].start()
    return lambda name: copies[name].wait()


def inverse_rms(v):
    return lax.rsqrt(jnp.mean(v * v, axis=-1, keepdims=True) + EPS)


class Copies:
    def __init__(self, sems):
        self.sems, self.made = sems, []

    def start(self, src, dst):
        copy = pltpu.make_async_copy(src, dst, self.sems.at[len(self.made)])
        copy.start()
        self.made.append(copy)
        return copy

    def close(self):
        for copy in self.made:
            copy.wait()


def turn(v, cos, sin):
    lane = lax.broadcasted_iota(jnp.int32, v.shape, 1)
    low = lax.rem(lane, 64) < 32
    swapped = jnp.where(low, pltpu.roll(v, 96, 1), pltpu.roll(v, 32, 1))
    return v * cos + swapped * sin


def fetch_latent_weights(kvd_hbm, kvd_ref, sems):
    copies = [
        pltpu.make_async_copy(kvd_hbm, kvd_ref.at[pl.ds(0, KVR + DR)], sems.at[0]),
        pltpu.make_async_copy(kvd_hbm.at[pl.ds(KVR, DR)], kvd_ref.at[pl.ds(KVR + DR, DR)], sems.at[1]),
    ]
    for c in copies:
        c.start()
    return copies


KB = 256


def masked(s, key0, query0, prefix):
    keys = key0 + lax.broadcasted_iota(jnp.int32, s.shape, 0)
    rows = query0 + lax.broadcasted_iota(jnp.int32, s.shape, 1)
    return jnp.where((keys <= rows) | (keys < prefix), s, NEG)


def key_extent(query_block):
    return max(2, query_block + 1)


def head_lanes(shape, head):
    lane = lax.broadcasted_iota(jnp.int32, shape, 1)
    return (lane >= 64) if head else (lane < 64)


def head_query(q_ref, rows, head):
    rope = q_ref[rows, 256:QCOLS]
    rope = jnp.where(head_lanes(rope.shape, head), rope.astype(f32), 0.0).astype(bf16)
    return jnp.concatenate([q_ref[rows, head * 128 : head * 128 + 128], rope], axis=1)


def head_key(kvw_ref, kr_ref, rows, head):
    return jnp.concatenate([kvw_ref[rows, head * 256 : head * 256 + 128], kr_ref[rows, :]], axis=1)


def attention(prefix, q_ref, kvw_ref, kr_ref, wo_ref, attn_ref, lse_ref, ot_ref, s_scr, put):
    for i in range(4):
        rows = pl.ds(i * KB, KB)
        for h in range(2):
            q = head_query(q_ref, rows, h)
            top = jnp.full((1, KB), NEG, f32)
            for k in range(key_extent(i)):
                keys = pl.ds(k * KB, KB)
                s = dot_nt(head_key(kvw_ref, kr_ref, keys, h), q)
                if k >= i:
                    s = masked(s, k * KB, i * KB, prefix)
                s_scr[keys, :] = s
                top = jnp.maximum(top, jnp.max(s, axis=0, keepdims=True))
            top = top * (SCALE * LOG2E)
            total = jnp.zeros((1, KB), f32)
            out = jnp.zeros((DV, KB), f32)
            for k in range(key_extent(i)):
                keys = pl.ds(k * KB, KB)
                p = jnp.exp2(s_scr[keys, :] * (SCALE * LOG2E) - top)
                total = total + jnp.sum(p, axis=0, keepdims=True)
                out = out + dot_tn(kvw_ref[keys, h * 256 + 128 : h * 256 + 256], p.astype(bf16))
            out = out / total
            lse_ref[h : h + 1, rows] = top + jnp.log2(total)
            ot_ref[h, :, rows] = out
            attn_ref[rows, h * 128 : h * 128 + 128] = out.T.astype(bf16)
        put(i, dot(attn_ref[rows, :], wo_ref[...]).astype(bf16))


def own_total(n, pv, bufs):
    m1, m2, m3 = bufs[8:]
    return pv[n["me"]].astype(f32) + m1[...].astype(f32) + m2[...].astype(f32) + m3[...].astype(f32)


def fetch_hidden_weights(sg, eg, dst, zero_ref, sems, base):
    pieces = [(sg, 0, FS_OWN), (eg.at[0], 384, FE_OWN), (eg.at[1], 384 + FE_OWN, FE_OWN)]
    pieces += [(zero_ref, 736, 32), (zero_ref, FS_OWN, 32)]
    copies = []
    for i, (src, at, count) in enumerate(pieces):
        c = pltpu.make_async_copy(src, dst.at[pl.ds(at, count)], sems.at[base + i])
        c.start()
        copies.append(c)
    return copies


def ffn_rows(mixed, dm, route, wg_ref, wu_ref):
    a = dot_nt(mixed, wg_ref[...])
    b = dot_nt(mixed, wu_ref[...])
    first = (route == 0.0).astype(f32)
    second = (route == 1.0).astype(f32)
    l0 = a[:, FS_OWN : FS_OWN + 1]
    l1 = a[:, FS_OWN + 1 : FS_OWN + 2]
    top = jnp.maximum(l0, l1)
    e0 = jnp.exp(l0 - top)
    e1 = jnp.exp(l1 - top)
    r0 = e0 / (e0 + e1)
    r1 = e1 / (e0 + e1)
    col = lax.broadcasted_iota(jnp.int32, (1, HID), 1)
    is_shared = col < 384
    in0 = (col >= 384) & (col < 384 + FE_OWN)
    in1 = (col >= 384 + FE_OWN) & (col < 384 + 2 * FE_OWN)
    gate = jnp.where(is_shared, 1.0, 0.0) + jnp.where(in0, first * r0, 0.0) + jnp.where(in1, second * r1, 0.0)
    sig = jax.nn.sigmoid(a)
    silu = a * sig
    act = silu * b
    m = (gate * act).astype(bf16)
    scaled = dm * gate
    down = dm * act
    g0 = first * jnp.sum(jnp.where(in0, down, 0.0), axis=1, keepdims=True)
    g1 = second * jnp.sum(jnp.where(in1, down, 0.0), axis=1, keepdims=True)
    mean = r0 * g0 + r1 * g1
    da = scaled * b * (sig * (1.0 + a * (1.0 - sig)))
    da = da + jnp.where(col == FS_OWN, r0 * (g0 - mean), 0.0) + jnp.where(col == FS_OWN + 1, r1 * (g1 - mean), 0.0)
    da = da.astype(bf16)
    db = (scaled * silu).astype(bf16)
    return m, da, db, dot(da, wg_ref[...]) + dot(db, wu_ref[...])


def front_kernel(
    prefix_ref, x_hbm, grad_hbm, gain_ref, wq_hbm, kvd_hbm, lgain_ref, kvup_hbm, cos_hbm, sin_hbm, wo_hbm,
    fgain_ref, routes_ref, rt_ref, sg, su, sd, eg, eu, ed,
    normed_out, q_out, kvw_out, kr_out, lnorm_out, latent_out, gall_out, attn_out, lse_out, ot_out,
    hidden_ref, mixed_out, m_out, da_out, db_out, p2_out, gsum_ref,
    xall, wq_ref, kvd_ref, normed_ref, q_ref, kvw_ref, kr_ref, lnorm_ref, latent_ref, x_ref, kvup_ref,
    cos_ref, sin_ref, wo_ref, gall, attn_ref, lse_ref, ot_ref, s_scr,
    mixed_ref, m_ref, da_ref, db_ref, own, dm_scr, wg_ref, wu_ref, wd_ref, zero_ref, *rest,
):
    bufs, (xs, xr, gs, gr, ss, rs, ms, mr, ls, hs, ws, es, os) = rest[:11], rest[11:]
    n = neighbours()
    me = n["me"]
    prefix = prefix_ref[0]
    loads = Copies(hs)
    early = Copies(es)
    zero_ref[...] = jnp.zeros_like(zero_ref)
    entry_barrier(ring_peers(n))

    def shard_rows(slot):
        return pl.ds(pl.multiple_of(slot * OWN, OWN), OWN)

    def compute(slot, src):
        x = src.astype(f32)
        rows = shard_rows(slot)
        normed = (x * inverse_rms(x) * row(gain_ref)).astype(bf16)
        normed_ref[rows, :] = normed
        raw = dot(normed, wq_ref[...])
        cos = cos_ref[rows, :]
        sin = sin_ref[rows, :]
        q_ref[rows, :128] = raw[:, :128].astype(bf16)
        q_ref[rows, 128:256] = raw[:, 192:320].astype(bf16)
        rope = jnp.concatenate([raw[:, 128:192], raw[:, 320:384]], axis=1)
        q_ref[rows, 256:] = turn(rope, cos, sin).astype(bf16)
        raw = dot_nt(normed, kvd_ref[...])
        latent = raw[:, :KVR]
        latent_ref[rows, :] = latent
        lnorm = (latent * inverse_rms(latent) * row(lgain_ref)).astype(bf16)
        lnorm_ref[rows, :] = lnorm
        kr_ref[rows, :] = turn(raw[:, KVR:], cos, sin).astype(bf16)
        kvw_ref[rows, :] = dot(lnorm, kvup_ref[...]).astype(bf16)
        early.start(normed_ref.at[rows], normed_out.at[rows])

    second = gather_steps(n, grad_hbm, gall, gs, gr)
    for k, slot in enumerate(gather_steps(n, x_hbm, xall, xs, xr)):
        if k == 0:
            loads.start(x_hbm, x_ref)
            loads.start(wq_hbm, wq_ref)
            copies = fetch_latent_weights(kvd_hbm, kvd_ref, ls)
            for src, dst in ((kvup_hbm, kvup_ref), (cos_hbm, cos_ref), (sin_hbm, sin_ref)):
                loads.start(src, dst)
            loads.start(wo_hbm, wo_ref)
            loads.start(grad_hbm, gall.at[me])
            loads.close()
            for c in copies:
                c.wait()
            weights = fetch_hidden_weights(sd, ed, wd_ref, zero_ref, ws, 0)
            weights += fetch_hidden_weights(sg, eg, wg_ref, zero_ref, ws, 5)
            weights += fetch_hidden_weights(su, eu, wu_ref, zero_ref, ws, 10)
            compute(slot, x_ref[...])
            continue
        if k in (1, 4):
            next(second)
        compute(slot, xall[slot])
    for src, dst in (
        (q_ref, q_out), (kvw_ref, kvw_out), (kr_ref, kr_out), (lnorm_ref, lnorm_out), (latent_ref, latent_out)
    ):
        early.start(src, dst)

    def put(i, block):
        for t in range(2):
            xall[i * 2 + t] = block[t * OWN : t * OWN + OWN]

    next(second)
    attention(prefix, q_ref, kvw_ref, kr_ref, wo_ref, attn_ref, lse_ref, ot_ref, s_scr, put)
    for src, dst in ((attn_ref, attn_out), (lse_ref, lse_out), (ot_ref, ot_out)):
        early.start(src, dst)

    def dm_pair(k):
        two = pl.ds(k * 2, 2)
        dm_scr[two] = dot_nt(gall[two].reshape(256, WIDE), wd_ref[...]).reshape(2, OWN, HID)

    def work(point):
        if point == 1:
            for _ in second:
                pass
            early.start(gall, gall_out)
            for c in weights[:5]:
                c.wait()
            dm_pair(0)
        elif point == 2:
            dm_pair(1)
        elif point == 3:
            dm_pair(2)
        elif point == 4:
            dm_pair(3)
            for c in weights[5:]:
                c.wait()
            router = jnp.concatenate([rt_ref[...].astype(f32), jnp.zeros((30, WIDE), f32)], axis=0)
            wg_ref[pl.ds(FS_OWN, 32), :] = router.astype(bf16)

    reduce_ring(n, xall, lambda name: None, bufs, ss, rs, work)
    hidden = x_ref[...].astype(f32) + own_total(n, xall, bufs)
    hidden_ref[...] = hidden
    own[...] = (hidden * inverse_rms(hidden) * row(fgain_ref)).astype(bf16)
    mixed_ref[me] = own[...]
    gsum_ref[...] = jnp.zeros_like(gsum_ref)
    waiting = []
    by_token = routes_ref[...].astype(f32).T
    early.close()
    stores = Copies(os)

    def on_shard(slot):
        waiting.append(slot)
        if len(waiting) < 2:
            return
        pair = list(waiting)
        waiting.clear()
        mixed = jnp.concatenate([mixed_ref[s] for s in pair], axis=0)
        dm = jnp.concatenate([dm_scr[s] for s in pair], axis=0)
        shard = lax.broadcasted_iota(jnp.int32, (OWN, SHARDS), 1)
        route = jnp.concatenate(
            [jnp.sum(jnp.where(shard == s, by_token, 0.0), axis=1, keepdims=True) for s in pair], axis=0
        )
        m, da, db, back = ffn_rows(mixed, dm, route, wg_ref, wu_ref)
        gsum_ref[...] += jnp.sum(back * mixed.astype(f32), axis=0, keepdims=True)
        back = back.astype(bf16)
        for i, s in enumerate(pair):
            part = slice(i * OWN, i * OWN + OWN)
            rows = shard_rows(s)
            m_ref[s] = m[part]
            da_ref[s] = da[part]
            db_ref[s] = db[part]
            normed_ref[rows, :] = back[part]
            for src, dst in ((mixed_ref, mixed_out), (m_ref, m_out), (da_ref, da_out), (db_ref, db_out)):
                stores.start(src.at[s], dst.at[s])
            stores.start(normed_ref.at[rows], p2_out.at[rows])

    gather_ring(n, own, mixed_ref, ms, mr, on_shard)
    stores.close()


def front(prefix, x, grad, gain, wq, kvd, lgain, kvup, cos, sin, wo, fgain, routes, rt, sg, su, sd, eg, eu, ed):
    def rows(c, t=bf16):
        return jax.ShapeDtypeStruct((LENGTH, c), t)

    def shards(c):
        return jax.ShapeDtypeStruct((SHARDS, OWN, c), bf16)

    def other(*shape):
        return jax.ShapeDtypeStruct(shape, f32)

    return pl.pallas_call(
        front_kernel,
        out_shape=(
            rows(WIDE), rows(QCOLS), rows(512), rows(128), rows(KVR), rows(KVR, f32), shards(WIDE), rows(256),
            other(2, LENGTH), other(2, DV, LENGTH), other(OWN, WIDE),
            shards(WIDE), shards(HID), shards(HID), shards(HID), rows(WIDE), other(1, WIDE),
        ),
        in_specs=[pl.BlockSpec(memory_space=pltpu.SMEM), anym(), anym(), vmem(), anym(), anym(), vmem()]
        + [anym()] * 4
        + [vmem()] * 3
        + [anym()] * 6,
        out_specs=[anym()] * 10 + [vmem()] + [anym()] * 5 + [vmem()],
        scratch_shapes=[
            VMEM((SHARDS, OWN, WIDE), bf16),
            VMEM((WIDE, QCOLS), bf16),
            VMEM((LATENT_ROWS, WIDE), bf16),
            VMEM((LENGTH, WIDE), bf16),
            VMEM((LENGTH, QCOLS), bf16),
            VMEM((LENGTH, 512), bf16),
            VMEM((LENGTH, 128), bf16),
            VMEM((LENGTH, KVR), bf16),
            VMEM((LENGTH, KVR), f32),
            VMEM((OWN, WIDE), bf16),
            VMEM((KVR, 512), bf16),
            VMEM((LENGTH, 128), f32),
            VMEM((LENGTH, 128), f32),
            VMEM((256, WIDE), bf16),
            VMEM((SHARDS, OWN, WIDE), bf16),
            VMEM((LENGTH, 256), bf16),
            VMEM((2, LENGTH), f32),
            VMEM((2, DV, LENGTH), f32),
            VMEM((LENGTH, KB), f32),
            VMEM((SHARDS, OWN, WIDE), bf16),
            VMEM((SHARDS, OWN, HID), bf16),
            VMEM((SHARDS, OWN, HID), bf16),
            VMEM((SHARDS, OWN, HID), bf16),
            VMEM((OWN, WIDE), bf16),
            VMEM((SHARDS, OWN, HID), f32),
            VMEM((HID, WIDE), bf16),
            VMEM((HID, WIDE), bf16),
            VMEM((HID, WIDE), bf16),
            VMEM((32, WIDE), bf16),
        ]
        + reduce_scratch(WIDE)
        + [DMA((17,))] * 8
        + [DMA((2,)), DMA((7,)), DMA((15,)), DMA((17,)), DMA((40,))],
        compiler_params=pltpu.CompilerParams(
            collective_id=0, has_side_effects=True, vmem_limit_bytes=62 * MIB
        ),
        cost_estimate=pl.CostEstimate(flops=25 * 10**9, bytes_accessed=5 * 10**7, transcendentals=3 * 10**6),
        name="front",
    )(prefix, x, grad, gain, wq, kvd, lgain, kvup, cos, sin, wo, fgain, routes, rt, sg, su, sd, eg, eu, ed)


def rows_of(ref):
    return ref[...].reshape(LENGTH, ref.shape[-1])


BLOCKS = 9


QUARTER = 288


def turn_kernel(
    p_ref, hidden_ref, grad_ref, gain_ref, mixed_hbm, gall_hbm, m_hbm, da_hbm, db_hbm, sd, ed,
    hgrad_ref, hall_ref, sum_ref, router_ref, moe_hbm,
    mixed_ref, gall_ref, m_ref, da_ref, db_ref, half_ref, hs, pv, low, dw_scr, core_scr, moe_scr, wd_ref, zero_ref,
    got, *rest,
):
    bufs, (ss, rs, gs, gr, cs, cr, ys, yr, ls, ws, os) = rest[:11], rest[11:]
    n = neighbours()
    d = copies_of()
    ready = load_partials(n, p_ref, pv, ls)
    zero_ref[...] = jnp.zeros_like(zero_ref)
    loads = Copies(hs)
    copies = []
    entry_barrier(ring_peers(n), (d["core"], d["yp"], d["ym"]))
    stores = Copies(os)
    crossed = []
    sent = []
    theirs = pl.multiple_of((1 - d["c"]) * OWN, OWN)
    mine = pl.multiple_of(d["c"] * OWN, OWN)
    sums = [YSum(d, 48, half_ref, 384 * k, got.at[k], ys, yr, 6 * k) for k in range(3)]

    def product(index, left, right, block):
        k = index * 3 + block
        if block == 0:
            for c in {2: loads.made[:2], 0: loads.made[2:4], 1: loads.made[4:]}[index]:
                c.wait()
        left = left[:, :, pl.ds(block * 256, 256)].reshape(LENGTH, 256)
        dw_scr[k] = dot_tn(left, rows_of(right)).astype(bf16)
        c = dp_copy(dw_scr.at[k, pl.ds(theirs, OWN)], core_scr.at[k], cs.at[k], cr.at[k], d["core"])
        c.start()
        crossed.append((k, c))
        if k == 1:
            router_ref[...] = dw_scr[1, FS_OWN - 256 : FS_OWN - 240, :]

    def expert_sum(block):
        two = pl.ds(block * 2, 2)
        moe_scr[two] = dot(m_ref[two].reshape(256, HID), wd_ref[...]).astype(bf16).reshape(2, OWN, WIDE)
        stores.start(moe_scr.at[two], moe_hbm.at[two])

    def meet():
        k, c = crossed.pop(0)
        c.wait_recv()
        half_ref[pl.ds(k * OWN, OWN), :] = added(dw_scr[k, pl.ds(mine, OWN), :], core_scr[k])
        sent.append(c)

    jobs = [functools.partial(product, 2, m_ref, gall_ref, b) for b in range(3)]
    jobs += [functools.partial(product, 0, da_ref, mixed_ref, b) for b in range(3)]
    jobs += [functools.partial(product, 1, db_ref, mixed_ref, b) for b in range(3)]
    plan = {0: 3, 1: 2, 2: 2, 3: 1, 4: 1}

    def work(point):
        if point == 0:
            for src, dst in (
                (m_hbm, m_ref), (gall_hbm, gall_ref), (da_hbm, da_ref), (mixed_hbm, mixed_ref), (db_hbm, db_ref)
            ):
                loads.start(src, dst)
            copies.extend(fetch_hidden_weights(sd, ed, wd_ref, zero_ref, ws, 0))
        if point == 1:
            meet_all(2)
        for _ in range(plan[point]):
            jobs.pop(0)()
        if point == 2:
            while len(crossed) > 1:
                meet()
            sums[0].step(0)
        elif point == 3:
            sums[2].step(1)
        elif point == 4:
            meet_all(1)
            sums[0].step(1)

    def meet_all(part):
        while crossed:
            meet()
        sums[part].step(0)

    reduce_ring(n, pv, ready, bufs, ss, rs, work)
    total = own_total(n, pv, bufs)
    hidden = hidden_ref[...]
    inv = inverse_rms(hidden)
    unit = hidden * inv
    scaled = total * row(gain_ref)
    back = inv * (scaled - unit * jnp.mean(scaled * unit, axis=-1, keepdims=True))
    hgrad = grad_ref[...].astype(f32) + back
    hgrad_ref[...] = hgrad
    low[...] = hgrad.astype(bf16)
    for k, _ in enumerate(gather_steps(n, low, hall_ref, gs, gr)):
        if k == 0:
            stores.start(low, hall_ref.at[n["me"]])
            for c in copies:
                c.wait()
            expert_sum(0)
            expert_sum(1)
            sums[2].step(2)
            sums[1].step(1)
        elif k == 1:
            expert_sum(2)
            expert_sum(3)
            sums[0].step(2)
        elif k == 3:
            sums[1].step(2)
            sums[2].step(3)
        elif k == 5:
            sums[0].step(3)
    sums[1].step(3)
    for k in range(3):
        for way in range(2):
            sum_ref[pl.ds(k * 96 + way * 48, 48), :] = got[k, 2, way]
        sums[k].close()
    stores.close()
    for c in sent:
        c.wait_send()


def turn_back(p, hidden, grad, gain, mixed, gall, m, da, db, sd, ed):
    outs = (
        jax.ShapeDtypeStruct((OWN, WIDE), f32),
        jax.ShapeDtypeStruct((SHARDS, OWN, WIDE), bf16),
        jax.ShapeDtypeStruct((QUARTER, WIDE), bf16),
        jax.ShapeDtypeStruct((16, WIDE), bf16),
        jax.ShapeDtypeStruct((SHARDS, OWN, WIDE), bf16),
    )
    return pl.pallas_call(
        turn_kernel,
        out_shape=outs,
        in_specs=[anym()] + [vmem()] * 3 + [anym()] * 7,
        out_specs=[vmem(), anym(), vmem(), vmem(), anym()],
        scratch_shapes=[
            VMEM((SHARDS, OWN, WIDE), bf16),
            VMEM((SHARDS, OWN, WIDE), bf16),
            VMEM((SHARDS, OWN, HID), bf16),
            VMEM((SHARDS, OWN, HID), bf16),
            VMEM((SHARDS, OWN, HID), bf16),
            VMEM((BLOCKS * OWN, WIDE), bf16),
            DMA((5,)),
            VMEM((SHARDS, OWN, WIDE), bf16),
            VMEM((OWN, WIDE), bf16),
            VMEM((BLOCKS, 256, WIDE), bf16),
            VMEM((BLOCKS, OWN, WIDE), bf16),
            VMEM((SHARDS, OWN, WIDE), bf16),
            VMEM((HID, WIDE), bf16),
            VMEM((32, WIDE), bf16),
            VMEM((3, 3, 2, 48, WIDE), bf16),
        ]
        + reduce_scratch(WIDE)
        + [DMA((17,))] * 4
        + [DMA((BLOCKS,)), DMA((BLOCKS,)), DMA((18,)), DMA((18,)), DMA((8,)), DMA((5,)), DMA((5,))],
        compiler_params=pltpu.CompilerParams(
            collective_id=2, has_side_effects=True, vmem_limit_bytes=60 * MIB
        ),
        cost_estimate=pl.CostEstimate(flops=13 * 10**9, bytes_accessed=4 * 10**7, transcendentals=0),
        name="turn_back",
    )(p, hidden, grad, gain, mixed, gall, m, da, db, sd, ed)


LATE = 3072
PACK_COLS = 1280


def attend_back_kernel(
    prefix_ref, hall_hbm, wo_ref, q_ref, kvw_ref, kr_ref, lse_ref, ot_ref,
    kvup_ref, latent_hbm, lgain_ref, cos_ref, sin_ref, wq_hbm, kvd_hbm,
    normed_hbm, gain_ref, fgain_ref, gsum_ref, router_ref, ysum_ref,
    p_out, all_ref, jq_out, jk_out, kvg_out, tail_ref,
    hall_ref, latent_ref, wq_ref, normed_ref, p_ref, hs, os, do_scr, dk_scr, dv_scr, jq_scr, jk_scr, kvg_scr, kvd_ref, far_scr, quarter, ls, xs, xr, ys, yr,
):
    prefix = prefix_ref[0]
    d = copies_of()
    loads = Copies(hs)
    for i in range(4):
        loads.start(hall_hbm.at[pl.ds(i * KB, KB)], hall_ref.at[pl.ds(i * KB, KB)])
    for src, dst in ((latent_hbm, latent_ref), (wq_hbm, wq_ref), (normed_hbm, normed_ref)):
        loads.start(src, dst)
    stores = Copies(os)
    entry_barrier((), (d["xo"], d["yp"], d["ym"]))
    half = QUARTER // 2
    parts = [pl.ds(0, half), pl.ds(half, half)]
    crosses = [dp_copy(ysum_ref.at[r], far_scr.at[r], xs.at[k], xr.at[k], d["xo"]) for k, r in enumerate(parts)]
    for cross in crosses:
        cross.start()
    spread = []

    def meet(k):
        crosses[k].wait_recv()
        quarter[parts[k], :] = added(ysum_ref[parts[k], :], far_scr[parts[k], :])
        if k == 0:
            for i, peer in enumerate((d["yp"], d["ym"])):
                copy = dp_copy(quarter.at[parts[k]], all_ref.at[d["y"], parts[k]], ys.at[i], yr.at[i], peer)
                copy.start()
                spread.append(copy)
        stores.start(quarter.at[parts[k]], all_ref.at[d["y"], parts[k]])

    copies = fetch_latent_weights(kvd_hbm, kvd_ref, ls)
    for i in range(4):
        rows = pl.ds(i * KB, KB)
        loads.made[i].wait()
        do_scr[rows, :] = dot_nt(hall_ref[rows, :], wo_ref[...]).astype(bf16)
    dk_scr[...] = jnp.zeros_like(dk_scr)
    dv_scr[...] = jnp.zeros_like(dv_scr)
    for i in range(4):
        rows = pl.ds(i * KB, KB)
        plain = []
        turned = jnp.zeros((KB, 128), f32)
        for h in range(2):
            q = head_query(q_ref, rows, h)
            do = do_scr[rows, h * 128 : h * 128 + 128]
            lse = lse_ref[h : h + 1, rows]
            delta = jnp.sum(do.astype(f32).T * ot_ref[h, :, rows], axis=0, keepdims=True)
            dq = jnp.zeros((KB, 256), f32)
            for k in range(key_extent(i)):
                keys = pl.ds(k * KB, KB)
                key = head_key(kvw_ref, kr_ref, keys, h)
                s = dot_nt(key, q)
                if k >= i:
                    s = masked(s, k * KB, i * KB, prefix)
                p = jnp.exp2(s * (SCALE * LOG2E) - lse)
                dp = dot_nt(kvw_ref[keys, h * 256 + 128 : h * 256 + 256], do)
                ds = (p * (dp - delta)).astype(bf16)
                dv_scr[h, keys, :] += dot(p.astype(bf16), do)
                dk_scr[h, keys, :] += dot(ds, q)
                dq = dq + dot_tn(ds, key)
            dq = dq * SCALE
            plain.append(dq[:, :128])
            turned = turned + jnp.where(head_lanes(turned.shape, h), dq[:, 128:], 0.0)
        turned = turn(turned, cos_ref[rows, :], -sin_ref[rows, :])
        j = jnp.concatenate([plain[0], turned[:, :64], plain[1], turned[:, 64:]], axis=1)
        jq_scr[rows, :] = j.astype(bf16)
    meet(0)
    for c in copies + loads.made[4:]:
        c.wait()
    gain_sum = jnp.zeros((1, WIDE), f32)
    lgain_sum = jnp.zeros((1, KVR), f32)
    for i in range(4):
        rows = pl.ds(i * KB, KB)
        for h in range(2):
            kvg_scr[rows, h * 256 : h * 256 + 128] = (dk_scr[h, rows, :128] * SCALE).astype(bf16)
            kvg_scr[rows, h * 256 + 128 : h * 256 + 256] = dv_scr[h, rows, :].astype(bf16)
        dkr = (dk_scr[0, rows, 128:] + dk_scr[1, rows, 128:]) * SCALE
        jk_scr[rows, KVR:] = turn(dkr, cos_ref[rows, :], -sin_ref[rows, :]).astype(bf16)
        dl = dot_nt(kvg_scr[rows, :], kvup_ref[...])
        latent = latent_ref[rows, :]
        inv = inverse_rms(latent)
        unit = latent * inv
        lgain_sum = lgain_sum + jnp.sum(dl * unit, axis=0, keepdims=True)
        scaled = dl * row(lgain_ref)
        back = inv * (scaled - unit * jnp.mean(scaled * unit, axis=-1, keepdims=True))
        jk_scr[rows, :KVR] = back.astype(bf16)
        into = dot_nt(jq_scr[rows, :], wq_ref[...]) + dot(jk_scr[rows, :], kvd_ref[...])
        gain_sum = gain_sum + jnp.sum(into * normed_ref[rows, :].astype(f32), axis=0, keepdims=True)
        into = into.astype(bf16)
        for t in range(2):
            p_ref[i * 2 + t] = into[t * OWN : t * OWN + OWN]
        stores.start(p_ref.at[pl.ds(i * 2, 2)], p_out.at[pl.ds(i * 2, 2)])
        for src, dst in ((jq_scr, jq_out), (jk_scr, jk_out), (kvg_scr, kvg_out)):
            stores.start(src.at[rows], dst.at[rows])
    empty = jnp.zeros((1, 192), f32)
    lat = jnp.concatenate([v for t in range(SHARDS) for v in (lgain_sum[:, t * 64 : t * 64 + 64], empty)], axis=1)
    tail_ref[...] = jnp.concatenate(
        [
            gain_sum / row(gain_ref),
            gsum_ref[...] / row(fgain_ref),
            router_ref[:2, :].astype(f32),
            lat,
            jnp.zeros((3, WIDE), f32),
        ],
        axis=0,
    )
    meet(1)
    for copy in spread:
        copy.wait()
    for cross in crosses:
        cross.wait_send()
    stores.close()


def attend_back(*args):
    return pl.pallas_call(
        attend_back_kernel,
        out_shape=(
            jax.ShapeDtypeStruct((SHARDS, OWN, WIDE), bf16),
            jax.ShapeDtypeStruct((4, QUARTER, WIDE), bf16),
            jax.ShapeDtypeStruct((LENGTH, QCOLS), bf16),
            jax.ShapeDtypeStruct((LENGTH, LATENT_ROWS), bf16),
            jax.ShapeDtypeStruct((LENGTH, 512), bf16),
            jax.ShapeDtypeStruct((8, WIDE), f32),
        ),
        in_specs=[pl.BlockSpec(memory_space=pltpu.SMEM), anym()]
        + [vmem()] * 7
        + [anym()]
        + [vmem()] * 3
        + [anym()] * 3
        + [vmem()] * 5,
        out_specs=[anym()] * 5 + [vmem()],
        scratch_shapes=[
            VMEM((LENGTH, WIDE), bf16),
            VMEM((LENGTH, KVR), f32),
            VMEM((WIDE, QCOLS), bf16),
            VMEM((LENGTH, WIDE), bf16),
            VMEM((SHARDS, OWN, WIDE), bf16),
            DMA((8,)),
            DMA((18,)),
            VMEM((LENGTH, 256), bf16),
            VMEM((2, LENGTH, 256), f32),
            VMEM((2, LENGTH, DV), f32),
            VMEM((LENGTH, QCOLS), bf16),
            VMEM((LENGTH, LATENT_ROWS), bf16),
            VMEM((LENGTH, 512), bf16),
            VMEM((LATENT_ROWS, WIDE), bf16),
            VMEM((QUARTER, WIDE), bf16),
            VMEM((QUARTER, WIDE), bf16),
            DMA((2,)),
            DMA((2,)),
            DMA((2,)),
            DMA((2,)),
            DMA((2,)),
        ],
        compiler_params=pltpu.CompilerParams(
            collective_id=4, has_side_effects=True, vmem_limit_bytes=60 * MIB
        ),
        cost_estimate=pl.CostEstimate(flops=18 * 10**9, bytes_accessed=4 * 10**7, transcendentals=2 * 10**6),
        name="attend_back",
    )(*args)


LATE_HALF = LATE // 2
LATE_PIECE = LATE_HALF // 8


def half_pieces(y, all_ref, second_ref, opposite_ref):
    half = QUARTER // 2
    below, above = lax.rem(y + 3, 4), lax.rem(y + 1, 4)

    def view(ref, lead, offset=0):
        return lambda start, count: ref.at[lead, pl.ds(start - offset, count)]

    return (
        (view(all_ref, y), y, 0, QUARTER),
        (view(all_ref, below), below, 0, half),
        (view(all_ref, above), above, 0, half),
        (view(second_ref, 0, half), below, half, half),
        (view(second_ref, 1, half), above, half, half),
        (lambda start, count: opposite_ref.at[pl.ds(start, count)], lax.rem(y + 2, 4), 0, QUARTER),
    )


def last_kernel(
    p_ref, x_ref, hgrad_ref, gain_ref, tail_ref, hidden_ref, all_ref, moe_ref,
    normed_hbm, hall_hbm, jq_hbm, jk_hbm, kvg_hbm, attn_hbm, lnorm_hbm,
    out_ref, moved_ref, second_ref, opposite_ref, other, lall, packs,
    normed_ref, hall_ref, jq_ref, jk_ref, kvg_ref, attn_ref, lnorm_ref, hs,
    pv, pack_pv, moe_pv, pack, late, core_scr, half, got, near, far,
    pack_core, by_y, pack_near, pack_far, *rest,
):
    bufs, pack_bufs, moe_bufs = rest[:11], rest[11:22], rest[22:33]
    ss, rs, ps, pr, ms, mr, ys, yr, xs, xr, gs, gr, cs, cr, zs, zr, ls, mls = rest[33:]
    n = neighbours()
    d = copies_of()
    c, y = d["c"], d["y"]
    ready = load_partials(n, p_ref, pv, ls)
    loads = Copies(hs)
    theirs = pl.ds(pl.multiple_of((1 - c) * LATE_HALF, OWN), LATE_HALF)
    mine = pl.ds(pl.multiple_of(c * LATE_HALF, OWN), LATE_HALF)
    pack_theirs = pl.ds(pl.multiple_of((1 - c) * 64, 64), 64)
    pack_mine = pl.ds(pl.multiple_of(c * 64, 64), 64)
    entry_barrier(ring_peers(n), (d["core"], d["yp"], d["ym"], d["y2"], d["xo"]))
    first = dp_copy(late.at[theirs], core_scr, cs.at[0], cr.at[0], d["core"])
    cross = dp_copy(near, far, xs.at[0], xr.at[0], d["xo"])
    rows0, rows1 = pl.ds(0, QUARTER // 2), pl.ds(QUARTER // 2, QUARTER // 2)
    below = lax.rem(y + 3, 4)
    spread = [
        dp_copy(all_ref.at[y, rows1], second_ref.at[0], gs.at[0], gr.at[0], d["yp"]),
        dp_copy(all_ref.at[y, rows1], second_ref.at[1], gs.at[1], gr.at[1], d["ym"]),
    ]
    onward = [
        dp_copy(all_ref.at[below, rows0], opposite_ref.at[rows0], gs.at[2], gr.at[2], d["yp"]),
        dp_copy(second_ref.at[1], opposite_ref.at[rows1], gs.at[3], gr.at[3], d["ym"]),
    ]
    ring = reduce_steps(n, pv, ready, bufs, ss, rs)
    next(ring)
    for src, dst in (
        (jk_hbm, jk_ref), (normed_hbm, normed_ref), (jq_hbm, jq_ref), (lnorm_hbm, lnorm_ref), (kvg_hbm, kvg_ref),
        (attn_hbm, attn_ref), (hall_hbm, hall_ref),
    ):
        loads.start(src, dst)
    moe_ready = load_partials(n, moe_ref, moe_pv, mls)
    for copy in spread:
        copy.start()
    for copy in loads.made[:2]:
        copy.wait()
    blank = jnp.zeros((56, KB), f32)
    for i in range(8):
        cols = pl.ds(i * KB, KB)
        down = dot_tn(jk_ref[...], normed_ref[:, cols])
        for k in range(4):
            pack_pv[i, :, k * KB : k * KB + KB] = down[k * OWN : k * OWN + OWN].astype(bf16)
        rope = down[KVR : KVR + DR] + down[KVR + DR :]
        end = jnp.concatenate([rope, tail_ref[:, i * KB : i * KB + KB], blank], axis=0)
        pack_pv[i, :, 4 * KB :] = end.astype(bf16)
    pack_ring = reduce_steps(n, pack_pv, lambda name: None, pack_bufs, ps, pr)
    next(pack_ring)
    next(ring)
    for copy in loads.made[2:]:
        copy.wait()
    late[pl.ds(1536, KVR), :] = dot_tn(lnorm_ref[...], kvg_ref[...]).astype(bf16)
    for i in range(4):
        cols = pl.ds(i * 512, 512)
        late[pl.ds(2048 + i * 256, 256), :] = dot_tn(attn_ref[...], hall_ref[:, cols]).astype(bf16)
        query = dot_tn(normed_ref[:, cols], jq_ref[...]).astype(bf16)
        for k in range(3):
            late[pl.ds(k * 512, 512), i * 128 : i * 128 + 128] = query[:, k * 128 : k * 128 + 128]
    first.start()
    next(ring)
    first.wait_recv()
    half[...] = added(late[mine, :], core_scr[...])
    deal = y_deal(d, half, 2 * LATE_PIECE, got, ys, yr, 0)
    for copy in deal:
        copy.start()
    next(ring)
    next(pack_ring)
    next(ring)
    next(pack_ring)
    next(pack_ring)
    next(pack_ring)
    for copy in deal:
        copy.wait_recv()
    own_rows = pl.ds(pl.multiple_of(y * (2 * LATE_PIECE), 16), 2 * LATE_PIECE)
    total = half[own_rows, :].astype(f32)
    for hops in (1, 2, 3):
        total = total + got[lax.rem(y + hops, 4)].astype(f32)
    near[...] = total.astype(bf16)
    cross.start()
    for copy in spread:
        copy.wait_recv()
    for copy in onward:
        copy.start()
    moe_ring = reduce_steps(n, moe_pv, moe_ready, moe_bufs, ms, mr)
    next(moe_ring)
    next(ring, None)
    total = own_total(n, pv, bufs)
    x = x_ref[...].astype(f32)
    inv = inverse_rms(x)
    unit = x * inv
    scaled = total * row(gain_ref)
    back = inv * (scaled - unit * jnp.mean(scaled * unit, axis=-1, keepdims=True))
    out_ref[...] = (hgrad_ref[...] + back).astype(bf16)
    next(pack_ring, None)
    pack[...] = own_total(n, pack_pv, pack_bufs).astype(bf16)
    pack_first = dp_copy(pack.at[pack_theirs], pack_core, cs.at[1], cr.at[1], d["core"])
    pack_first.start()
    cross.wait_recv()
    lall[c, y] = added(near[...], far[...])
    pack_first.wait_recv()
    by_y[y] = added(pack[pack_mine, :], pack_core[...])
    pack_spread = y_spread(d, by_y, gs, gr, 4)
    for copy in pack_spread:
        copy.start()
    ygather = YGather(d, LATE_PIECE, lall.at[c], zs, zr)
    ygather.step(0)
    next(moe_ring)
    for copy in onward:
        copy.wait_recv()
    swaps = []
    for i, (view, slot, start, count) in enumerate(half_pieces(y, all_ref, second_ref, opposite_ref)):
        rows = pl.ds(start, count)
        swaps.append(dp_copy(view(start, count), other.at[slot, rows], cs.at[4 + i], cr.at[4 + i], d["core"]))
        swaps[-1].start()
    for copy in pack_spread:
        copy.wait_recv()
    total = by_y[0].astype(f32) + by_y[1].astype(f32) + by_y[2].astype(f32) + by_y[3].astype(f32)
    pack_near[...] = total.astype(bf16)
    pack_cross = dp_copy(pack_near, pack_far, xs.at[1], xr.at[1], d["xo"])
    pack_cross.start()
    next(moe_ring)
    next(moe_ring)
    next(moe_ring)
    ygather.step(1)
    pack_cross.wait_recv()
    packs[c] = added(pack_near[...], pack_far[...])
    pack_back = dp_copy(packs.at[c], packs.at[c], cs.at[3], cr.at[3], d["core"])
    pack_back.start()
    ygather.step(2)
    late_back = dp_copy(lall.at[c], lall.at[c], cs.at[2], cr.at[2], d["core"])
    late_back.start()
    next(moe_ring, None)
    moved_ref[...] = (hidden_ref[...] + own_total(n, moe_pv, moe_bufs)).astype(bf16)
    for copy in (pack_back, late_back, *swaps):
        copy.wait_recv()
    for copy in (first, cross, pack_first, pack_cross, pack_back, late_back):
        copy.wait_send()
    for copy in (*spread, *onward, *deal, *pack_spread, *ygather.all, *swaps):
        copy.wait_send()


def last(p, x, hgrad, gain, tail, hidden, quarters, moe, normed, hall, jq, jk, kvg, attn, lnorm):
    return pl.pallas_call(
        last_kernel,
        out_shape=(
            jax.ShapeDtypeStruct((OWN, WIDE), bf16),
            jax.ShapeDtypeStruct((OWN, WIDE), bf16),
            jax.ShapeDtypeStruct((2, QUARTER // 2, WIDE), bf16),
            jax.ShapeDtypeStruct((QUARTER, WIDE), bf16),
            jax.ShapeDtypeStruct((4, QUARTER, WIDE), bf16),
            jax.ShapeDtypeStruct((2, 4, 2 * LATE_PIECE, 512), bf16),
            jax.ShapeDtypeStruct((2, 64, PACK_COLS), bf16),
        ),
        in_specs=[anym()] + [vmem()] * 5 + [anym()] * 9,
        out_specs=[vmem(), vmem(), anym(), anym(), anym(), vmem(), vmem()],
        scratch_shapes=[
            VMEM((LENGTH, WIDE), bf16),
            VMEM((LENGTH, WIDE), bf16),
            VMEM((LENGTH, QCOLS), bf16),
            VMEM((LENGTH, LATENT_ROWS), bf16),
            VMEM((LENGTH, 512), bf16),
            VMEM((LENGTH, 256), bf16),
            VMEM((LENGTH, KVR), bf16),
            DMA((7,)),
            VMEM((SHARDS, OWN, WIDE), bf16),
            VMEM((SHARDS, OWN, PACK_COLS), bf16),
            VMEM((SHARDS, OWN, WIDE), bf16),
            VMEM((OWN, PACK_COLS), bf16),
            VMEM((LATE, 512), bf16),
            VMEM((LATE_HALF, 512), bf16),
            VMEM((LATE_HALF, 512), bf16),
            VMEM((4, 2 * LATE_PIECE, 512), bf16),
            VMEM((2 * LATE_PIECE, 512), bf16),
            VMEM((2 * LATE_PIECE, 512), bf16),
            VMEM((64, PACK_COLS), bf16),
            VMEM((4, 64, PACK_COLS), bf16),
            VMEM((64, PACK_COLS), bf16),
            VMEM((64, PACK_COLS), bf16),
        ]
        + reduce_scratch(WIDE)
        + reduce_scratch(PACK_COLS)
        + reduce_scratch(WIDE)
        + [DMA((17,))] * 6
        + [DMA((3,)), DMA((3,)), DMA((2,)), DMA((2,)), DMA((7,)), DMA((7,)), DMA((10,)), DMA((10,))]
        + [DMA((4,)), DMA((4,)), DMA((8,)), DMA((8,))],
        compiler_params=pltpu.CompilerParams(
            collective_id=5, has_side_effects=True, vmem_limit_bytes=60 * MIB
        ),
        cost_estimate=pl.CostEstimate(flops=6 * 10**9, bytes_accessed=2 * 10**7, transcendentals=0),
        name="last",
    )(p, x, hgrad, gain, tail, hidden, quarters, moe, normed, hall, jq, jk, kvg, attn, lnorm)


def widen_kernel(
    own_hbm, second_hbm, opposite_hbm, other_hbm, lall_hbm, pack_ref,
    q_ref, kv_ref, o_ref, down_ref, again_ref, fgain_ref, router_ref, lgain_ref, sg, su, sd, eg, eu, ed,
    wide, full_ref, lall_ref, os, hs,
):
    stores = []
    loads = Copies(hs)
    d = copies_of()
    c, y = d["c"], d["y"]

    def place(view, slot, start, count, core):
        for k in range(3):
            low, high = max(start, 96 * k), min(start + count, 96 * k + 96)
            if low < high:
                at = pl.multiple_of(384 * k + 96 * slot + (low - 96 * k), 16)
                loads.start(view(low, high - low), full_ref.at[core, pl.ds(at, high - low)])

    for view, slot, start, count in half_pieces(y, own_hbm, second_hbm, opposite_hbm):
        place(view, slot, start, count, c)
    for slot in range(4):
        place(lambda start, count, slot=slot: other_hbm.at[slot, pl.ds(start, count)], slot, 0, QUARTER, 1 - c)
    loads.start(lall_hbm, lall_ref)

    def put(start, count, dst):
        copy = pltpu.make_async_copy(wide.at[pl.ds(start, count)], dst, os.at[len(stores)])
        copy.start()
        stores.append(copy)

    for index, (shared, experts) in enumerate(((sg, eg), (su, eu), (sd, ed))):
        base = index * HID
        if index == 0:
            for copy in loads.made[:-1]:
                copy.wait()
        for k in range(index * 3, index * 3 + 3):
            for core in range(2):
                wide[pl.ds(k * 256 + core * OWN, OWN), :] = full_ref[core, pl.ds(k * OWN, OWN), :].astype(f32)
        put(base, FS_OWN, shared)
        put(base + 384, FE_OWN, experts.at[0])
        put(base + 384 + FE_OWN, FE_OWN, experts.at[1])
    loads.made[-1].wait()
    for k in range(3):
        for i in range(4):
            block = lall_ref[0, pl.ds(k * 512, 512), i * 128 : i * 128 + 128]
            q_ref[pl.ds(i * 512, 512), k * 128 : k * 128 + 128] = block.astype(f32)
    kv_ref[...] = lall_ref[1, pl.ds(0, KVR), :].astype(f32)
    for i in range(4):
        o_ref[:, i * 512 : i * 512 + 512] = lall_ref[1, pl.ds(512 + i * 256, 256), :].astype(f32)
    for j in range(4):
        down_ref[pl.ds(j * OWN, OWN), :] = pack_ref[:, j * KB : j * KB + KB].astype(f32)
    down_ref[pl.ds(KVR, DR), :] = pack_ref[:DR, 4 * KB :].astype(f32)
    tail = pack_ref[DR : DR + 16, 4 * KB :].astype(f32)
    again_ref[...] = tail[0:1]
    fgain_ref[...] = tail[1:2]
    router_ref[...] = tail[2:4]
    lgain_ref[...] = tail[4:5, :64]
    for copy in stores:
        copy.wait()


def widen(own, second, opposite, other, lall, packs):
    def out(*shape):
        return jax.ShapeDtypeStruct(shape, f32)

    shared, experts = out(FS_OWN, WIDE), out(2, FE_OWN, WIDE)
    return pl.pallas_call(
        widen_kernel,
        out_shape=(
            out(WIDE, QCOLS), out(KVR, 512), out(256, WIDE), out(576, 256),
            out(1, 256), out(1, 256), out(2, 256), out(1, 64), shared, shared, shared, experts, experts, experts,
        ),
        in_specs=[anym()] * 5 + [vmem()],
        out_specs=[vmem()] * 8 + [anym()] * 6,
        scratch_shapes=[
            VMEM((3 * HID, WIDE), f32),
            VMEM((2, BLOCKS * OWN, WIDE), bf16),
            VMEM((2, LATE_HALF, 512), bf16),
            DMA((9,)),
            DMA((27,)),
        ],
        compiler_params=pltpu.CompilerParams(vmem_limit_bytes=60 * MIB),
        cost_estimate=pl.CostEstimate(flops=10**7, bytes_accessed=4 * 10**7, transcendentals=0),
        name="widen",
    )(own, second, opposite, other, lall.reshape(2, LATE_HALF, 512), packs.reshape(OWN, PACK_COLS))


def rope_tables():
    half = DR // 2
    frequency = ROPE_BASE ** (-(np.arange(half, dtype=np.float64) * 2.0) / DR)
    angles = np.arange(LENGTH, dtype=np.float64)[:, None] * frequency[None, :]
    cos = np.cos(angles).astype(np.float32)
    sin = np.sin(angles).astype(np.float32)
    return np.concatenate([cos] * 4, axis=1), np.concatenate([-sin, sin, -sin, sin], axis=1)


def after(value, *others):
    return lax.optimization_barrier((value, *others))[0]


def flat(v):
    return v.reshape(LENGTH, v.shape[-1])


def body(
    layer_in, grad_out, routes, prefix, attn_gain, query_proj, kv_down, latent_gain, kv_up,
    out_proj, ffn_gain, router_proj, shared_gate, shared_up, shared_down, expert_gate, expert_up, expert_down,
):
    cos_np, sin_np = rope_tables()
    cos, sin = jnp.asarray(cos_np), jnp.asarray(sin_np)
    again, lgain, fgain = (v.reshape(-1, 128) for v in (attn_gain, latent_gain, ffn_gain))
    kvd = kv_down.T
    sg, su = shared_gate.T, shared_up.T
    eg, eu = jnp.swapaxes(expert_gate, 1, 2), jnp.swapaxes(expert_up, 1, 2)
    rt = router_proj.T

    (
        normed, q, kvw, kr, lnorm, latent, grad_all, attn, lse, ot, hidden, mixed, m, da, db, p2, gsum
    ) = front(
        prefix, layer_in, grad_out, again, query_proj, kvd, lgain, kv_up, cos, sin, out_proj,
        fgain, routes.reshape(SHARDS, OWN), rt, sg, su, shared_down, eg, eu, expert_down,
    )
    p2 = p2.reshape(SHARDS, OWN, WIDE)
    hgrad, hall, ysum, router_rows, moe = turn_back(
        p2, hidden, grad_out, fgain, mixed, grad_all, m, da, db, shared_down, expert_down
    )
    hall = flat(hall)
    p3, quarters, jq, jk, kvg, tail = attend_back(
        prefix, hall, out_proj, q, kvw, kr, lse, ot, kv_up, latent, lgain, cos, sin, query_proj, kvd,
        normed, again, fgain, gsum, router_rows, ysum,
    )
    input_grad, layer_out, second, opposite, other, lall, packs = last(
        p3, layer_in, hgrad, again, tail, hidden, quarters, moe, normed, hall, jq, jk, kvg, attn, lnorm
    )
    dq, dkv, do, ddown, dag, dfg, drouter, dlg, dsg, dsu, dsd, deg, deu, ded = widen(
        quarters, second, opposite, other, lall, packs
    )
    return (
        layer_out,
        input_grad,
        dag.reshape(256),
        dq,
        ddown.T,
        dlg.reshape(64),
        dkv,
        do,
        dfg.reshape(256),
        drouter.T,
        dsg.T,
        dsu.T,
        dsd,
        jnp.swapaxes(deg, 1, 2),
        jnp.swapaxes(deu, 1, 2),
        ded,
    )


def solution(mesh):
    placed = (
        P(("dp", "tensor"), None),
        P(("dp", "tensor"), None),
        P("dp", None),
        P("dp"),
        P(),
        P(None, "tensor"),
        P(),
        P(),
        P(None, "tensor"),
        P("tensor", None),
        P(),
        P(),
        P(None, "tensor"),
        P(None, "tensor"),
        P("tensor", None),
        P(None, None, "tensor"),
        P(None, None, "tensor"),
        P(None, "tensor", None),
    )
    return jax.shard_map(
        body,
        mesh=mesh,
        in_specs=placed,
        out_specs=(
            P(("dp", "tensor"), None),
            P(("dp", "tensor"), None),
            P("tensor"),
            P(None, "tensor"),
            P("tensor", None),
            P("tensor"),
            P(None, "tensor"),
            P("tensor", None),
            P("tensor"),
            P("tensor", None),
            P(None, "tensor"),
            P(None, "tensor"),
            P("tensor", None),
            P(None, None, "tensor"),
            P(None, None, "tensor"),
            P(None, "tensor", None),
        ),
        check_vma=False,
    )
```

```python
import functools

import jax
import jax.numpy as jnp
import numpy as np
from jax import lax
from jax.experimental import pallas as pl
from jax.experimental.pallas import tpu as pltpu
from jax.sharding import PartitionSpec as P

DN = 128
DR = 64
DV = 128
KVR = 512
EPS = 1e-06
ROPE_BASE = 10000.0
LOG2E = 1.4426950408889634
SCALE = (DN + DR) ** (-0.5)
NEG = -1e30
MIB = 2**20
MESH = pl.DeviceIdType.MESH
f32 = jnp.float32
bf16 = jnp.bfloat16
VMEM = pltpu.VMEM
DMA = pltpu.SemaphoreType.DMA

OWN = 128
SHARDS = 8
LENGTH = OWN * SHARDS
WIDE = 2048
FS_OWN = 352
FE_OWN = 176
HID = 768
QCOLS = 384
LATENT_ROWS = 640


def vmem():
    return pl.BlockSpec(memory_space=pltpu.VMEM)


def anym():
    return pl.BlockSpec(memory_space=pltpu.HBM)


def row(ref):
    v = ref[...].astype(f32)
    return jnp.concatenate([v[i : i + 1] for i in range(v.shape[0])], axis=1)


def dot(a, b):
    return jnp.dot(a, b, preferred_element_type=f32)


def dot_nt(a, b):
    return lax.dot_general(a, b, (((1,), (1,)), ((), ())), preferred_element_type=f32)


def dot_tn(a, b):
    return lax.dot_general(a, b, (((0,), (0,)), ((), ())), preferred_element_type=f32)


def neighbours():
    t = lax.axis_index("tensor")
    x = t // 4
    z = t % 4
    zp = lax.rem(z + 1, 4)
    zm = lax.rem(z + 3, 4)
    z2 = lax.rem(z + 2, 4)
    own = x * 4
    far = (1 - x) * 4
    return dict(
        me=t, tp=own + zp, tm=own + zm, t2=own + z2, tx=far + z, xp=far + zp, xm=far + zm, x2=far + z2
    )


def copies_of():
    d = lax.axis_index("dp")
    c = lax.rem(d, 2)
    y = lax.rem(d // 2, 4)
    plane = d // 8
    here = plane * 8 + c
    return dict(
        c=c, y=y, core=d + 1 - 2 * c, y2=here + lax.rem(y + 2, 4) * 2, yp=here + lax.rem(y + 1, 4) * 2, ym=here + lax.rem(y + 3, 4) * 2,
        xo=(1 - plane) * 8 + y * 2 + c,
    )


def entry_barrier(tensor=(), dp=()):
    sem = pltpu.get_barrier_semaphore()
    for peer in tensor:
        pl.semaphore_signal(sem, inc=1, device_id={"tensor": peer}, device_id_type=MESH)
    for peer in dp:
        pl.semaphore_signal(sem, inc=1, device_id={"dp": peer}, device_id_type=MESH)
    pl.semaphore_wait(sem, len(tensor) + len(dp))


def ring_peers(n):
    return (n["tp"], n["tm"], n["tx"])


class YSum:
    def __init__(self, d, rows, a_ref, base, got, ss, rs, sem):
        self.d, self.rows, self.a, self.base, self.got = d, rows, a_ref, base, got
        self.ss, self.rs, self.sem = ss, rs, sem
        self.pending = None
        self.all = []

    def piece(self, way, hops):
        owner = lax.rem(self.d["y"] + ((3 - hops) if way == 0 else (1 + hops)) + 4, 4)
        start = pl.multiple_of(self.base + (owner * 2 + way) * self.rows, 16)
        return pl.ds(start, self.rows)

    def step(self, s):
        if s:
            for c in self.pending:
                c.wait_recv()
            for way in range(2):
                here = self.piece(way, s)
                self.got[s - 1, way] = added(self.got[s - 1, way], self.a[here, :])
        if s == 3:
            return
        self.pending = []
        for way in range(2):
            src = self.a.at[self.piece(way, 0)] if s == 0 else self.got.at[s - 1, way]
            c = pltpu.make_async_remote_copy(
                src_ref=src,
                dst_ref=self.got.at[s, way],
                send_sem=self.ss.at[self.sem + s * 2 + way],
                recv_sem=self.rs.at[self.sem + s * 2 + way],
                device_id={"dp": self.d["yp"] if way == 0 else self.d["ym"]},
                device_id_type=MESH,
            )
            c.start()
            self.pending.append(c)
            self.all.append(c)

    def close(self):
        for c in self.all:
            c.wait_send()


class YGather:
    def __init__(self, d, rows, g_ref, ss, rs):
        self.d, self.rows, self.g, self.ss, self.rs = d, rows, g_ref, ss, rs
        self.all = []

    def send(self, i, slot, start, count, way):
        view = self.g.at[slot, pl.ds(start, count)]
        copy = dp_copy(view, view, self.ss.at[i], self.rs.at[i], self.d["yp"] if way == 0 else self.d["ym"])
        copy.start()
        self.all.append(copy)

    def step(self, s):
        y = self.d["y"]
        if s == 0:
            self.send(0, y, 0, 2 * self.rows, 0)
            self.send(1, y, 0, 2 * self.rows, 1)
        elif s == 1:
            self.all[0].wait_recv()
            self.send(2, lax.rem(y + 3, 4), 0, self.rows, 0)
            self.all[1].wait_recv()
            self.send(3, lax.rem(y + 1, 4), self.rows, self.rows, 1)
        else:
            self.all[2].wait_recv()
            self.all[3].wait_recv()


def y_spread(d, ref, ss, rs, sem):
    mine = ref.at[d["y"]]
    return [
        dp_copy(mine, mine, ss.at[sem + i], rs.at[sem + i], d[peer]) for i, peer in enumerate(("y2", "yp", "ym"))
    ]


def y_deal(d, ref, rows, got, ss, rs, sem):
    y = d["y"]
    copies = []
    for i, (hops, peer) in enumerate(((2, "y2"), (1, "yp"), (3, "ym"))):
        start = pl.multiple_of(lax.rem(y + hops, 4) * rows, 16)
        src = ref.at[pl.ds(start, rows)]
        copies.append(dp_copy(src, got.at[y], ss.at[sem + i], rs.at[sem + i], d[peer]))
    return copies


def dp_copy(src, dst, ss, rs, peer):
    return pltpu.make_async_remote_copy(
        src_ref=src, dst_ref=dst, send_sem=ss, recv_sem=rs, device_id={"dp": peer}, device_id_type=MESH
    )


def sender(ss, rs):
    def send(i, src, dst, dev):
        return pltpu.make_async_remote_copy(
            src_ref=src,
            dst_ref=dst,
            send_sem=ss.at[i],
            recv_sem=rs.at[i],
            device_id={"tensor": dev},
            device_id_type=MESH,
        )

    return send


def gather_steps(n, x_ref, o_ref, ss, rs):
    send = sender(ss, rs)

    def s(i, src, slot, o, k, dev):
        return send(i, src, o_ref.at[slot, pl.ds(o, k)], dev)

    def part(slot, o, k):
        return o_ref.at[slot, pl.ds(o, k)]

    me, tp, tm, tx, t2, xp, xm, x2 = (n[k] for k in ("me", "tp", "tm", "tx", "t2", "xp", "xm", "x2"))
    s1a = s(0, x_ref.at[pl.ds(0, 64)], me, 0, 64, tp)
    s2a = s(1, x_ref.at[pl.ds(64, 64)], me, 64, 64, tm)
    s3 = s(2, x_ref, me, 0, 128, tx)
    s1b = s(11, x_ref.at[pl.ds(64, 64)], me, 64, 64, tp)
    s2b = s(12, x_ref.at[pl.ds(0, 64)], me, 0, 64, tm)
    for c in (s1a, s2a, s3, s1b, s2b):
        c.start()
    yield me
    s1a.wait_recv()
    s4 = s(3, part(tm, 0, 64), tm, 0, 64, tp)
    s6a = s(5, part(tm, 0, 64), tm, 0, 64, tx)
    s4.start()
    s6a.start()
    s2a.wait_recv()
    s5 = s(4, part(tp, 64, 64), tp, 64, 64, tm)
    s7a = s(6, part(tp, 64, 64), tp, 64, 64, tx)
    s5.start()
    s7a.start()
    s3.wait_recv()
    s8 = s(7, part(tx, 80, 48), tx, 80, 48, tp)
    s9 = s(8, part(tx, 0, 48), tx, 0, 48, tm)
    s8.start()
    s9.start()
    s1b.wait_recv()
    s6b = s(13, part(tm, 64, 16), tm, 64, 16, tx)
    s6b.start()
    s2b.wait_recv()
    s7b = s(14, part(tp, 48, 16), tp, 48, 16, tx)
    s7b.start()
    yield tm
    s6a.wait_recv()
    s10 = s(9, part(xm, 0, 64), xm, 0, 64, tp)
    s10.start()
    s7a.wait_recv()
    s11 = s(10, part(xp, 64, 64), xp, 64, 64, tm)
    s11.start()
    yield tp
    yield tx
    s4.wait_recv()
    s5.wait_recv()
    yield t2
    s8.wait_recv()
    s6b.wait_recv()
    yield xm
    s9.wait_recv()
    s7b.wait_recv()
    yield xp
    s10.wait_recv()
    s11.wait_recv()
    yield x2
    for c in (s1a, s1b, s2a, s2b, s3, s4, s5, s6a, s6b, s7a, s7b, s8, s9, s10, s11):
        c.wait_send()


def gather_ring(n, x_ref, o_ref, ss, rs, on_shard=None):
    for slot in gather_steps(n, x_ref, o_ref, ss, rs):
        if on_shard:
            on_shard(slot)


def reduce_steps(n, pv, ready, bufs, ss, rs):
    send = sender(ss, rs)
    me, tp, tm, tx, t2, xp, xm, x2 = (n[k] for k in ("me", "tp", "tm", "tx", "t2", "xp", "xm", "x2"))
    r10, r11, r8, r9, r6, r7, r4, r5, m1, m2, m3 = bufs

    def s(i, slot, o, k, dst, dev):
        return send(i, pv.at[slot, pl.ds(o, k)], dst, dev)

    def add(slot, o, k, buf):
        pv[slot, pl.ds(o, k)] = added(pv[slot, pl.ds(o, k)], buf[...])

    ready("x2")
    s10 = s(0, x2, 0, 64, r10, tm)
    s11 = s(1, x2, 64, 64, r11, tp)
    s10.start()
    s11.start()
    ready("tx")
    s3b = s(10, tx, 48, 32, m3.at[pl.ds(48, 32)], tx)
    s3b.start()
    ready("xm")
    ready("xp")
    s6b = s(15, xm, 64, 16, r6.at[pl.ds(64, 16)], tx)
    s7b = s(16, xp, 48, 16, r7.at[pl.ds(0, 16)], tx)
    s6b.start()
    s7b.start()
    ready("t2")
    s4 = s(2, t2, 0, 64, r4, tm)
    s5 = s(3, t2, 64, 64, r5, tp)
    s4.start()
    s5.start()
    s8 = s(4, xm, 80, 48, r8, tm)
    s9 = s(5, xp, 0, 48, r9, tp)
    s8.start()
    s9.start()
    ready("tm")
    ready("tp")
    s1b = s(11, tm, 80, 48, m1.at[pl.ds(80, 48)], tm)
    s2b = s(12, tp, 0, 48, m2.at[pl.ds(0, 48)], tp)
    s1b.start()
    s2b.start()
    yield
    s10.wait_recv()
    add(xm, 0, 64, r10)
    s6 = s(6, xm, 0, 64, r6.at[pl.ds(0, 64)], tx)
    s6.start()
    s11.wait_recv()
    add(xp, 64, 64, r11)
    s7 = s(7, xp, 64, 64, r7.at[pl.ds(16, 64)], tx)
    s7.start()
    yield
    s8.wait_recv()
    add(tx, 80, 48, r8)
    s9.wait_recv()
    add(tx, 0, 48, r9)
    s3a = s(13, tx, 80, 48, m3.at[pl.ds(80, 48)], tx)
    s3c = s(14, tx, 0, 48, m3.at[pl.ds(0, 48)], tx)
    s3a.start()
    s3c.start()
    yield
    s4.wait_recv()
    add(tm, 0, 64, r4)
    s6.wait_recv()
    s6b.wait_recv()
    add(tm, 0, 80, r6)
    s1 = s(8, tm, 0, 80, m1.at[pl.ds(0, 80)], tm)
    s1.start()
    yield
    s5.wait_recv()
    add(tp, 64, 64, r5)
    s7.wait_recv()
    s7b.wait_recv()
    add(tp, 48, 80, r7)
    s2 = s(9, tp, 48, 80, m2.at[pl.ds(48, 80)], tp)
    s2.start()
    yield
    ready("me")
    for c in (s3a, s3b, s3c, s1b, s2b, s1, s2):
        c.wait_recv()
    for c in (s1, s1b, s2, s2b, s3a, s3b, s3c, s4, s5, s6, s6b, s7, s7b, s8, s9, s10, s11):
        c.wait_send()


def reduce_ring(n, pv, ready, bufs, ss, rs, work=None):
    for point, _ in enumerate(reduce_steps(n, pv, ready, bufs, ss, rs)):
        if work:
            work(point)


def reduce_scratch(columns):
    rows = (64, 64, 48, 48, 80, 80, 64, 64, 128, 128, 128)
    return [VMEM((r, columns), bf16) for r in rows]


def added(a, b):
    return (a.astype(f32) + b.astype(f32)).astype(bf16)


def load_partials(n, p_ref, pv, ls):
    order = ("x2", "tx", "xm", "xp", "t2", "tm", "tp", "me")
    copies = {}
    for i, name in enumerate(order):
        copies[name] = pltpu.make_async_copy(p_ref.at[n[name]], pv.at[n[name]], ls.at[i])
        copies[name].start()
    return lambda name: copies[name].wait()


def inverse_rms(v):
    return lax.rsqrt(jnp.mean(v * v, axis=-1, keepdims=True) + EPS)


class Copies:
    def __init__(self, sems):
        self.sems, self.made = sems, []

    def start(self, src, dst):
        copy = pltpu.make_async_copy(src, dst, self.sems.at[len(self.made)])
        copy.start()
        self.made.append(copy)
        return copy

    def close(self):
        for copy in self.made:
            copy.wait()


def turn(v, cos, sin):
    lane = lax.broadcasted_iota(jnp.int32, v.shape, 1)
    low = lax.rem(lane, 64) < 32
    swapped = jnp.where(low, pltpu.roll(v, 96, 1), pltpu.roll(v, 32, 1))
    return v * cos + swapped * sin


def fetch_latent_weights(kvd_hbm, kvd_ref, sems):
    copies = [
        pltpu.make_async_copy(kvd_hbm, kvd_ref.at[pl.ds(0, KVR + DR)], sems.at[0]),
        pltpu.make_async_copy(kvd_hbm.at[pl.ds(KVR, DR)], kvd_ref.at[pl.ds(KVR + DR, DR)], sems.at[1]),
    ]
    for c in copies:
        c.start()
    return copies


KB = 256


def masked(s, key0, query0, prefix):
    keys = key0 + lax.broadcasted_iota(jnp.int32, s.shape, 0)
    rows = query0 + lax.broadcasted_iota(jnp.int32, s.shape, 1)
    return jnp.where((keys <= rows) | (keys < prefix), s, NEG)


def key_extent(query_block):
    return max(2, query_block + 1)


def head_lanes(shape, head):
    lane = lax.broadcasted_iota(jnp.int32, shape, 1)
    return (lane >= 64) if head else (lane < 64)


def head_query(q_ref, rows, head):
    rope = q_ref[rows, 256:QCOLS]
    rope = jnp.where(head_lanes(rope.shape, head), rope.astype(f32), 0.0).astype(bf16)
    return jnp.concatenate([q_ref[rows, head * 128 : head * 128 + 128], rope], axis=1)


def head_key(kvw_ref, kr_ref, rows, head):
    return jnp.concatenate([kvw_ref[rows, head * 256 : head * 256 + 128], kr_ref[rows, :]], axis=1)


def attention(prefix, q_ref, kvw_ref, kr_ref, wo_ref, attn_ref, lse_ref, ot_ref, s_scr, put):
    for i in range(4):
        rows = pl.ds(i * KB, KB)
        for h in range(2):
            q = head_query(q_ref, rows, h)
            top = jnp.full((1, KB), NEG, f32)
            for k in range(key_extent(i)):
                keys = pl.ds(k * KB, KB)
                s = dot_nt(head_key(kvw_ref, kr_ref, keys, h), q)
                if k >= i:
                    s = masked(s, k * KB, i * KB, prefix)
                s_scr[keys, :] = s
                top = jnp.maximum(top, jnp.max(s, axis=0, keepdims=True))
            top = top * (SCALE * LOG2E)
            total = jnp.zeros((1, KB), f32)
            out = jnp.zeros((DV, KB), f32)
            for k in range(key_extent(i)):
                keys = pl.ds(k * KB, KB)
                p = jnp.exp2(s_scr[keys, :] * (SCALE * LOG2E) - top)
                total = total + jnp.sum(p, axis=0, keepdims=True)
                out = out + dot_tn(kvw_ref[keys, h * 256 + 128 : h * 256 + 256], p.astype(bf16))
            out = out / total
            lse_ref[h : h + 1, rows] = top + jnp.log2(total)
            ot_ref[h, :, rows] = out
            attn_ref[rows, h * 128 : h * 128 + 128] = out.T.astype(bf16)
        put(i, dot(attn_ref[rows, :], wo_ref[...]).astype(bf16))


def own_total(n, pv, bufs):
    m1, m2, m3 = bufs[8:]
    return pv[n["me"]].astype(f32) + m1[...].astype(f32) + m2[...].astype(f32) + m3[...].astype(f32)


def fetch_hidden_weights(sg, eg, dst, zero_ref, sems, base):
    pieces = [(sg, 0, FS_OWN), (eg.at[0], 384, FE_OWN), (eg.at[1], 384 + FE_OWN, FE_OWN)]
    pieces += [(zero_ref, 736, 32), (zero_ref, FS_OWN, 32)]
    copies = []
    for i, (src, at, count) in enumerate(pieces):
        c = pltpu.make_async_copy(src, dst.at[pl.ds(at, count)], sems.at[base + i])
        c.start()
        copies.append(c)
    return copies


def ffn_rows(mixed, dm, route, wg_ref, wu_ref):
    a = dot_nt(mixed, wg_ref[...])
    b = dot_nt(mixed, wu_ref[...])
    first = (route == 0.0).astype(f32)
    second = (route == 1.0).astype(f32)
    l0 = a[:, FS_OWN : FS_OWN + 1]
    l1 = a[:, FS_OWN + 1 : FS_OWN + 2]
    top = jnp.maximum(l0, l1)
    e0 = jnp.exp(l0 - top)
    e1 = jnp.exp(l1 - top)
    r0 = e0 / (e0 + e1)
    r1 = e1 / (e0 + e1)
    col = lax.broadcasted_iota(jnp.int32, (1, HID), 1)
    is_shared = col < 384
    in0 = (col >= 384) & (col < 384 + FE_OWN)
    in1 = (col >= 384 + FE_OWN) & (col < 384 + 2 * FE_OWN)
    gate = jnp.where(is_shared, 1.0, 0.0) + jnp.where(in0, first * r0, 0.0) + jnp.where(in1, second * r1, 0.0)
    sig = jax.nn.sigmoid(a)
    silu = a * sig
    act = silu * b
    m = (gate * act).astype(bf16)
    scaled = dm * gate
    down = dm * act
    g0 = first * jnp.sum(jnp.where(in0, down, 0.0), axis=1, keepdims=True)
    g1 = second * jnp.sum(jnp.where(in1, down, 0.0), axis=1, keepdims=True)
    mean = r0 * g0 + r1 * g1
    da = scaled * b * (sig * (1.0 + a * (1.0 - sig)))
    da = da + jnp.where(col == FS_OWN, r0 * (g0 - mean), 0.0) + jnp.where(col == FS_OWN + 1, r1 * (g1 - mean), 0.0)
    da = da.astype(bf16)
    db = (scaled * silu).astype(bf16)
    return m, da, db, dot(da, wg_ref[...]) + dot(db, wu_ref[...])


def front_kernel(
    prefix_ref, x_hbm, grad_hbm, gain_ref, wq_hbm, kvd_hbm, lgain_ref, kvup_hbm, cos_hbm, sin_hbm, wo_hbm,
    fgain_ref, routes_ref, rt_ref, sg, su, sd, eg, eu, ed,
    normed_out, q_out, kvw_out, kr_out, lnorm_out, latent_out, gall_out, attn_out, lse_out, ot_out,
    hidden_ref, mixed_out, m_out, da_out, db_out, p2_out, gsum_ref,
    xall, wq_ref, kvd_ref, normed_ref, q_ref, kvw_ref, kr_ref, lnorm_ref, latent_ref, x_ref, kvup_ref,
    cos_ref, sin_ref, wo_ref, gall, attn_ref, lse_ref, ot_ref, s_scr,
    mixed_ref, m_ref, da_ref, db_ref, own, dm_scr, wg_ref, wu_ref, wd_ref, zero_ref, *rest,
):
    bufs, (xs, xr, gs, gr, ss, rs, ms, mr, ls, hs, ws, es, os) = rest[:11], rest[11:]
    n = neighbours()
    me = n["me"]
    prefix = prefix_ref[0]
    loads = Copies(hs)
    early = Copies(es)
    zero_ref[...] = jnp.zeros_like(zero_ref)
    entry_barrier(ring_peers(n))

    def shard_rows(slot):
        return pl.ds(pl.multiple_of(slot * OWN, OWN), OWN)

    def compute(slot, src):
        x = src.astype(f32)
        rows = shard_rows(slot)
        normed = (x * inverse_rms(x) * row(gain_ref)).astype(bf16)
        normed_ref[rows, :] = normed
        raw = dot(normed, wq_ref[...])
        cos = cos_ref[rows, :]
        sin = sin_ref[rows, :]
        q_ref[rows, :128] = raw[:, :128].astype(bf16)
        q_ref[rows, 128:256] = raw[:, 192:320].astype(bf16)
        rope = jnp.concatenate([raw[:, 128:192], raw[:, 320:384]], axis=1)
        q_ref[rows, 256:] = turn(rope, cos, sin).astype(bf16)
        raw = dot_nt(normed, kvd_ref[...])
        latent = raw[:, :KVR]
        latent_ref[rows, :] = latent
        lnorm = (latent * inverse_rms(latent) * row(lgain_ref)).astype(bf16)
        lnorm_ref[rows, :] = lnorm
        kr_ref[rows, :] = turn(raw[:, KVR:], cos, sin).astype(bf16)
        kvw_ref[rows, :] = dot(lnorm, kvup_ref[...]).astype(bf16)
        early.start(normed_ref.at[rows], normed_out.at[rows])

    second = gather_steps(n, grad_hbm, gall, gs, gr)
    for k, slot in enumerate(gather_steps(n, x_hbm, xall, xs, xr)):
        if k == 0:
            loads.start(x_hbm, x_ref)
            loads.start(wq_hbm, wq_ref)
            copies = fetch_latent_weights(kvd_hbm, kvd_ref, ls)
            for src, dst in ((kvup_hbm, kvup_ref), (cos_hbm, cos_ref), (sin_hbm, sin_ref)):
                loads.start(src, dst)
            loads.start(wo_hbm, wo_ref)
            loads.start(grad_hbm, gall.at[me])
            loads.close()
            for c in copies:
                c.wait()
            weights = fetch_hidden_weights(sd, ed, wd_ref, zero_ref, ws, 0)
            weights += fetch_hidden_weights(sg, eg, wg_ref, zero_ref, ws, 5)
            weights += fetch_hidden_weights(su, eu, wu_ref, zero_ref, ws, 10)
            compute(slot, x_ref[...])
            continue
        if k in (1, 4):
            next(second)
        compute(slot, xall[slot])
    for src, dst in (
        (q_ref, q_out), (kvw_ref, kvw_out), (kr_ref, kr_out), (lnorm_ref, lnorm_out), (latent_ref, latent_out)
    ):
        early.start(src, dst)

    def put(i, block):
        for t in range(2):
            xall[i * 2 + t] = block[t * OWN : t * OWN + OWN]

    next(second)
    attention(prefix, q_ref, kvw_ref, kr_ref, wo_ref, attn_ref, lse_ref, ot_ref, s_scr, put)
    for src, dst in ((attn_ref, attn_out), (lse_ref, lse_out), (ot_ref, ot_out)):
        early.start(src, dst)

    def dm_pair(k):
        two = pl.ds(k * 2, 2)
        dm_scr[two] = dot_nt(gall[two].reshape(256, WIDE), wd_ref[...]).reshape(2, OWN, HID)

    def work(point):
        if point == 1:
            for _ in second:
                pass
            early.start(gall, gall_out)
            for c in weights[:5]:
                c.wait()
            dm_pair(0)
        elif point == 2:
            dm_pair(1)
        elif point == 3:
            dm_pair(2)
        elif point == 4:
            dm_pair(3)
            for c in weights[5:]:
                c.wait()
            router = jnp.concatenate([rt_ref[...].astype(f32), jnp.zeros((30, WIDE), f32)], axis=0)
            wg_ref[pl.ds(FS_OWN, 32), :] = router.astype(bf16)

    reduce_ring(n, xall, lambda name: None, bufs, ss, rs, work)
    hidden = x_ref[...].astype(f32) + own_total(n, xall, bufs)
    hidden_ref[...] = hidden
    own[...] = (hidden * inverse_rms(hidden) * row(fgain_ref)).astype(bf16)
    mixed_ref[me] = own[...]
    gsum_ref[...] = jnp.zeros_like(gsum_ref)
    waiting = []
    by_token = routes_ref[...].astype(f32).T
    early.close()
    stores = Copies(os)

    def on_shard(slot):
        waiting.append(slot)
        if len(waiting) < 2:
            return
        pair = list(waiting)
        waiting.clear()
        mixed = jnp.concatenate([mixed_ref[s] for s in pair], axis=0)
        dm = jnp.concatenate([dm_scr[s] for s in pair], axis=0)
        shard = lax.broadcasted_iota(jnp.int32, (OWN, SHARDS), 1)
        route = jnp.concatenate(
            [jnp.sum(jnp.where(shard == s, by_token, 0.0), axis=1, keepdims=True) for s in pair], axis=0
        )
        m, da, db, back = ffn_rows(mixed, dm, route, wg_ref, wu_ref)
        gsum_ref[...] += jnp.sum(back * mixed.astype(f32), axis=0, keepdims=True)
        back = back.astype(bf16)
        for i, s in enumerate(pair):
            part = slice(i * OWN, i * OWN + OWN)
            rows = shard_rows(s)
            m_ref[s] = m[part]
            da_ref[s] = da[part]
            db_ref[s] = db[part]
            normed_ref[rows, :] = back[part]
            for src, dst in ((mixed_ref, mixed_out), (m_ref, m_out), (da_ref, da_out), (db_ref, db_out)):
                stores.start(src.at[s], dst.at[s])
            stores.start(normed_ref.at[rows], p2_out.at[rows])

    gather_ring(n, own, mixed_ref, ms, mr, on_shard)
    stores.close()


def front(prefix, x, grad, gain, wq, kvd, lgain, kvup, cos, sin, wo, fgain, routes, rt, sg, su, sd, eg, eu, ed):
    def rows(c, t=bf16):
        return jax.ShapeDtypeStruct((LENGTH, c), t)

    def shards(c):
        return jax.ShapeDtypeStruct((SHARDS, OWN, c), bf16)

    def other(*shape):
        return jax.ShapeDtypeStruct(shape, f32)

    return pl.pallas_call(
        front_kernel,
        out_shape=(
            rows(WIDE), rows(QCOLS), rows(512), rows(128), rows(KVR), rows(KVR, f32), shards(WIDE), rows(256),
            other(2, LENGTH), other(2, DV, LENGTH), other(OWN, WIDE),
            shards(WIDE), shards(HID), shards(HID), shards(HID), rows(WIDE), other(1, WIDE),
        ),
        in_specs=[pl.BlockSpec(memory_space=pltpu.SMEM), anym(), anym(), vmem(), anym(), anym(), vmem()]
        + [anym()] * 4
        + [vmem()] * 3
        + [anym()] * 6,
        out_specs=[anym()] * 10 + [vmem()] + [anym()] * 5 + [vmem()],
        scratch_shapes=[
            VMEM((SHARDS, OWN, WIDE), bf16),
            VMEM((WIDE, QCOLS), bf16),
            VMEM((LATENT_ROWS, WIDE), bf16),
            VMEM((LENGTH, WIDE), bf16),
            VMEM((LENGTH, QCOLS), bf16),
            VMEM((LENGTH, 512), bf16),
            VMEM((LENGTH, 128), bf16),
            VMEM((LENGTH, KVR), bf16),
            VMEM((LENGTH, KVR), f32),
            VMEM((OWN, WIDE), bf16),
            VMEM((KVR, 512), bf16),
            VMEM((LENGTH, 128), f32),
            VMEM((LENGTH, 128), f32),
            VMEM((256, WIDE), bf16),
            VMEM((SHARDS, OWN, WIDE), bf16),
            VMEM((LENGTH, 256), bf16),
            VMEM((2, LENGTH), f32),
            VMEM((2, DV, LENGTH), f32),
            VMEM((LENGTH, KB), f32),
            VMEM((SHARDS, OWN, WIDE), bf16),
            VMEM((SHARDS, OWN, HID), bf16),
            VMEM((SHARDS, OWN, HID), bf16),
            VMEM((SHARDS, OWN, HID), bf16),
            VMEM((OWN, WIDE), bf16),
            VMEM((SHARDS, OWN, HID), f32),
            VMEM((HID, WIDE), bf16),
            VMEM((HID, WIDE), bf16),
            VMEM((HID, WIDE), bf16),
            VMEM((32, WIDE), bf16),
        ]
        + reduce_scratch(WIDE)
        + [DMA((17,))] * 8
        + [DMA((2,)), DMA((7,)), DMA((15,)), DMA((17,)), DMA((40,))],
        compiler_params=pltpu.CompilerParams(
            collective_id=0, has_side_effects=True, vmem_limit_bytes=62 * MIB
        ),
        cost_estimate=pl.CostEstimate(flops=25 * 10**9, bytes_accessed=5 * 10**7, transcendentals=3 * 10**6),
        name="front",
    )(prefix, x, grad, gain, wq, kvd, lgain, kvup, cos, sin, wo, fgain, routes, rt, sg, su, sd, eg, eu, ed)


def rows_of(ref):
    return ref[...].reshape(LENGTH, ref.shape[-1])


BLOCKS = 9


QUARTER = 288


def turn_kernel(
    p_ref, hidden_ref, grad_ref, gain_ref, mixed_hbm, gall_hbm, m_hbm, da_hbm, db_hbm, sd, ed,
    hgrad_ref, hall_ref, sum_ref, router_ref, moe_hbm,
    mixed_ref, gall_ref, m_ref, da_ref, db_ref, half_ref, hs, pv, low, dw_scr, core_scr, moe_scr, wd_ref, zero_ref,
    got, *rest,
):
    bufs, (ss, rs, gs, gr, cs, cr, ys, yr, ls, ws, os) = rest[:11], rest[11:]
    n = neighbours()
    d = copies_of()
    ready = load_partials(n, p_ref, pv, ls)
    zero_ref[...] = jnp.zeros_like(zero_ref)
    loads = Copies(hs)
    copies = []
    entry_barrier(ring_peers(n), (d["core"], d["yp"], d["ym"]))
    stores = Copies(os)
    crossed = []
    sent = []
    theirs = pl.multiple_of((1 - d["c"]) * OWN, OWN)
    mine = pl.multiple_of(d["c"] * OWN, OWN)
    sums = [YSum(d, 48, half_ref, 384 * k, got.at[k], ys, yr, 6 * k) for k in range(3)]

    def product(index, left, right, block):
        k = index * 3 + block
        if block == 0:
            for c in {2: loads.made[:2], 0: loads.made[2:4], 1: loads.made[4:]}[index]:
                c.wait()
        left = left[:, :, pl.ds(block * 256, 256)].reshape(LENGTH, 256)
        dw_scr[k] = dot_tn(left, rows_of(right)).astype(bf16)
        c = dp_copy(dw_scr.at[k, pl.ds(theirs, OWN)], core_scr.at[k], cs.at[k], cr.at[k], d["core"])
        c.start()
        crossed.append((k, c))
        if k == 1:
            router_ref[...] = dw_scr[1, FS_OWN - 256 : FS_OWN - 240, :]

    def expert_sum(block):
        two = pl.ds(block * 2, 2)
        moe_scr[two] = dot(m_ref[two].reshape(256, HID), wd_ref[...]).astype(bf16).reshape(2, OWN, WIDE)
        stores.start(moe_scr.at[two], moe_hbm.at[two])

    def meet():
        k, c = crossed.pop(0)
        c.wait_recv()
        half_ref[pl.ds(k * OWN, OWN), :] = added(dw_scr[k, pl.ds(mine, OWN), :], core_scr[k])
        sent.append(c)

    jobs = [functools.partial(product, 2, m_ref, gall_ref, b) for b in range(3)]
    jobs += [functools.partial(product, 0, da_ref, mixed_ref, b) for b in range(3)]
    jobs += [functools.partial(product, 1, db_ref, mixed_ref, b) for b in range(3)]
    plan = {0: 3, 1: 2, 2: 2, 3: 1, 4: 1}

    def work(point):
        if point == 0:
            for src, dst in (
                (m_hbm, m_ref), (gall_hbm, gall_ref), (da_hbm, da_ref), (mixed_hbm, mixed_ref), (db_hbm, db_ref)
            ):
                loads.start(src, dst)
            copies.extend(fetch_hidden_weights(sd, ed, wd_ref, zero_ref, ws, 0))
        if point == 1:
            meet_all(2)
        for _ in range(plan[point]):
            jobs.pop(0)()
        if point == 2:
            while len(crossed) > 1:
                meet()
            sums[0].step(0)
        elif point == 3:
            sums[2].step(1)
        elif point == 4:
            meet_all(1)

    def meet_all(part):
        while crossed:
            meet()
        sums[part].step(0)

    reduce_ring(n, pv, ready, bufs, ss, rs, work)
    total = own_total(n, pv, bufs)
    hidden = hidden_ref[...]
    inv = inverse_rms(hidden)
    unit = hidden * inv
    scaled = total * row(gain_ref)
    back = inv * (scaled - unit * jnp.mean(scaled * unit, axis=-1, keepdims=True))
    hgrad = grad_ref[...].astype(f32) + back
    hgrad_ref[...] = hgrad
    low[...] = hgrad.astype(bf16)
    for k, _ in enumerate(gather_steps(n, low, hall_ref, gs, gr)):
        if k == 0:
            stores.start(low, hall_ref.at[n["me"]])
            for c in copies:
                c.wait()
            expert_sum(0)
            expert_sum(1)
            sums[2].step(2)
            sums[0].step(1)
        elif k == 1:
            sums[1].step(1)
            expert_sum(2)
            expert_sum(3)
            sums[0].step(2)
        elif k == 3:
            sums[1].step(2)
            sums[2].step(3)
        elif k == 5:
            sums[0].step(3)
    sums[1].step(3)
    for k in range(3):
        for way in range(2):
            sum_ref[pl.ds(k * 96 + way * 48, 48), :] = got[k, 2, way]
        sums[k].close()
    stores.close()
    for c in sent:
        c.wait_send()


def turn_back(p, hidden, grad, gain, mixed, gall, m, da, db, sd, ed):
    outs = (
        jax.ShapeDtypeStruct((OWN, WIDE), f32),
        jax.ShapeDtypeStruct((SHARDS, OWN, WIDE), bf16),
        jax.ShapeDtypeStruct((QUARTER, WIDE), bf16),
        jax.ShapeDtypeStruct((16, WIDE), bf16),
        jax.ShapeDtypeStruct((SHARDS, OWN, WIDE), bf16),
    )
    return pl.pallas_call(
        turn_kernel,
        out_shape=outs,
        in_specs=[anym()] + [vmem()] * 3 + [anym()] * 7,
        out_specs=[vmem(), anym(), vmem(), vmem(), anym()],
        scratch_shapes=[
            VMEM((SHARDS, OWN, WIDE), bf16),
            VMEM((SHARDS, OWN, WIDE), bf16),
            VMEM((SHARDS, OWN, HID), bf16),
            VMEM((SHARDS, OWN, HID), bf16),
            VMEM((SHARDS, OWN, HID), bf16),
            VMEM((BLOCKS * OWN, WIDE), bf16),
            DMA((5,)),
            VMEM((SHARDS, OWN, WIDE), bf16),
            VMEM((OWN, WIDE), bf16),
            VMEM((BLOCKS, 256, WIDE), bf16),
            VMEM((BLOCKS, OWN, WIDE), bf16),
            VMEM((SHARDS, OWN, WIDE), bf16),
            VMEM((HID, WIDE), bf16),
            VMEM((32, WIDE), bf16),
            VMEM((3, 3, 2, 48, WIDE), bf16),
        ]
        + reduce_scratch(WIDE)
        + [DMA((17,))] * 4
        + [DMA((BLOCKS,)), DMA((BLOCKS,)), DMA((18,)), DMA((18,)), DMA((8,)), DMA((5,)), DMA((5,))],
        compiler_params=pltpu.CompilerParams(
            collective_id=2, has_side_effects=True, vmem_limit_bytes=60 * MIB
        ),
        cost_estimate=pl.CostEstimate(flops=13 * 10**9, bytes_accessed=4 * 10**7, transcendentals=0),
        name="turn_back",
    )(p, hidden, grad, gain, mixed, gall, m, da, db, sd, ed)


LATE = 3072
PACK_COLS = 1280


def attend_back_kernel(
    prefix_ref, hall_hbm, wo_ref, q_ref, kvw_ref, kr_ref, lse_ref, ot_ref,
    kvup_ref, latent_hbm, lgain_ref, cos_ref, sin_ref, wq_hbm, kvd_hbm,
    normed_hbm, gain_ref, fgain_ref, gsum_ref, router_ref, ysum_ref,
    p_out, all_ref, jq_out, jk_out, kvg_out, tail_ref,
    hall_ref, latent_ref, wq_ref, normed_ref, p_ref, hs, os, do_scr, dk_scr, dv_scr, jq_scr, jk_scr, kvg_scr, kvd_ref, far_scr, quarter, ls, xs, xr, ys, yr,
):
    prefix = prefix_ref[0]
    d = copies_of()
    loads = Copies(hs)
    for i in range(4):
        loads.start(hall_hbm.at[pl.ds(i * KB, KB)], hall_ref.at[pl.ds(i * KB, KB)])
    for src, dst in ((latent_hbm, latent_ref), (wq_hbm, wq_ref), (normed_hbm, normed_ref)):
        loads.start(src, dst)
    stores = Copies(os)
    entry_barrier((), (d["xo"], d["yp"], d["ym"]))
    half = QUARTER // 2
    parts = [pl.ds(0, half), pl.ds(half, half)]
    crosses = [dp_copy(ysum_ref.at[r], far_scr.at[r], xs.at[k], xr.at[k], d["xo"]) for k, r in enumerate(parts)]
    for cross in crosses:
        cross.start()
    spread = []

    def meet(k):
        crosses[k].wait_recv()
        quarter[parts[k], :] = added(ysum_ref[parts[k], :], far_scr[parts[k], :])
        if k == 0:
            for i, peer in enumerate((d["yp"], d["ym"])):
                copy = dp_copy(quarter.at[parts[k]], all_ref.at[d["y"], parts[k]], ys.at[i], yr.at[i], peer)
                copy.start()
                spread.append(copy)
        stores.start(quarter.at[parts[k]], all_ref.at[d["y"], parts[k]])

    copies = fetch_latent_weights(kvd_hbm, kvd_ref, ls)
    for i in range(4):
        rows = pl.ds(i * KB, KB)
        loads.made[i].wait()
        do_scr[rows, :] = dot_nt(hall_ref[rows, :], wo_ref[...]).astype(bf16)
    dk_scr[...] = jnp.zeros_like(dk_scr)
    dv_scr[...] = jnp.zeros_like(dv_scr)
    for i in range(4):
        rows = pl.ds(i * KB, KB)
        plain = []
        turned = jnp.zeros((KB, 128), f32)
        for h in range(2):
            q = head_query(q_ref, rows, h)
            do = do_scr[rows, h * 128 : h * 128 + 128]
            lse = lse_ref[h : h + 1, rows]
            delta = jnp.sum(do.astype(f32).T * ot_ref[h, :, rows], axis=0, keepdims=True)
            dq = jnp.zeros((KB, 256), f32)
            for k in range(key_extent(i)):
                keys = pl.ds(k * KB, KB)
                key = head_key(kvw_ref, kr_ref, keys, h)
                s = dot_nt(key, q)
                if k >= i:
                    s = masked(s, k * KB, i * KB, prefix)
                p = jnp.exp2(s * (SCALE * LOG2E) - lse)
                dp = dot_nt(kvw_ref[keys, h * 256 + 128 : h * 256 + 256], do)
                ds = (p * (dp - delta)).astype(bf16)
                dv_scr[h, keys, :] += dot(p.astype(bf16), do)
                dk_scr[h, keys, :] += dot(ds, q)
                dq = dq + dot_tn(ds, key)
            dq = dq * SCALE
            plain.append(dq[:, :128])
            turned = turned + jnp.where(head_lanes(turned.shape, h), dq[:, 128:], 0.0)
        turned = turn(turned, cos_ref[rows, :], -sin_ref[rows, :])
        j = jnp.concatenate([plain[0], turned[:, :64], plain[1], turned[:, 64:]], axis=1)
        jq_scr[rows, :] = j.astype(bf16)
    meet(0)
    for c in copies + loads.made[4:]:
        c.wait()
    gain_sum = jnp.zeros((1, WIDE), f32)
    lgain_sum = jnp.zeros((1, KVR), f32)
    for i in range(4):
        rows = pl.ds(i * KB, KB)
        for h in range(2):
            kvg_scr[rows, h * 256 : h * 256 + 128] = (dk_scr[h, rows, :128] * SCALE).astype(bf16)
            kvg_scr[rows, h * 256 + 128 : h * 256 + 256] = dv_scr[h, rows, :].astype(bf16)
        dkr = (dk_scr[0, rows, 128:] + dk_scr[1, rows, 128:]) * SCALE
        jk_scr[rows, KVR:] = turn(dkr, cos_ref[rows, :], -sin_ref[rows, :]).astype(bf16)
        dl = dot_nt(kvg_scr[rows, :], kvup_ref[...])
        latent = latent_ref[rows, :]
        inv = inverse_rms(latent)
        unit = latent * inv
        lgain_sum = lgain_sum + jnp.sum(dl * unit, axis=0, keepdims=True)
        scaled = dl * row(lgain_ref)
        back = inv * (scaled - unit * jnp.mean(scaled * unit, axis=-1, keepdims=True))
        jk_scr[rows, :KVR] = back.astype(bf16)
        into = dot_nt(jq_scr[rows, :], wq_ref[...]) + dot(jk_scr[rows, :], kvd_ref[...])
        gain_sum = gain_sum + jnp.sum(into * normed_ref[rows, :].astype(f32), axis=0, keepdims=True)
        into = into.astype(bf16)
        for t in range(2):
            p_ref[i * 2 + t] = into[t * OWN : t * OWN + OWN]
        stores.start(p_ref.at[pl.ds(i * 2, 2)], p_out.at[pl.ds(i * 2, 2)])
        for src, dst in ((jq_scr, jq_out), (jk_scr, jk_out), (kvg_scr, kvg_out)):
            stores.start(src.at[rows], dst.at[rows])
    empty = jnp.zeros((1, 192), f32)
    lat = jnp.concatenate([v for t in range(SHARDS) for v in (lgain_sum[:, t * 64 : t * 64 + 64], empty)], axis=1)
    tail_ref[...] = jnp.concatenate(
        [
            gain_sum / row(gain_ref),
            gsum_ref[...] / row(fgain_ref),
            router_ref[:2, :].astype(f32),
            lat,
            jnp.zeros((3, WIDE), f32),
        ],
        axis=0,
    )
    meet(1)
    for copy in spread:
        copy.wait()
    for cross in crosses:
        cross.wait_send()
    stores.close()


def attend_back(*args):
    return pl.pallas_call(
        attend_back_kernel,
        out_shape=(
            jax.ShapeDtypeStruct((SHARDS, OWN, WIDE), bf16),
            jax.ShapeDtypeStruct((4, QUARTER, WIDE), bf16),
            jax.ShapeDtypeStruct((LENGTH, QCOLS), bf16),
            jax.ShapeDtypeStruct((LENGTH, LATENT_ROWS), bf16),
            jax.ShapeDtypeStruct((LENGTH, 512), bf16),
            jax.ShapeDtypeStruct((8, WIDE), f32),
        ),
        in_specs=[pl.BlockSpec(memory_space=pltpu.SMEM), anym()]
        + [vmem()] * 7
        + [anym()]
        + [vmem()] * 3
        + [anym()] * 3
        + [vmem()] * 5,
        out_specs=[anym()] * 5 + [vmem()],
        scratch_shapes=[
            VMEM((LENGTH, WIDE), bf16),
            VMEM((LENGTH, KVR), f32),
            VMEM((WIDE, QCOLS), bf16),
            VMEM((LENGTH, WIDE), bf16),
            VMEM((SHARDS, OWN, WIDE), bf16),
            DMA((8,)),
            DMA((18,)),
            VMEM((LENGTH, 256), bf16),
            VMEM((2, LENGTH, 256), f32),
            VMEM((2, LENGTH, DV), f32),
            VMEM((LENGTH, QCOLS), bf16),
            VMEM((LENGTH, LATENT_ROWS), bf16),
            VMEM((LENGTH, 512), bf16),
            VMEM((LATENT_ROWS, WIDE), bf16),
            VMEM((QUARTER, WIDE), bf16),
            VMEM((QUARTER, WIDE), bf16),
            DMA((2,)),
            DMA((2,)),
            DMA((2,)),
            DMA((2,)),
            DMA((2,)),
        ],
        compiler_params=pltpu.CompilerParams(
            collective_id=4, has_side_effects=True, vmem_limit_bytes=60 * MIB
        ),
        cost_estimate=pl.CostEstimate(flops=18 * 10**9, bytes_accessed=4 * 10**7, transcendentals=2 * 10**6),
        name="attend_back",
    )(*args)


LATE_HALF = LATE // 2
LATE_PIECE = LATE_HALF // 8


def half_pieces(y, all_ref, second_ref, opposite_ref):
    half = QUARTER // 2
    below, above = lax.rem(y + 3, 4), lax.rem(y + 1, 4)

    def view(ref, lead, offset=0):
        return lambda start, count: ref.at[lead, pl.ds(start - offset, count)]

    return (
        (view(all_ref, y), y, 0, QUARTER),
        (view(all_ref, below), below, 0, half),
        (view(all_ref, above), above, 0, half),
        (view(second_ref, 0, half), below, half, half),
        (view(second_ref, 1, half), above, half, half),
        (lambda start, count: opposite_ref.at[pl.ds(start, count)], lax.rem(y + 2, 4), 0, QUARTER),
    )


def last_kernel(
    p_ref, x_ref, hgrad_ref, gain_ref, tail_ref, hidden_ref, all_ref, moe_ref,
    normed_hbm, hall_hbm, jq_hbm, jk_hbm, kvg_hbm, attn_hbm, lnorm_hbm,
    out_ref, moved_ref, second_ref, opposite_ref, other, lall, packs,
    normed_ref, hall_ref, jq_ref, jk_ref, kvg_ref, attn_ref, lnorm_ref, hs,
    pv, pack_pv, moe_pv, pack, late, core_scr, half, got, near, far,
    pack_core, by_y, pack_near, pack_far, *rest,
):
    bufs, pack_bufs, moe_bufs = rest[:11], rest[11:22], rest[22:33]
    ss, rs, ps, pr, ms, mr, ys, yr, xs, xr, gs, gr, cs, cr, zs, zr, ls, mls = rest[33:]
    n = neighbours()
    d = copies_of()
    c, y = d["c"], d["y"]
    ready = load_partials(n, p_ref, pv, ls)
    loads = Copies(hs)
    theirs = pl.ds(pl.multiple_of((1 - c) * LATE_HALF, OWN), LATE_HALF)
    mine = pl.ds(pl.multiple_of(c * LATE_HALF, OWN), LATE_HALF)
    pack_theirs = pl.ds(pl.multiple_of((1 - c) * 64, 64), 64)
    pack_mine = pl.ds(pl.multiple_of(c * 64, 64), 64)
    entry_barrier(ring_peers(n), (d["core"], d["yp"], d["ym"], d["y2"], d["xo"]))
    first = dp_copy(late.at[theirs], core_scr, cs.at[0], cr.at[0], d["core"])
    cross = dp_copy(near, far, xs.at[0], xr.at[0], d["xo"])
    rows0, rows1 = pl.ds(0, QUARTER // 2), pl.ds(QUARTER // 2, QUARTER // 2)
    below = lax.rem(y + 3, 4)
    spread = [
        dp_copy(all_ref.at[y, rows1], second_ref.at[0], gs.at[0], gr.at[0], d["yp"]),
        dp_copy(all_ref.at[y, rows1], second_ref.at[1], gs.at[1], gr.at[1], d["ym"]),
    ]
    onward = [
        dp_copy(all_ref.at[below, rows0], opposite_ref.at[rows0], gs.at[2], gr.at[2], d["yp"]),
        dp_copy(second_ref.at[1], opposite_ref.at[rows1], gs.at[3], gr.at[3], d["ym"]),
    ]
    ring = reduce_steps(n, pv, ready, bufs, ss, rs)
    next(ring)
    for src, dst in (
        (jk_hbm, jk_ref), (normed_hbm, normed_ref), (jq_hbm, jq_ref), (lnorm_hbm, lnorm_ref), (kvg_hbm, kvg_ref),
        (attn_hbm, attn_ref), (hall_hbm, hall_ref),
    ):
        loads.start(src, dst)
    moe_ready = load_partials(n, moe_ref, moe_pv, mls)
    for copy in spread:
        copy.start()
    for copy in loads.made[:2]:
        copy.wait()
    blank = jnp.zeros((56, KB), f32)
    for i in range(8):
        cols = pl.ds(i * KB, KB)
        down = dot_tn(jk_ref[...], normed_ref[:, cols])
        for k in range(4):
            pack_pv[i, :, k * KB : k * KB + KB] = down[k * OWN : k * OWN + OWN].astype(bf16)
        rope = down[KVR : KVR + DR] + down[KVR + DR :]
        end = jnp.concatenate([rope, tail_ref[:, i * KB : i * KB + KB], blank], axis=0)
        pack_pv[i, :, 4 * KB :] = end.astype(bf16)
    pack_ring = reduce_steps(n, pack_pv, lambda name: None, pack_bufs, ps, pr)
    next(pack_ring)
    next(ring)
    for copy in loads.made[2:]:
        copy.wait()
    late[pl.ds(1536, KVR), :] = dot_tn(lnorm_ref[...], kvg_ref[...]).astype(bf16)
    for i in range(4):
        cols = pl.ds(i * 512, 512)
        late[pl.ds(2048 + i * 256, 256), :] = dot_tn(attn_ref[...], hall_ref[:, cols]).astype(bf16)
        query = dot_tn(normed_ref[:, cols], jq_ref[...]).astype(bf16)
        for k in range(3):
            late[pl.ds(k * 512, 512), i * 128 : i * 128 + 128] = query[:, k * 128 : k * 128 + 128]
    first.start()
    next(ring)
    first.wait_recv()
    half[...] = added(late[mine, :], core_scr[...])
    deal = y_deal(d, half, 2 * LATE_PIECE, got, ys, yr, 0)
    for copy in deal:
        copy.start()
    next(ring)
    next(pack_ring)
    next(ring)
    next(pack_ring)
    next(pack_ring)
    next(pack_ring)
    for copy in deal:
        copy.wait_recv()
    own_rows = pl.ds(pl.multiple_of(y * (2 * LATE_PIECE), 16), 2 * LATE_PIECE)
    total = half[own_rows, :].astype(f32)
    for hops in (1, 2, 3):
        total = total + got[lax.rem(y + hops, 4)].astype(f32)
    near[...] = total.astype(bf16)
    cross.start()
    for copy in spread:
        copy.wait_recv()
    for copy in onward:
        copy.start()
    moe_ring = reduce_steps(n, moe_pv, moe_ready, moe_bufs, ms, mr)
    next(moe_ring)
    next(ring, None)
    total = own_total(n, pv, bufs)
    x = x_ref[...].astype(f32)
    inv = inverse_rms(x)
    unit = x * inv
    scaled = total * row(gain_ref)
    back = inv * (scaled - unit * jnp.mean(scaled * unit, axis=-1, keepdims=True))
    out_ref[...] = (hgrad_ref[...] + back).astype(bf16)
    next(pack_ring, None)
    pack[...] = own_total(n, pack_pv, pack_bufs).astype(bf16)
    pack_first = dp_copy(pack.at[pack_theirs], pack_core, cs.at[1], cr.at[1], d["core"])
    pack_first.start()
    cross.wait_recv()
    lall[c, y] = added(near[...], far[...])
    pack_first.wait_recv()
    by_y[y] = added(pack[pack_mine, :], pack_core[...])
    pack_spread = y_spread(d, by_y, gs, gr, 4)
    for copy in pack_spread:
        copy.start()
    ygather = YGather(d, LATE_PIECE, lall.at[c], zs, zr)
    ygather.step(0)
    next(moe_ring)
    for copy in onward:
        copy.wait_recv()
    swaps = []
    for i, (view, slot, start, count) in enumerate(half_pieces(y, all_ref, second_ref, opposite_ref)):
        rows = pl.ds(start, count)
        swaps.append(dp_copy(view(start, count), other.at[slot, rows], cs.at[4 + i], cr.at[4 + i], d["core"]))
        swaps[-1].start()
    for copy in pack_spread:
        copy.wait_recv()
    total = by_y[0].astype(f32) + by_y[1].astype(f32) + by_y[2].astype(f32) + by_y[3].astype(f32)
    pack_near[...] = total.astype(bf16)
    pack_cross = dp_copy(pack_near, pack_far, xs.at[1], xr.at[1], d["xo"])
    pack_cross.start()
    next(moe_ring)
    next(moe_ring)
    next(moe_ring)
    ygather.step(1)
    pack_cross.wait_recv()
    packs[c] = added(pack_near[...], pack_far[...])
    pack_back = dp_copy(packs.at[c], packs.at[c], cs.at[3], cr.at[3], d["core"])
    pack_back.start()
    ygather.step(2)
    late_back = dp_copy(lall.at[c], lall.at[c], cs.at[2], cr.at[2], d["core"])
    late_back.start()
    next(moe_ring, None)
    moved_ref[...] = (hidden_ref[...] + own_total(n, moe_pv, moe_bufs)).astype(bf16)
    for copy in (pack_back, late_back, *swaps):
        copy.wait_recv()
    for copy in (first, cross, pack_first, pack_cross, pack_back, late_back):
        copy.wait_send()
    for copy in (*spread, *onward, *deal, *pack_spread, *ygather.all, *swaps):
        copy.wait_send()


def last(p, x, hgrad, gain, tail, hidden, quarters, moe, normed, hall, jq, jk, kvg, attn, lnorm):
    return pl.pallas_call(
        last_kernel,
        out_shape=(
            jax.ShapeDtypeStruct((OWN, WIDE), bf16),
            jax.ShapeDtypeStruct((OWN, WIDE), bf16),
            jax.ShapeDtypeStruct((2, QUARTER // 2, WIDE), bf16),
            jax.ShapeDtypeStruct((QUARTER, WIDE), bf16),
            jax.ShapeDtypeStruct((4, QUARTER, WIDE), bf16),
            jax.ShapeDtypeStruct((2, 4, 2 * LATE_PIECE, 512), bf16),
            jax.ShapeDtypeStruct((2, 64, PACK_COLS), bf16),
        ),
        in_specs=[anym()] + [vmem()] * 5 + [anym()] * 9,
        out_specs=[vmem(), vmem(), anym(), anym(), anym(), vmem(), vmem()],
        scratch_shapes=[
            VMEM((LENGTH, WIDE), bf16),
            VMEM((LENGTH, WIDE), bf16),
            VMEM((LENGTH, QCOLS), bf16),
            VMEM((LENGTH, LATENT_ROWS), bf16),
            VMEM((LENGTH, 512), bf16),
            VMEM((LENGTH, 256), bf16),
            VMEM((LENGTH, KVR), bf16),
            DMA((7,)),
            VMEM((SHARDS, OWN, WIDE), bf16),
            VMEM((SHARDS, OWN, PACK_COLS), bf16),
            VMEM((SHARDS, OWN, WIDE), bf16),
            VMEM((OWN, PACK_COLS), bf16),
            VMEM((LATE, 512), bf16),
            VMEM((LATE_HALF, 512), bf16),
            VMEM((LATE_HALF, 512), bf16),
            VMEM((4, 2 * LATE_PIECE, 512), bf16),
            VMEM((2 * LATE_PIECE, 512), bf16),
            VMEM((2 * LATE_PIECE, 512), bf16),
            VMEM((64, PACK_COLS), bf16),
            VMEM((4, 64, PACK_COLS), bf16),
            VMEM((64, PACK_COLS), bf16),
            VMEM((64, PACK_COLS), bf16),
        ]
        + reduce_scratch(WIDE)
        + reduce_scratch(PACK_COLS)
        + reduce_scratch(WIDE)
        + [DMA((17,))] * 6
        + [DMA((3,)), DMA((3,)), DMA((2,)), DMA((2,)), DMA((7,)), DMA((7,)), DMA((10,)), DMA((10,))]
        + [DMA((4,)), DMA((4,)), DMA((8,)), DMA((8,))],
        compiler_params=pltpu.CompilerParams(
            collective_id=5, has_side_effects=True, vmem_limit_bytes=60 * MIB
        ),
        cost_estimate=pl.CostEstimate(flops=6 * 10**9, bytes_accessed=2 * 10**7, transcendentals=0),
        name="last",
    )(p, x, hgrad, gain, tail, hidden, quarters, moe, normed, hall, jq, jk, kvg, attn, lnorm)


def widen_kernel(
    own_hbm, second_hbm, opposite_hbm, other_hbm, lall_hbm, pack_ref, grad_hbm, moved_hbm,
    q_out, kv_out, o_out, down_out, again_ref, fgain_ref, router_ref, lgain_ref, sg, su, sd, eg, eu, ed,
    grad_out, moved_out,
    wide, full_ref, lall_ref, q_ref, kv_ref, o_ref, down_ref, passed, os, hs,
):
    stores = Copies(os)
    loads = Copies(hs)
    d = copies_of()
    c, y = d["c"], d["y"]
    pieces = [piece + (c,) for piece in half_pieces(y, own_hbm, second_hbm, opposite_hbm)]
    for slot in range(4):
        view = lambda start, count, slot=slot: other_hbm.at[slot, pl.ds(start, count)]
        pieces.append((view, slot, 0, QUARTER, 1 - c))

    def load_product(k):
        begun = len(loads.made)
        for view, slot, start, count, core in pieces:
            low, high = max(start, 96 * k), min(start + count, 96 * k + 96)
            if low < high:
                at = pl.multiple_of(384 * k + 96 * slot + (low - 96 * k), 16)
                loads.start(view(low, high - low), full_ref.at[core, pl.ds(at, high - low)])
        return loads.made[begun:]

    def product(index, arrived, shared, experts):
        for copy in arrived:
            copy.wait()
        for k in range(index * 3, index * 3 + 3):
            for core in range(2):
                wide[pl.ds(k * 256 + core * OWN, OWN), :] = full_ref[core, pl.ds(k * OWN, OWN), :].astype(f32)
        base = index * HID
        stores.start(wide.at[pl.ds(base, FS_OWN)], shared)
        stores.start(wide.at[pl.ds(base + 384, FE_OWN)], experts.at[0])
        stores.start(wide.at[pl.ds(base + 384 + FE_OWN, FE_OWN)], experts.at[1])

    arrived = [load_product(0)]
    late = loads.start(lall_hbm, lall_ref)
    arrived += [load_product(1), load_product(2)]
    through = [loads.start(grad_hbm, passed.at[0]), loads.start(moved_hbm, passed.at[1])]
    product(0, arrived[0], sg, eg)
    late.wait()
    for k in range(3):
        for i in range(4):
            block = lall_ref[0, pl.ds(k * 512, 512), i * 128 : i * 128 + 128]
            q_ref[pl.ds(i * 512, 512), k * 128 : k * 128 + 128] = block.astype(f32)
    kv_ref[...] = lall_ref[1, pl.ds(0, KVR), :].astype(f32)
    for i in range(4):
        o_ref[:, i * 512 : i * 512 + 512] = lall_ref[1, pl.ds(512 + i * 256, 256), :].astype(f32)
    for j in range(4):
        down_ref[pl.ds(j * OWN, OWN), :] = pack_ref[:, j * KB : j * KB + KB].astype(f32)
    down_ref[pl.ds(KVR, DR), :] = pack_ref[:DR, 4 * KB :].astype(f32)
    for src, dst in ((q_ref, q_out), (kv_ref, kv_out), (o_ref, o_out), (down_ref, down_out)):
        stores.start(src, dst)
    product(1, arrived[1], su, eu)
    for copy, dst, k in ((through[0], grad_out, 0), (through[1], moved_out, 1)):
        copy.wait()
        stores.start(passed.at[k], dst)
    product(2, arrived[2], sd, ed)
    tail = pack_ref[DR : DR + 16, 4 * KB :].astype(f32)
    again_ref[...] = tail[0:1]
    fgain_ref[...] = tail[1:2]
    router_ref[...] = tail[2:4]
    lgain_ref[...] = tail[4:5, :64]
    stores.close()


def widen(own, second, opposite, other, lall, packs, input_grad, layer_out):
    def out(*shape):
        return jax.ShapeDtypeStruct(shape, f32)

    shared, experts = out(FS_OWN, WIDE), out(2, FE_OWN, WIDE)
    rows = jax.ShapeDtypeStruct((OWN, WIDE), bf16)
    return pl.pallas_call(
        widen_kernel,
        out_shape=(
            out(WIDE, QCOLS), out(KVR, 512), out(256, WIDE), out(576, 256),
            out(1, 256), out(1, 256), out(2, 256), out(1, 64), shared, shared, shared, experts, experts, experts,
            rows, rows,
        ),
        in_specs=[anym()] * 5 + [vmem()] + [anym()] * 2,
        out_specs=[anym()] * 4 + [vmem()] * 4 + [anym()] * 8,
        scratch_shapes=[
            VMEM((3 * HID, WIDE), f32),
            VMEM((2, BLOCKS * OWN, WIDE), bf16),
            VMEM((2, LATE_HALF, 512), bf16),
            VMEM((WIDE, QCOLS), f32),
            VMEM((KVR, 512), f32),
            VMEM((256, WIDE), f32),
            VMEM((576, 256), f32),
            VMEM((2, OWN, WIDE), bf16),
            DMA((15,)),
            DMA((29,)),
        ],
        compiler_params=pltpu.CompilerParams(vmem_limit_bytes=60 * MIB),
        cost_estimate=pl.CostEstimate(flops=10**7, bytes_accessed=4 * 10**7, transcendentals=0),
        name="widen",
    )(
        own, second, opposite, other, lall.reshape(2, LATE_HALF, 512), packs.reshape(OWN, PACK_COLS),
        input_grad, layer_out,
    )


def rope_tables():
    half = DR // 2
    frequency = ROPE_BASE ** (-(np.arange(half, dtype=np.float64) * 2.0) / DR)
    angles = np.arange(LENGTH, dtype=np.float64)[:, None] * frequency[None, :]
    cos = np.cos(angles).astype(np.float32)
    sin = np.sin(angles).astype(np.float32)
    return np.concatenate([cos] * 4, axis=1), np.concatenate([-sin, sin, -sin, sin], axis=1)


def after(value, *others):
    return lax.optimization_barrier((value, *others))[0]


def flat(v):
    return v.reshape(LENGTH, v.shape[-1])


def body(
    layer_in, grad_out, routes, prefix, attn_gain, query_proj, kv_down, latent_gain, kv_up,
    out_proj, ffn_gain, router_proj, shared_gate, shared_up, shared_down, expert_gate, expert_up, expert_down,
):
    cos_np, sin_np = rope_tables()
    cos, sin = jnp.asarray(cos_np), jnp.asarray(sin_np)
    again, lgain, fgain = (v.reshape(-1, 128) for v in (attn_gain, latent_gain, ffn_gain))
    kvd = kv_down.T
    sg, su = shared_gate.T, shared_up.T
    eg, eu = jnp.swapaxes(expert_gate, 1, 2), jnp.swapaxes(expert_up, 1, 2)
    rt = router_proj.T

    (
        normed, q, kvw, kr, lnorm, latent, grad_all, attn, lse, ot, hidden, mixed, m, da, db, p2, gsum
    ) = front(
        prefix, layer_in, grad_out, again, query_proj, kvd, lgain, kv_up, cos, sin, out_proj,
        fgain, routes.reshape(SHARDS, OWN), rt, sg, su, shared_down, eg, eu, expert_down,
    )
    p2 = p2.reshape(SHARDS, OWN, WIDE)
    hgrad, hall, ysum, router_rows, moe = turn_back(
        p2, hidden, grad_out, fgain, mixed, grad_all, m, da, db, shared_down, expert_down
    )
    hall = flat(hall)
    p3, quarters, jq, jk, kvg, tail = attend_back(
        prefix, hall, out_proj, q, kvw, kr, lse, ot, kv_up, latent, lgain, cos, sin, query_proj, kvd,
        normed, again, fgain, gsum, router_rows, ysum,
    )
    input_grad, layer_out, second, opposite, other, lall, packs = last(
        p3, layer_in, hgrad, again, tail, hidden, quarters, moe, normed, hall, jq, jk, kvg, attn, lnorm
    )
    dq, dkv, do, ddown, dag, dfg, drouter, dlg, dsg, dsu, dsd, deg, deu, ded, input_grad, layer_out = widen(
        quarters, second, opposite, other, lall, packs, input_grad, layer_out
    )
    return (
        layer_out,
        input_grad,
        dag.reshape(256),
        dq,
        ddown.T,
        dlg.reshape(64),
        dkv,
        do,
        dfg.reshape(256),
        drouter.T,
        dsg.T,
        dsu.T,
        dsd,
        jnp.swapaxes(deg, 1, 2),
        jnp.swapaxes(deu, 1, 2),
        ded,
    )


def solution(mesh):
    placed = (
        P(("dp", "tensor"), None),
        P(("dp", "tensor"), None),
        P("dp", None),
        P("dp"),
        P(),
        P(None, "tensor"),
        P(),
        P(),
        P(None, "tensor"),
        P("tensor", None),
        P(),
        P(),
        P(None, "tensor"),
        P(None, "tensor"),
        P("tensor", None),
        P(None, None, "tensor"),
        P(None, None, "tensor"),
        P(None, "tensor", None),
    )
    return jax.shard_map(
        body,
        mesh=mesh,
        in_specs=placed,
        out_specs=(
            P(("dp", "tensor"), None),
            P(("dp", "tensor"), None),
            P("tensor"),
            P(None, "tensor"),
            P("tensor", None),
            P("tensor"),
            P(None, "tensor"),
            P("tensor", None),
            P("tensor"),
            P("tensor", None),
            P(None, "tensor"),
            P(None, "tensor"),
            P("tensor", None),
            P(None, None, "tensor"),
            P(None, None, "tensor"),
            P(None, "tensor", None),
        ),
        check_vma=False,
    )
```
